32 devices in a mesh: dp: 8 (over z, y), mp: 4 (over x, core).
Axes of the slice: x: 2, y: 2, z: 4, core: 2. Of those that a mesh axis runs over, the one named last changes fastest.
Arguments:
- tokens: bfloat16 [64, 512, 768], P('dp', 'mp'), may hold values from -6 to 6
- cotangent: bfloat16 [64, 512, 768], P('dp', 'mp'), may hold values from -6 to 6
- lengths: int32 [64], P('dp'), may hold values from 256 to 512, as said below
- gain_attn: float32 [768], replicated, may hold values from 0.5 to 1.5
- gain_ff: float32 [768], replicated, may hold values from 0.5 to 1.5
- bias_table: float32 [32, 12], P(None, 'mp'), may hold values from -4 to 4
- w_query: float32 [768, 768], P('dp', 'mp'), may hold values from -0.109375 to 0.109375
- w_key: float32 [768, 768], P('dp', 'mp'), may hold values from -0.109375 to 0.109375
- w_value: float32 [768, 768], P('dp', 'mp'), may hold values from -0.21875 to 0.21875
- w_out_attn: float32 [768, 768], P('mp', 'dp'), may hold values from -0.875 to 0.875
- w_in_ff: float32 [768, 3072], P('dp', 'mp'), may hold values from -0.21875 to 0.21875
- w_out_ff: float32 [3072, 768], P('mp', 'dp'), may hold values from -0.109375 to 0.109375
Outputs:
- layer_out: bfloat16 [64, 512, 768], P('dp', 'mp')
- input_grad: bfloat16 [64, 512, 768], P('dp', 'mp')
- grad_gain_attn: float32 [768], replicated
- grad_gain_ff: float32 [768], replicated
- grad_bias_table: float32 [32, 12], P(None, 'mp')
- grad_query: float32 [768, 768], P('dp', 'mp')
- grad_key: float32 [768, 768], P('dp', 'mp')
- grad_value: float32 [768, 768], P('dp', 'mp')
- grad_out_attn: float32 [768, 768], P('mp', 'dp')
- grad_in_ff: float32 [768, 3072], P('dp', 'mp')
- grad_out_ff: float32 [3072, 768], P('mp', 'dp')
The draws below stay inside these ranges and needn't reach their ends.
Inputs may be any that keep to these rules, and one draw needn't show every extreme that they name: `lengths`: each length is 256 or 512; among the 8 pairs of each aligned block at least one has 512 and one has 256.
All inputs are finite; a program needn't handle non-finite values.
Results may differ from the reference program's by a relative error of at most 0.018.
Values may be sent and summed in bfloat16 or wider, within the bound.
A program may use at most 256 MiB of HBM per device.

```python
import jax
import jax.numpy as jnp
import numpy as np
from jax import lax

D = 768
HEADS = 12
DH = 64
FF = 3072
BUCKETS = 32
SEQ = 512
PAIRS_DEV = 8
PAIRS = 64


def draw_lengths(key, part):
    key = jax.random.fold_in(key, 7)
    base_key, order_key = jax.random.split(key)
    groups = PAIRS // PAIRS_DEV
    halves = jax.random.randint(base_key, (groups, PAIRS_DEV), 1, 3)
    group_keys = jax.random.split(order_key, groups)
    orders = jax.vmap(lambda single: jax.random.permutation(single, PAIRS_DEV))(group_keys)
    halves = jnp.where(orders == 0, 2, jnp.where(orders == 1, 1, halves))
    return (halves * (SEQ // 2)).reshape(PAIRS).astype(jnp.int32)


def level_of(rng, dims, cuts, least, top_value):
    level = 1.0
    for dim, shards_of in cuts:
        heights = jax.random.uniform(jax.random.fold_in(jax.random.fold_in(rng, 6), dim), (shards_of,), jnp.float32, least / len(cuts), top_value / len(cuts))
        level = level * jnp.repeat(jnp.exp(heights), dims[dim] // shards_of).reshape((-1,) + (1,) * (len(dims) - 1 - dim))
    return level


def normal_values(key, extent, deviation, most, cuts=(), held_as=jnp.bfloat16):
    entries = deviation * jax.random.normal(key, extent, jnp.float32)
    if cuts:
        entries = entries * level_of(key, extent, cuts, -0.22, 0.18)
    return jnp.clip(entries, -most, most).astype(held_as)


def setup_inputs(seed: int = 0) -> dict:
    key_list = jax.random.split(jax.random.key(seed), 13)
    tokens = normal_values(key_list[0], (PAIRS, SEQ, D), 1.0, 6.0, ((0, 8), (1, 4)))
    cotangent = normal_values(key_list[1], (PAIRS, SEQ, D), 1.0, 6.0, ((0, 8), (1, 4)))
    lengths = draw_lengths(jax.random.fold_in(key_list[12], 71), 0)
    gain_attn = jnp.clip(1.0 + 0.1 * jax.random.normal(key_list[3], (D,), jnp.float32), 0.5, 1.5)
    gain_ff = jnp.clip(1.0 + 0.1 * jax.random.normal(key_list[4], (D,), jnp.float32), 0.5, 1.5)
    bias_table = normal_values(key_list[5], (BUCKETS, HEADS), 1.0, 4.0, ((1, 4),), jnp.float32)
    w_query = normal_values(key_list[6], (D, HEADS * DH), (4 * D) ** -0.5, 0.109375, ((0, 8), (1, 4)), jnp.float32)
    w_key = normal_values(key_list[7], (D, HEADS * DH), (4 * D) ** -0.5, 0.109375, ((0, 8), (1, 4)), jnp.float32)
    w_value = normal_values(key_list[8], (D, HEADS * DH), D ** -0.5, 0.21875, ((0, 8), (1, 4)), jnp.float32)
    w_out_attn = normal_values(key_list[9], (HEADS * DH, D), (HEADS * DH // 16) ** -0.5, 0.875, ((0, 4), (1, 8)), jnp.float32)
    w_in_ff = normal_values(key_list[10], (D, FF), D ** -0.5, 0.21875, ((0, 8), (1, 4)), jnp.float32)
    w_out_ff = normal_values(key_list[11], (FF, D), FF ** -0.5, 0.109375, ((0, 4), (1, 8)), jnp.float32)
    return dict(tokens=tokens, cotangent=cotangent, lengths=lengths, gain_attn=gain_attn, gain_ff=gain_ff, bias_table=bias_table, w_query=w_query, w_key=w_key, w_value=w_value, w_out_attn=w_out_attn, w_in_ff=w_in_ff, w_out_ff=w_out_ff)


@jax.custom_vjp
def low(v):
    return lax.optimization_barrier(v.astype(jnp.bfloat16)).astype(jnp.float32)

@jax.custom_vjp
def low_back(v):
    return v

def low_keep(v):
    return (low(v), None)

def low_pass(kept, grad):
    return (grad,)

def back_keep(v):
    return (v, None)

def back_low(kept, grad):
    return (low(grad),)
low.defvjp(low_keep, low_pass)
low_back.defvjp(back_keep, back_low)
epsilon = 1e-06
far_reach = 128
largest_bucket = lax.Precision.HIGHEST

def bucket_table(pair_length, element_count):
    places = np.arange(pair_length)
    offset = places[None, :] - places[:, None]
    half_count = element_count // 2
    upper = (offset > 0).astype(np.int64) * half_count
    distance = np.abs(offset)
    exact_span = half_count // 2
    scaled = np.log(np.maximum(distance, 1) / exact_span) / np.log(far_reach / exact_span) * (half_count - exact_span)
    larger = np.minimum(exact_span + scaled.astype(np.int64), half_count - 1)
    return (upper + np.where(distance < exact_span, distance, larger)).astype(np.int32)

def rms_norm(x, gain):
    return x * lax.rsqrt(lax.optimization_barrier(jnp.mean(x * x, axis=-1, keepdims=True)) + epsilon) * gain

def attend_pair(query, keys, values, position_bias_grid, pair_length):
    seq_len = query.shape[0]
    scores = jnp.einsum('qhd,khd->hqk', query, keys, precision=largest_bucket)
    biases = jnp.transpose(position_bias_grid[bucket_table(seq_len, position_bias_grid.shape[0])], (2, 0, 1))
    scores = low_back(scores + biases)
    usable = jnp.arange(seq_len) < pair_length
    scores = jnp.where(usable[None, None, :], scores, -1e+30)
    probs = jax.nn.softmax(scores, axis=-1)
    return jnp.einsum('hqk,khd->qhd', low(probs), values, precision=largest_bucket)

def forward(x, group_lengths, gain_attn, gain_ff, bias_table, w_query, w_key, w_value, w_out_attn, w_in_ff, w_out_ff):
    pairs, seq_len, width = x.shape
    flattened = x.reshape(pairs * seq_len, width)
    normed_one = low(rms_norm(flattened, gain_attn))

    def project(weight):
        made = low(low_back(jnp.dot(normed_one, low(weight), precision=largest_bucket)))
        return made.reshape(pairs, seq_len, HEADS, DH)
    query = project(w_query)
    keys = project(w_key)
    values = project(w_value)

    def one_pair(element):
        return attend_pair(element[0], element[1], element[2], bias_table, element[3])
    attended = lax.map(jax.checkpoint(one_pair), (query, keys, values, group_lengths))
    attended = low(low_back(attended.reshape(pairs * seq_len, HEADS * DH)))
    branch = low_back(jnp.dot(attended, low(w_out_attn), precision=largest_bucket))
    hidden = flattened + branch
    normed_two = low(rms_norm(hidden, gain_ff))
    pre_act = low_back(jnp.dot(normed_two, low(w_in_ff), precision=largest_bucket))
    acted = low(jax.nn.gelu(pre_act))
    ff_branch = low_back(jnp.dot(acted, low(w_out_ff), precision=largest_bucket))
    return (hidden + ff_branch).reshape(pairs, seq_len, width)

def reference(tokens, cotangent, lengths, gain_attn, gain_ff, bias_table, w_query, w_key, w_value, w_out_attn, w_in_ff, w_out_ff):
    groups = PAIRS // PAIRS_DEV
    inputs = tokens.astype(jnp.float32).reshape(groups, PAIRS_DEV, SEQ, D)
    upstream = cotangent.astype(jnp.float32).reshape(groups, PAIRS_DEV, SEQ, D)
    grouped_lengths = lengths.reshape(groups, PAIRS_DEV).astype(jnp.int32)
    params = (gain_attn, gain_ff, bias_table, w_query, w_key, w_value, w_out_attn, w_in_ff, w_out_ff)

    def group_step(running, element):
        group_x, group_dy, group_len = element

        def apply_layer(inner_x, *weights):
            return forward(inner_x, group_len, *weights)
        result, backward = jax.vjp(apply_layer, group_x, *params)
        grads = backward(group_dy)
        running = tuple((before + after for before, after in zip(running, grads[1:])))
        return (running, (result.astype(jnp.bfloat16), grads[0].astype(jnp.bfloat16)))
    zeros_start = tuple((jnp.zeros(param.shape, jnp.float32) for param in params))
    summed, (results, input_grads) = lax.scan(group_step, zeros_start, (inputs, upstream, grouped_lengths))
    return (results.reshape(PAIRS, SEQ, D), input_grads.reshape(PAIRS, SEQ, D), summed[0], summed[1], summed[2], summed[3], summed[4], summed[5], summed[6], summed[7], summed[8])
```

```python
import functools

import jax
import jax.numpy as jnp
import numpy as np
from jax import lax
from jax.experimental import pallas as pl
from jax.experimental.pallas import tpu as pltpu
from jax.sharding import PartitionSpec as P

BF = jnp.bfloat16
F32 = jnp.float32
MESH = pl.DeviceIdType.MESH
EPS = 1e-06
FAR = 128
HIGHEST = lax.Precision.HIGHEST
MIB = 2**20


def bucket_of(offset, count):
    half = count // 2
    upper = (offset > 0).astype(np.int64) * half
    distance = np.abs(offset)
    exact = half // 2
    scaled = np.log(np.maximum(distance, 1) / exact) / np.log(FAR / exact) * (half - exact)
    larger = np.minimum(exact + scaled.astype(np.int64), half - 1)
    return (upper + np.where(distance < exact, distance, larger)).astype(np.int32)


class Place:
    def __init__(self, ndp, nmp):
        self.dp, self.mp = lax.axis_index("dp"), lax.axis_index("mp")
        self.x, self.c = self.mp // 2, self.mp % 2
        self.z, self.y = self.dp // 2, self.dp % 2
        self.nz = ndp // 2
        self.nmp = nmp

    def at(self, x=None, c=None, z=None, y=None):
        x = self.x if x is None else x
        c = self.c if c is None else c
        z = self.z if z is None else z
        y = self.y if y is None else y
        return (z * 2 + y, x * 2 + c)

    def greet(self):
        bar = pltpu.get_barrier_semaphore()

        def tell(who):
            pl.semaphore_signal(bar, inc=1, device_id=who, device_id_type=MESH)

        tell(self.at(c=1 - self.c))
        tell(self.at(x=1 - self.x))
        tell(self.at(x=1 - self.x, c=1 - self.c))
        tell(self.at(y=1 - self.y))

        def tell_z(k, carry):
            tell(self.at(z=lax.rem(self.z + k, self.nz)))
            return carry

        lax.fori_loop(1, self.nz, tell_z, 0)
        pl.semaphore_wait(bar, 4 + self.nz - 1)


def remote(src, dst, ssem, rsem, who):
    return pltpu.make_async_remote_copy(
        src_ref=src, dst_ref=dst, send_sem=ssem, recv_sem=rsem, device_id=who, device_id_type=MESH
    )


def loop(lo, hi, fn):
    def step(k, carry):
        fn(k)
        return carry

    lax.fori_loop(lo, hi, step, 0)


class Gather:
    def __init__(self, here, pack, order, W, ssem, rsem):
        self.h, self.order = here, order
        self.W = W.at[pack]
        self.ss, self.rs = ssem.at[pack], rsem.at[pack]

    def zi(self, k):
        return lax.rem(self.h.z + k, self.h.nz)

    def send(self, src, kind, idx, who, sidx=None):
        sidx = idx if sidx is None else sidx
        return remote(src, src, self.ss.at[kind, sidx], self.rs.at[kind, idx], who)

    def first_to(self, k):
        h = self.h
        if self.order == "xzy":
            return self.send(self.W.at[h.x, h.c, h.z, h.y], 0, 0, h.at(x=1 - h.x))
        z = self.zi(k)
        return self.send(self.W.at[h.x, h.c, h.z, h.y], 0, h.z, h.at(z=z), z)

    def first_from(self, k):
        h = self.h
        if self.order == "xzy":
            return self.send(self.W.at[1 - h.x, h.c, h.z, h.y], 0, 0, h.at(x=1 - h.x))
        z = self.zi(k)
        return self.send(self.W.at[h.x, h.c, z, h.y], 0, z, h.at(z=z), z)

    def second_to(self, k):
        h, z = self.h, self.zi(k)
        if self.order == "xzy":
            return self.send(self.W.at[:, h.c, h.z, h.y], 1, h.z, h.at(z=z), z)
        peer = h.at(x=1 - h.x) if self.order == "zxy" else h.at(y=1 - h.y)
        return self.send(self.W.at[h.x, h.c, z, h.y], 1, z, peer)

    def second_from(self, k):
        h, z = self.h, self.zi(k)
        if self.order == "xzy":
            return self.send(self.W.at[:, h.c, z, h.y], 1, z, h.at(z=z), z)
        if self.order == "zxy":
            return self.send(self.W.at[1 - h.x, h.c, z, h.y], 1, z, h.at(x=1 - h.x))
        return self.send(self.W.at[h.x, h.c, z, 1 - h.y], 1, z, h.at(y=1 - h.y))

    def third_to(self, half, k):
        h, z = self.h, self.zi(k)
        if self.order == "zyx":
            y = h.y if half == 0 else 1 - h.y
            return self.send(self.W.at[h.x, h.c, z, y], 2 + half, z, h.at(x=1 - h.x))
        x = h.x if half == 0 else 1 - h.x
        return self.send(self.W.at[x, h.c, z, h.y], 2 + half, z, h.at(y=1 - h.y))

    def third_from(self, half, k):
        h, z = self.h, self.zi(k)
        if self.order == "zyx":
            y = h.y if half == 0 else 1 - h.y
            return self.send(self.W.at[1 - h.x, h.c, z, y], 2 + half, z, h.at(x=1 - h.x))
        x = h.x if half == 0 else 1 - h.x
        return self.send(self.W.at[x, h.c, z, 1 - h.y], 2 + half, z, h.at(y=1 - h.y))

    def sib(self, half, k, c):
        h, z = self.h, self.zi(k)
        if self.order == "zyx":
            x = h.x if half == 0 else 1 - h.x
            block = self.W.at[x, c, z, :]
        else:
            y = h.y if half == 0 else 1 - h.y
            block = self.W.at[:, c, z, y]
        return self.send(block, 4 + half, z, h.at(c=1 - h.c))

    def start_first(self):
        if self.order == "xzy":
            self.first_to(0).start()
        else:
            loop(1, self.h.nz, lambda k: self.first_to(k).start())

    def after_first(self):
        nz = self.h.nz
        if self.order == "xzy":
            self.first_from(0).wait_recv()
            loop(1, nz, lambda k: self.second_to(k).start())
            self.third_to(0, 0).start()
            self.third_to(1, 0).start()
            self.sib(0, 0, self.h.c).start()
        else:

            def on(k):
                pl.when(k > 0)(lambda: self.first_from(k).wait_recv())
                self.second_to(k).start()
                self.third_to(0, k).start()

            loop(0, nz, on)

    def after_second(self):
        nz = self.h.nz
        if self.order == "xzy":

            def on(k):
                self.second_from(k).wait_recv()
                self.third_to(0, k).start()
                self.third_to(1, k).start()
                self.sib(0, k, self.h.c).start()

            loop(1, nz, on)
        else:

            def on(k):
                self.second_from(k).wait_recv()
                self.third_to(1, k).start()
                self.sib(0, k, self.h.c).start()

            loop(0, nz, on)

    def after_third(self):
        def on(k):
            self.third_from(0, k).wait_recv()
            self.third_from(1, k).wait_recv()
            self.sib(1, k, self.h.c).start()

        loop(0, self.h.nz, on)

    def finish(self):
        nz = self.h.nz

        def on(k):
            for half in (0, 1):
                self.sib(half, k, 1 - self.h.c).wait_recv()
                self.sib(half, k, self.h.c).wait_send()
                self.third_to(half, k).wait_send()

        loop(0, nz, on)
        if self.order == "xzy":
            self.first_to(0).wait_send()
            loop(1, nz, lambda k: self.second_to(k).wait_send())
        else:
            loop(1, nz, lambda k: self.first_to(k).wait_send())
            loop(0, nz, lambda k: self.second_to(k).wait_send())


class Swap:
    def __init__(self, here, src, dst, ssem, rsem, lsem, back):
        self.h, self.src, self.dst, self.ss, self.rs, self.ls, self.back = here, src, dst, ssem, rsem, lsem, back
        self.share = (dst if back else src).shape[0] // here.nmp

    def views(self, sender, receiver):
        src, dst = self.src, self.dst
        if self.back:
            return src.at[:, receiver], dst.at[pl.ds(sender * self.share, self.share)]
        return src.at[pl.ds(receiver * self.share, self.share)], dst.at[:, sender]

    def to(self, k):
        other = lax.rem(self.h.mp + k, self.h.nmp)
        src, dst = self.views(self.h.mp, other)
        return remote(src, dst, self.ss.at[k], self.rs.at[k], (self.h.dp, other))

    def come(self, k):
        other = lax.rem(self.h.mp + self.h.nmp - k, self.h.nmp)
        src, dst = self.views(other, self.h.mp)
        return remote(dst, dst, self.ss.at[k], self.rs.at[k], (self.h.dp, other))

    def local(self):
        src, dst = self.views(self.h.mp, self.h.mp)
        return pltpu.make_async_copy(src, dst, self.ls.at[0])

    def start(self):
        for k in range(1, self.h.nmp):
            self.to(k).start()
        self.local().start()

    def finish(self):
        for k in range(1, self.h.nmp):
            self.come(k).wait_recv()
            self.to(k).wait_send()
        self.local().wait()


def gather_kernel(ndp, nmp, own, tok, cot, bias, W, X, DY, BT, ssem, rsem, tsem, bsem, lsem):
    h = Place(ndp, nmp)
    h.greet()
    for p in range(3):
        pltpu.make_async_copy(own.at[p], W.at[p, h.x, h.c, h.z, h.y], lsem.at[p]).start()
    sx = Swap(h, tok, X, tsem.at[0], tsem.at[1], tsem.at[4], False)
    sd = Swap(h, cot, DY, tsem.at[2], tsem.at[3], tsem.at[5], False)
    for p in range(3):
        pltpu.make_async_copy(own.at[p], W.at[p, h.x, h.c, h.z, h.y], lsem.at[p]).wait()
    A = Gather(h, 0, "xzy", W, ssem, rsem)
    B = Gather(h, 1, "zxy", W, ssem, rsem)
    C = Gather(h, 2, "zyx", W, ssem, rsem)
    A.start_first()
    bts = []
    for k in range(1, nmp):
        other = lax.rem(h.mp + k, nmp)
        bts.append(remote(bias, BT.at[h.mp], bsem.at[0, k], bsem.at[1, k], (h.dp, other)))
        bts[-1].start()
    own_bias = pltpu.make_async_copy(bias, BT.at[h.mp], lsem.at[3])
    own_bias.start()
    sx.start()
    A.after_first()
    A.after_second()
    B.start_first()
    A.after_third()
    C.start_first()
    B.after_first()
    C.after_first()
    B.after_second()
    C.after_second()
    sx.finish()
    sd.start()
    A.finish()
    B.after_third()
    C.after_third()
    B.finish()
    C.finish()
    sd.finish()
    own_bias.wait()
    for k in range(1, nmp):
        other = lax.rem(h.mp + nmp - k, nmp)
        remote(bias, BT.at[other], bsem.at[0, k], bsem.at[1, k], (h.dp, other)).wait_recv()
        bts[k - 1].wait_send()


def gather_all(own, tok, cot, bias, ndp, nmp):
    n, rows, width = own.shape
    pairs, positions, _ = tok.shape
    nz = ndp // 2
    share = pairs // nmp
    any_ = pl.BlockSpec(memory_space=pl.ANY)
    dma = pltpu.SemaphoreType.DMA
    return pl.pallas_call(
        functools.partial(gather_kernel, ndp, nmp),
        out_shape=(
            jax.ShapeDtypeStruct((n, nmp // 2, 2, nz, 2, rows, width), BF),
            jax.ShapeDtypeStruct((share, nmp, positions, width), BF),
            jax.ShapeDtypeStruct((share, nmp, positions, width), BF),
            jax.ShapeDtypeStruct((nmp,) + bias.shape, F32),
        ),
        in_specs=[any_] * 4,
        out_specs=(any_,) * 4,
        scratch_shapes=[dma((n, 6, nz)), dma((n, 6, nz)), dma((6, nmp)), dma((2, nmp)), dma((4,))],
        compiler_params=pltpu.CompilerParams(collective_id=0, has_side_effects=True),
    )(own, tok, cot, bias)


class Scatter:
    def __init__(self, here, pack, G, mine, R0, R1, R2, R3, out, ssem, rsem, lsem):
        self.h, self.p = here, pack
        self.G, self.mine = G.at[pack], mine.at[pack]
        self.R0, self.R1, self.R2, self.R3, self.out = R0.at[pack], R1.at[pack], R2.at[pack], R3.at[pack], out
        self.ss, self.rs, self.ls = ssem.at[pack], rsem.at[pack], lsem.at[pack]

    def zi(self, k):
        return lax.rem(self.h.z + k, self.h.nz)

    def sib(self, x):
        h = self.h
        return remote(self.G.at[x, 1 - h.c], self.R0.at[x], self.ss.at[0, x], self.rs.at[0, x], h.at(c=1 - h.c))

    def local(self, x):
        return pltpu.make_async_copy(self.G.at[x, self.h.c], self.mine.at[x], self.ls.at[x])

    def ysend(self, k):
        h, z = self.h, self.zi(k)
        return remote(self.mine.at[:, z, 1 - h.y], self.R1.at[:, z], self.ss.at[1, z], self.rs.at[1, z], h.at(y=1 - h.y))

    def zsend(self, k):
        h, z = self.h, self.zi(k)
        return remote(self.R1.at[:, z], self.R2.at[h.z], self.ss.at[2, z], self.rs.at[2, h.z], h.at(z=z))

    def zcome(self, k):
        h, z = self.h, self.zi(k)
        return remote(self.R2.at[z], self.R2.at[z], self.ss.at[2, z], self.rs.at[2, z], h.at(z=z))

    def xsend(self):
        h = self.h
        return remote(self.R1.at[1 - h.x, h.z], self.R3, self.ss.at[3, 0], self.rs.at[3, 0], h.at(x=1 - h.x))

    def start(self):
        for x in range(2):
            self.local(x).start()
            self.sib(x).start()

    def after_sib(self):
        h = self.h
        for x in range(2):
            self.local(x).wait()
            self.sib(x).wait_recv()

        def on(k):
            z = self.zi(k)
            for y in (1 - h.y, h.y):
                for x in range(2):
                    self.mine[x, z, y] = (self.mine[x, z, y].astype(F32) + self.R0[x, z, y].astype(F32)).astype(BF)
                if y is not h.y:
                    self.ysend(k).start()

        loop(0, h.nz, on)

    def after_y(self):
        h = self.h

        def on(kk):
            k = lax.rem(kk + 1, h.nz)
            z = self.zi(k)
            self.ysend(k).wait_recv()
            for x in range(2):
                self.R1[x, z] = (self.mine[x, z, h.y].astype(F32) + self.R1[x, z].astype(F32)).astype(BF)
            pl.when(k > 0)(lambda: self.zsend(k).start())

        loop(0, h.nz, on)

    def after_z(self):
        h = self.h
        loop(1, h.nz, lambda k: self.zcome(k).wait_recv())

        def total(x):
            def add(k, acc):
                return acc + self.R2[self.zi(k), x].astype(F32)

            return lax.fori_loop(1, h.nz, add, self.R1[x, h.z].astype(F32))

        self.R1[1 - h.x, h.z] = total(1 - h.x).astype(BF)
        self.xsend().start()
        self.out[self.p] = total(h.x)

    def finish(self):
        h = self.h
        self.xsend().wait()
        self.out[self.p] += self.R3[...].astype(F32)
        for x in range(2):
            self.sib(x).wait_send()
        loop(0, h.nz, lambda k: self.ysend(k).wait_send())
        loop(1, h.nz, lambda k: self.zsend(k).wait_send())


def scatter_kernel(ndp, nmp, n, G, lay, ing, out, L, I, mine, R0, R1, R2, R3, ssem, rsem, lsem, tsem):
    h = Place(ndp, nmp)
    h.greet()
    packs = [Scatter(h, p, G, mine, R0, R1, R2, R3, out, ssem, rsem, lsem) for p in range(n)]
    sl = Swap(h, lay, L, tsem.at[0], tsem.at[1], tsem.at[4], True)
    si = Swap(h, ing, I, tsem.at[2], tsem.at[3], tsem.at[5], True)
    for s in packs:
        s.start()
    sl.start()
    for s in packs:
        s.after_sib()
    for s in packs:
        s.after_y()
    si.start()
    for s in packs:
        s.after_z()
    for s in packs:
        s.finish()
    sl.finish()
    si.finish()


def scatter_all(G, lay, ing, ndp, nmp):
    n, rows, width = G.shape[0], G.shape[-2], G.shape[-1]
    nz = ndp // 2
    share, _, positions, _ = lay.shape
    any_ = pl.BlockSpec(memory_space=pl.ANY)
    dma = pltpu.SemaphoreType.DMA
    back = jax.ShapeDtypeStruct((share * nmp, positions, width), BF)
    return pl.pallas_call(
        functools.partial(scatter_kernel, ndp, nmp, n),
        out_shape=(jax.ShapeDtypeStruct((n, rows, width), F32), back, back),
        in_specs=[any_] * 3,
        out_specs=(pl.BlockSpec(memory_space=pltpu.VMEM), any_, any_),
        scratch_shapes=[
            pltpu.VMEM((n, 2, nz, 2, rows, width), BF),
            pltpu.VMEM((n, 2, nz, 2, rows, width), BF),
            pltpu.VMEM((n, 2, nz, rows, width), BF),
            pltpu.VMEM((n, nz, 2, rows, width), BF),
            pltpu.VMEM((n, rows, width), BF),
            dma((n, 4, max(nz, 2))),
            dma((n, 4, max(nz, 2))),
            dma((n, 2)),
            dma((6, nmp)),
        ],
        compiler_params=pltpu.CompilerParams(collective_id=1, has_side_effects=True, vmem_limit_bytes=56 * MIB),
    )(G, lay, ing)


def dot(a, b, ca=1, cb=0):
    return lax.dot_general(a, b, (((ca,), (cb,)), ((), ())), preferred_element_type=F32)


def body(tokens, cotangent, lengths, gain_attn, gain_ff, bias_table, w_query, w_key, w_value, w_out_attn, w_in_ff, w_out_ff):
    ndp, nmp = lax.axis_size("dp"), lax.axis_size("mp")
    pairs, positions, width = tokens.shape
    seq = positions * nmp
    share = pairs // nmp
    buckets, heads_mp = bias_table.shape
    heads = heads_mp * nmp
    part = w_query.shape[1]
    dh = part // heads_mp
    rows = w_query.shape[0]
    padded = -(-rows // 16) * 16
    n = share * seq

    own = jnp.stack(
        [
            jnp.concatenate([w_query, w_key, w_value, w_out_attn.T], axis=1).astype(BF),
            w_in_ff.astype(BF),
            w_out_ff.T.astype(BF),
        ]
    )
    own = jnp.pad(own, ((0, 0), (0, padded - rows), (0, 0)))
    bias_own = jnp.zeros((8, 128), F32).at[:heads_mp, :buckets].set(bias_table.T)
    W, X, DY, BT = gather_all(own, tokens, cotangent, bias_own, ndp, nmp)
    W = W.reshape(3, nmp, ndp, padded, width)[:, :, :, :rows].reshape(3, nmp, width, width)
    A, B, C = W[0], W[1], W[2]
    table = BT[:, :heads_mp, :buckets].reshape(heads, buckets)
    lens = lax.dynamic_slice_in_dim(lengths, lax.axis_index("mp") * share, share)

    x = X.reshape(n, width).astype(F32)
    dy_low = DY.reshape(n, width)
    dy = dy_low.astype(F32)
    codes = bucket_of(np.arange(seq)[None, :] - np.arange(seq)[:, None], buckets)
    onehot = jnp.asarray(codes)[None] == jnp.arange(buckets, dtype=jnp.int32)[:, None, None]
    biases = jnp.einsum("hb,bij->hij", table, onehot.astype(F32), precision=HIGHEST)

    r1 = lax.rsqrt(jnp.mean(x * x, axis=-1, keepdims=True) + EPS)
    n1 = (x * r1 * gain_attn).astype(BF)
    qkv = [dot(n1, A[m][:, : 3 * part]).astype(BF) for m in range(nmp)]

    def cut(i):
        return jnp.stack([q[:, i * part : (i + 1) * part] for q in qkv], 1).reshape(share, seq, heads, dh)

    q, k, v = cut(0), cut(1), cut(2)
    s = jnp.einsum("pqhd,pkhd->phqk", q, k, preferred_element_type=F32) + biases[None]
    live = jnp.arange(seq)[None, :] < lens[:, None]
    s = jnp.where(live[:, None, None, :], s, -1e30)
    prob = jax.nn.softmax(s, axis=-1)
    plow = prob.astype(BF)
    o = jnp.einsum("phqk,pkhd->pqhd", plow, v, preferred_element_type=F32).astype(BF)
    om = o.reshape(n, nmp, part)
    att = sum(dot(om[:, m], A[m][:, 3 * part :], 1, 1) for m in range(nmp))
    h = x + att
    r2 = lax.rsqrt(jnp.mean(h * h, axis=-1, keepdims=True) + EPS)
    n2 = (h * r2 * gain_ff).astype(BF)
    ff = 0.0
    gn2 = 0.0
    g_in, g_out = [], []
    for m in range(nmp):
        a = dot(n2, B[m])
        u, back = jax.vjp(jax.nn.gelu, a)
        u = u.astype(BF)
        ff = ff + dot(u, C[m], 1, 1)
        g_out.append(dot(dy_low, u, 0, 0).astype(BF))
        ga = back(dot(dy_low, C[m]))[0].astype(BF)
        g_in.append(dot(n2, ga, 0, 0).astype(BF))
        gn2 = gn2 + dot(ga, B[m], 1, 1)
    layer = (h + ff).astype(BF)
    nh = h * r2
    gain_ff_part = jnp.sum(gn2 * nh, axis=0)
    e = gn2 * gain_ff
    gh = dy + r2 * (e - nh * jnp.mean(e * nh, axis=-1, keepdims=True))
    gh_low = gh.astype(BF)
    do = [dot(gh_low, A[m][:, 3 * part :]).astype(BF) for m in range(nmp)]
    do4 = jnp.stack(do, 1).reshape(share, seq, heads, dh)
    dP = jnp.einsum("pqhd,pkhd->phqk", do4, v, preferred_element_type=F32)
    gv = jnp.einsum("phqk,pqhd->pkhd", plow, do4, preferred_element_type=F32).astype(BF)
    gs = (prob * (dP - jnp.sum(prob * dP, axis=-1, keepdims=True))).astype(BF)
    gq = jnp.einsum("phqk,pkhd->pqhd", gs, k, preferred_element_type=F32).astype(BF)
    gk = jnp.einsum("phqk,pqhd->pkhd", gs, q, preferred_element_type=F32).astype(BF)
    gb = jnp.einsum("hij,bij->bh", jnp.sum(gs.astype(F32), 0), onehot.astype(F32), precision=HIGHEST)
    g_attn = []
    gn1 = 0.0
    for m in range(nmp):
        gm = jnp.concatenate([g.reshape(n, nmp, part)[:, m] for g in (gq, gk, gv)], 1)
        g_attn.append(jnp.concatenate([dot(n1, gm, 0, 0), dot(gh_low, om[:, m], 0, 0)], 1).astype(BF))
        gn1 = gn1 + dot(gm, A[m][:, : 3 * part], 1, 1)
    nx = x * r1
    gain_attn_part = jnp.sum(gn1 * nx, axis=0)
    e1 = gn1 * gain_attn
    ing = (gh + r1 * (e1 - nx * jnp.mean(e1 * nx, axis=-1, keepdims=True))).astype(BF)

    G = jnp.stack([jnp.stack(g_attn), jnp.stack(g_in), jnp.stack(g_out)]).reshape(3, nmp, ndp, rows, width)
    G = jnp.pad(G, ((0, 0), (0, 0), (0, 0), (0, padded - rows), (0, 0)))
    G = G.reshape(3, nmp // 2, 2, ndp // 2, 2, padded, width)
    S, layer_out, input_grad = scatter_all(
        G, layer.reshape(share, nmp, positions, width), ing.reshape(share, nmp, positions, width), ndp, nmp
    )
    S = S[:, :rows]
    sa = S[0]
    gga, ggf, gball = lax.psum((gain_attn_part, gain_ff_part, gb), ("dp", "mp"))
    gbt = lax.dynamic_slice_in_dim(gball, lax.axis_index("mp") * heads_mp, heads_mp, 1)
    return (
        layer_out,
        input_grad,
        gga,
        ggf,
        gbt,
        sa[:, :part],
        sa[:, part : 2 * part],
        sa[:, 2 * part : 3 * part],
        sa[:, 3 * part :].T,
        S[1],
        S[2].T,
    )


def solution(mesh):
    act = P("dp", "mp", None)
    rows, cols = P("dp", "mp"), P("mp", "dp")
    return jax.shard_map(
        body,
        mesh=mesh,
        in_specs=(act, act, P("dp"), P(), P(), P(None, "mp"), rows, rows, rows, cols, rows, cols),
        out_specs=(act, act, P(), P(), P(None, "mp"), rows, rows, rows, cols, rows, cols),
        check_vma=False,
    )
```

```python
import functools
import math

import jax
import jax.numpy as jnp
import numpy as np
from jax import lax
from jax.experimental import pallas as pl
from jax.experimental.pallas import tpu as pltpu
from jax.sharding import PartitionSpec as P

BF = jnp.bfloat16
F32 = jnp.float32
MESH = pl.DeviceIdType.MESH
EPS = 1e-06
FAR = 128
HIGHEST = lax.Precision.HIGHEST
MIB = 2**20


def bucket_of(offset, count):
    half = count // 2
    upper = (offset > 0).astype(np.int64) * half
    distance = np.abs(offset)
    exact = half // 2
    scaled = np.log(np.maximum(distance, 1) / exact) / np.log(FAR / exact) * (half - exact)
    larger = np.minimum(exact + scaled.astype(np.int64), half - 1)
    return (upper + np.where(distance < exact, distance, larger)).astype(np.int32)


class Place:
    def __init__(self, ndp, nmp, fine):
        self.dp, self.mp = lax.axis_index("dp"), lax.axis_index("mp")
        self.x, self.c = self.mp // 2, self.mp % 2
        self.fine = fine
        self.z, self.y = self.dp // fine // 2, self.dp // fine % 2
        self.nz = ndp // fine // 2
        self.nmp = nmp

    def at(self, x=None, c=None, z=None, y=None):
        x = self.x if x is None else x
        c = self.c if c is None else c
        z = self.z if z is None else z
        y = self.y if y is None else y
        return ((z * 2 + y) * self.fine + self.dp % self.fine, x * 2 + c)

    def zi(self, k):
        return lax.rem(self.z + k, self.nz)

    def greet(self):
        bar = pltpu.get_barrier_semaphore()

        def tell(who):
            pl.semaphore_signal(bar, inc=1, device_id=who, device_id_type=MESH)

        tell(self.at(c=1 - self.c))
        tell(self.at(x=1 - self.x))
        tell(self.at(x=1 - self.x, c=1 - self.c))
        tell(self.at(y=1 - self.y))
        loop(1, self.nz, lambda k: tell(self.at(z=self.zi(k))))

    def met(self):
        pl.semaphore_wait(pltpu.get_barrier_semaphore(), 4 + self.nz - 1)


def remote(src, dst, ssem, rsem, who):
    return pltpu.make_async_remote_copy(
        src_ref=src, dst_ref=dst, send_sem=ssem, recv_sem=rsem, device_id=who, device_id_type=MESH
    )


def loop(lo, hi, fn):
    def step(k, carry):
        fn(k)
        return carry

    lax.fori_loop(lo, hi, step, 0)


class Gather:
    def __init__(self, here, pack, order, W, ssem, rsem):
        self.h, self.order, self.nz = here, order, here.nz
        self.W = W.at[pack]
        self.ss, self.rs = ssem.at[pack], rsem.at[pack]

    def send(self, src, kind, idx, who, sidx=None):
        sidx = idx if sidx is None else sidx
        return remote(src, src, self.ss.at[kind, sidx], self.rs.at[kind, idx], who)

    def first(self, k, mine=True):
        h = self.h
        if self.order == "xzy":
            x = h.x if mine else 1 - h.x
            return self.send(self.W.at[x, h.c, h.z, h.y], 0, 0, h.at(x=1 - h.x))
        z = h.zi(k)
        own = h.z if mine else z
        return self.send(self.W.at[h.x, h.c, own, h.y], 0, own, h.at(z=z), z)

    def second(self, k, mine=True):
        h, z = self.h, self.h.zi(k)
        if self.order == "xzy":
            own = h.z if mine else z
            return self.send(self.W.at[:, h.c, own, h.y], 1, own, h.at(z=z), z)
        if self.order == "zxy":
            x = h.x if mine else 1 - h.x
            return self.send(self.W.at[x, h.c, z, h.y], 1, z, h.at(x=1 - h.x))
        y = h.y if mine else 1 - h.y
        return self.send(self.W.at[h.x, h.c, z, y], 1, z, h.at(y=1 - h.y))

    def third(self, half, k, mine=True):
        h, z = self.h, self.h.zi(k)
        x, y = h.x, h.y
        if self.order == "zyx":
            y = y if half == 0 else 1 - y
            x = x if mine else 1 - x
            return self.send(self.W.at[x, h.c, z, y], 2 + half, z, h.at(x=1 - h.x))
        x = x if half == 0 else 1 - x
        y = y if mine else 1 - y
        return self.send(self.W.at[x, h.c, z, y], 2 + half, z, h.at(y=1 - h.y))

    def sib(self, half, k, mine=True):
        h, z = self.h, self.h.zi(k)
        c = h.c if mine else 1 - h.c
        if self.order == "zyx":
            block = self.W.at[h.x if half == 0 else 1 - h.x, c, z]
        else:
            block = self.W.at[:, c, z, h.y if half == 0 else 1 - h.y]
        return self.send(block, 4 + half, z, h.at(c=1 - h.c))

    def sib_wait(self, half):
        loop(0, self.nz, lambda k: self.sib(half, k, False).wait_recv())

    def sent(self):
        def on(k):
            for half in (0, 1):
                self.sib(half, k).wait_send()
                self.third(half, k).wait_send()

        loop(0, self.nz, on)
        if self.order == "xzy":
            self.first(0).wait_send()
            loop(1, self.nz, lambda k: self.second(k).wait_send())
        else:
            loop(1, self.nz, lambda k: self.first(k).wait_send())
            loop(0, self.nz, lambda k: self.second(k).wait_send())


class Swap:
    def __init__(self, here, whole, flat, sems, back):
        self.h, self.whole, self.flat, self.sems, self.back = here, whole, flat, sems, back
        self.positions = whole.shape[1]
        self.share = whole.shape[0] // here.nmp

    def views(self, s, outer, inner):
        at = pl.multiple_of((s * self.h.nmp + inner) * self.positions, self.positions)
        return self.whole.at[outer * self.share + s], self.flat.at[pl.ds(at, self.positions)]

    def copy(self, s, k, mine):
        h = self.h
        other = lax.rem(h.mp + (k if mine else h.nmp - k), h.nmp)
        sender, receiver = (h.mp, other) if mine else (other, h.mp)
        if self.back:
            dst, src = self.views(s, sender, receiver)
        else:
            src, dst = self.views(s, receiver, sender)
        if not mine:
            src = dst
        return remote(src, dst, self.sems.at[0, k, s], self.sems.at[1, k, s], (h.dp, other))

    def local(self, s):
        whole, flat = self.views(s, self.h.mp, self.h.mp)
        src, dst = (flat, whole) if self.back else (whole, flat)
        return pltpu.make_async_copy(src, dst, self.sems.at[0, 0, s])

    def start(self):
        for k in range(1, self.h.nmp):
            for s in range(self.share):
                self.copy(s, k, True).start()
        for s in range(self.share):
            self.local(s).start()

    def come(self):
        for k in range(1, self.h.nmp):
            for s in range(self.share):
                self.copy(s, k, False).wait_recv()
        for s in range(self.share):
            self.local(s).wait()

    def sent(self):
        for k in range(1, self.h.nmp):
            for s in range(self.share):
                self.copy(s, k, True).wait_send()


def dot(a, b, ca=1, cb=0, precision=None):
    return lax.dot_general(a, b, (((ca,), (cb,)), ((), ())), preferred_element_type=F32, precision=precision)


def tile_rows(i, size):
    return pl.ds(pl.multiple_of(i * size, size), size)


TILE = 256


def rsq(v):
    return lax.rsqrt(jnp.mean(v * v, axis=-1, keepdims=True) + EPS)


def toeplitz(offsets, ST):
    heads, span = ST.shape[0], ST.shape[2]
    for h in range(heads):
        row = jnp.broadcast_to(offsets[h : h + 1, :], (128, offsets.shape[1]))
        ST[h] = pltpu.roll(row, 0, 1, stride=1, stride_axis=0)[:, :span]


def biased(s, ST, h, i0, dead):
    blocks = s.shape[0] // 128
    width = s.shape[1]
    pieces = []
    for j in range(blocks):
        c0 = 128 * (blocks - 1 - j) + i0
        piece = s[128 * j : 128 * (j + 1)] + ST[h, :, c0 : c0 + width]
        pieces.append(piece if j < blocks // 2 else piece + dead)
    return jnp.concatenate(pieces, 0)


def attend(QV, ST, h, part, dh, seq, dead, base, OV, LV):
    q0, k0, v0 = h * dh, part + h * dh, 2 * part + h * dh
    rows = pl.ds(base, seq)
    keys = QV[rows, k0 : k0 + dh]
    values_t = QV[rows, v0 : v0 + dh].T
    queries = QV[rows, q0 : q0 + dh]
    for i0 in range(0, seq, TILE):
        s = biased(dot(keys, queries[i0 : i0 + TILE], 1, 1), ST, h, i0, dead)
        top = jnp.max(s, axis=0, keepdims=True)
        e = jnp.exp(s - top)
        total = jnp.sum(e, axis=0, keepdims=True)
        out = dot(values_t, e.astype(BF)) * (1.0 / total)
        at = pl.ds(pl.multiple_of(base + i0, TILE), TILE)
        OV[at, h * dh : (h + 1) * dh] = out.astype(BF).T
        LV[h : h + 1, at] = top + jnp.log(total)


def forward_kernel(cfg, tok, cot, wq, wk, wv, wo, wi, wf, table, onehot, gain, lens, *refs):
    W, X, DY, OFF, H, QKV, O, LSE = refs[:8]
    OWN, OFFV, XV, N1, AV, QV, OV, LV, HV, ST = refs[8:18]
    ssem, rsem, tsem, dsem, bsem, lsem, asem, osem = refs[18:]
    ndp, nmp, fine, seq, heads_mp = cfg
    h = Place(ndp, nmp, fine)
    h.greet()
    rows, part = wq.shape
    n, width = XV.shape
    dh = part // heads_mp
    share = n // seq
    OWN[0, :, :part] = wq[...].astype(BF)
    OWN[0, :, part : 2 * part] = wk[...].astype(BF)
    OWN[0, :, 2 * part : 3 * part] = wv[...].astype(BF)
    OWN[0, :, 3 * part :] = wo[...].T.astype(BF)
    OWN[1] = wi[...].astype(BF)
    OWN[2] = wf[...].T.astype(BF)

    def own(p):
        return pltpu.make_async_copy(OWN.at[p], W.at[p, h.x, h.c, h.z, h.y], lsem.at[p])

    for p in range(3):
        own(p).start()
    OFFV[h.mp] = jnp.zeros_like(OFFV[0])
    OFFV[h.mp, :heads_mp] = dot(table[...], onehot[...], 0, 0, HIGHEST)

    def offs(k, mine=True):
        other = lax.rem(h.mp + (k if mine else nmp - k), nmp)
        at = OFFV.at[h.mp if mine else other]
        return remote(at, at, bsem.at[0, k], bsem.at[1, k], (h.dp, other))

    A = Gather(h, 0, "zyx", W, ssem, rsem)
    B = Gather(h, 1, "xzy", W, ssem, rsem)
    C = Gather(h, 2, "zxy", W, ssem, rsem)
    sx = Swap(h, tok, X, tsem, False)
    sd = Swap(h, cot, DY, dsem, False)
    nz = h.nz
    for p in range(3):
        own(p).wait()
    h.met()
    loop(1, nz, lambda k: A.first(k).start())
    A.second(0).start()
    sx.start()
    B.first(0).start()
    for k in range(1, nmp):
        offs(k).start()

    def a_second(k):
        A.first(k, False).wait_recv()
        A.second(k).start()

    loop(1, nz, a_second)
    loop(1, nz, lambda k: C.first(k).start())
    B.first(0, False).wait_recv()
    loop(1, nz, lambda k: B.second(k).start())

    def a_sib(k):
        A.second(k, False).wait_recv()
        A.sib(0, k).start()

    loop(0, nz, a_sib)
    sx.come()
    load_x = pltpu.make_async_copy(X, XV, lsem.at[0])
    load_x.start()

    def a_third(k):
        A.third(0, k).start()
        A.third(1, k).start()

    loop(0, nz, a_third)
    B.third(0, 0).start()
    B.third(1, 0).start()
    B.sib(0, 0).start()
    A.sib_wait(0)

    def group(i):
        return lax.rem(2 * h.x + i, nmp)

    def load_a(i):
        m = group(i)
        return pltpu.make_async_copy(W.at[0, m // 2, m % 2], AV.at[lax.rem(i, 2)], asem.at[lax.rem(i, 2)])

    def store(i):
        m, slot = group(i), lax.rem(i, 2)
        return (
            pltpu.make_async_copy(QV.at[slot], QKV.at[m], osem.at[0, slot]),
            pltpu.make_async_copy(OV.at[slot], O.at[m], osem.at[1, slot]),
            pltpu.make_async_copy(LV.at[slot], LSE.at[m], osem.at[2, slot]),
        )

    load_a(0).start()
    for k in range(1, nmp):
        offs(k, False).wait_recv()
    load_x.wait()

    def norm(t):
        r = tile_rows(t, TILE)
        x = XV[r, :].astype(F32)
        N1[r, :] = (x * rsq(x) * gain[...].reshape(1, width)).astype(BF)
        HV[r, :] = x

    loop(0, n // TILE, norm)

    def tick_b_second():
        def on(k):
            B.second(k, False).wait_recv()
            B.third(0, k).start()
            B.third(1, k).start()
            B.sib(0, k).start()

        loop(1, nz, on)

    def tick_a_third():
        def on(k):
            A.third(0, k, False).wait_recv()
            A.third(1, k, False).wait_recv()
            A.sib(1, k).start()

        loop(0, nz, on)

    def tick_c_first():
        C.second(0).start()
        C.third(0, 0).start()

        def on(k):
            C.first(k, False).wait_recv()
            C.second(k).start()
            C.third(0, k).start()

        loop(1, nz, on)

    def tick_c_second():
        def on(k):
            C.second(k, False).wait_recv()
            C.third(1, k).start()
            C.sib(0, k).start()

        loop(0, nz, on)

    def tick_third(T):
        def on(k):
            T.third(0, k, False).wait_recv()
            T.third(1, k, False).wait_recv()
            T.sib(1, k).start()

        loop(0, nz, on)

    ticks = {
        (0, 1, 2): tick_c_first,
        (1, 0, 1): tick_b_second,
        (1, 1, 2): tick_a_third,
        (2, 0, 0): sd.start,
        (3, 0, 0): tick_c_second,
    }

    def step(i):
        slot = lax.rem(i, 2)
        m = group(i)

        @pl.when(i == 2)
        def _():
            A.sib_wait(1)
            load_a(2).start()

        load_a(i).wait()
        pl.when((i == 0) | (i == 2))(lambda: load_a(i + 1).start())

        @pl.when(i >= 2)
        def _():
            for cp in store(i - 2):
                cp.wait()

        toeplitz(OFFV.at[m], ST)

        def project(t):
            r = tile_rows(t, TILE)
            w = AV[slot, :, :, :, : 3 * part].reshape(width, 3 * part)
            QV[slot, r, :] = dot(N1[r, :], w).astype(BF)

        loop(0, n // TILE, project)

        def pair(p):
            base = pl.multiple_of(p * seq, seq)
            off = jnp.where(lens[h.mp * share + p] < seq, -1e30, 0.0).astype(F32)
            for head in range(heads_mp):
                for (ti, tp, th), fn in ticks.items():
                    if th == head:
                        pl.when((i == ti) & (p == tp))(fn)
                attend(QV.at[slot], ST, head, part, dh, seq, off, base, OV.at[slot], LV.at[slot])

        loop(0, share, pair)

        def join(t):
            r = tile_rows(t, TILE)
            w = AV[slot, :, :, :, 3 * part :].reshape(width, part)
            HV[r, :] += dot(OV[slot, r, :], w, 1, 1)

        loop(0, n // TILE, join)
        for cp in store(i):
            cp.start()

    loop(0, nmp, step)
    out = [pltpu.make_async_copy(HV, H, lsem.at[1]), pltpu.make_async_copy(OFFV, OFF, lsem.at[2])]
    for cp in out:
        cp.start()
    tick_third(B)
    tick_third(C)
    for T in (B, C):
        T.sib_wait(0)
        T.sib_wait(1)
    for T in (A, B, C):
        T.sent()
    sx.sent()
    sd.come()
    sd.sent()
    for k in range(1, nmp):
        offs(k).wait_send()
    for i in (nmp - 2, nmp - 1):
        for cp in store(i):
            cp.wait()
    for cp in out:
        cp.wait()


def forward(tok, cot, ws, table, onehot, gain, lens, ndp, nmp, fine):
    pairs, positions, width = tok.shape
    rows, part = ws[0].shape
    hid = ws[4].shape[1]
    heads_mp = table.shape[1]
    seq = positions * nmp
    share = pairs // nmp
    n = share * seq
    nz = ndp // fine // 2
    any_ = pl.BlockSpec(memory_space=pl.ANY)
    vm = pl.BlockSpec(memory_space=pltpu.VMEM)
    dma = pltpu.SemaphoreType.DMA
    sds = jax.ShapeDtypeStruct
    return pl.pallas_call(
        functools.partial(forward_kernel, (ndp, nmp, fine, seq, heads_mp)),
        out_shape=(
            sds((3, nmp // 2, 2, nz, 2, rows, hid), BF),
            sds((n, width), BF),
            sds((n, width), BF),
            sds((nmp, 8, 2 * seq), F32),
            sds((n, width), F32),
            sds((nmp, n, 3 * part), BF),
            sds((nmp, n, part), BF),
            sds((nmp, 8, n), F32),
        ),
        in_specs=[any_, any_] + [vm] * 9 + [pl.BlockSpec(memory_space=pltpu.SMEM)],
        out_specs=(any_,) * 8,
        scratch_shapes=[
            pltpu.VMEM((3, rows, hid), BF),
            pltpu.VMEM((nmp, 8, 2 * seq), F32),
            pltpu.VMEM((n, width), BF),
            pltpu.VMEM((n, width), BF),
            pltpu.VMEM((2, nz, 2, rows, hid), BF),
            pltpu.VMEM((2, n, 3 * part), BF),
            pltpu.VMEM((2, n, part), BF),
            pltpu.VMEM((2, 8, n), F32),
            pltpu.VMEM((n, width), F32),
            pltpu.VMEM((heads_mp, 128, 2 * seq - 128), F32),
            dma((3, 6, nz)),
            dma((3, 6, nz)),
            dma((2, nmp, share)),
            dma((2, nmp, share)),
            dma((2, nmp)),
            dma((4,)),
            dma((2,)),
            dma((3, 2)),
        ],
        compiler_params=pltpu.CompilerParams(collective_id=0, has_side_effects=True, vmem_limit_bytes=56 * MIB),
    )(tok, cot, *ws, table, onehot, gain, lens)


GELU_C = float(np.sqrt(2.0 / np.pi))


def gelu_both(a):
    a2 = a * a
    t = jnp.tanh(a * (GELU_C + (GELU_C * 0.044715) * a2))
    half = 0.5 + 0.5 * t
    slope = half + (0.5 * a) * (1.0 - t * t) * (GELU_C + (3.0 * GELU_C * 0.044715) * a2)
    return a * half, slope


class Scatter:
    def __init__(self, here, pack, bufs, sems):
        self.h, self.p, self.nz = here, pack, here.nz
        self.MINE, self.R0, self.R1, self.R2, self.R3, self.ACC = [b.at[pack] for b in bufs]
        self.sems = [s.at[pack] for s in sems]
        self.rows = self.R3.shape[0]

    def slot(self, m):
        return jnp.where(m % 2 == self.h.c, m // 2, 2)

    def block(self, z, y):
        return pl.ds(pl.multiple_of((z * 2 + y) * self.rows, self.rows), self.rows)

    def sib(self, x):
        return remote(self.MINE.at[2], self.R0.at[x], self.sems[0].at[x], self.sems[1].at[x], self.h.at(c=1 - self.h.c))

    def ysend(self, x, k):
        h, z = self.h, self.h.zi(k)
        src = self.MINE.at[x, self.block(z, 1 - h.y)]
        return remote(src, self.R1.at[x, z], self.sems[2].at[x, z], self.sems[3].at[x, z], h.at(y=1 - h.y))

    def zsend(self, x, k):
        h, z = self.h, self.h.zi(k)
        return remote(self.R1.at[x, z], self.R2.at[x, h.z], self.sems[4].at[x, z], self.sems[5].at[x, h.z], h.at(z=z))

    def zcome(self, x, k):
        h, z = self.h, self.h.zi(k)
        return remote(self.R2.at[x, z], self.R2.at[x, z], self.sems[4].at[x, z], self.sems[5].at[x, z], h.at(z=z))

    def xsend(self):
        h = self.h
        return remote(self.R1.at[1 - h.x, h.z], self.R3, self.sems[6].at[0], self.sems[7].at[0], h.at(x=1 - h.x))

    def after_group(self, m):
        pl.when(m % 2 != self.h.c)(lambda: self.sib(m // 2).start())

    def before_group(self, m):
        pl.when(m == 3 - self.h.c)(lambda: self.sib(0).wait_send())

    def after_sib(self, x):
        self.sib(x).wait_recv()

        def on(k):
            r = self.block(self.h.zi(k), 1 - self.h.y)
            self.MINE[x, r] = (self.MINE[x, r].astype(F32) + self.R0[x, r].astype(F32)).astype(BF)
            self.ysend(x, k).start()

        loop(0, self.nz, on)

    def after_y(self, x):
        def on(kk):
            k = lax.rem(kk + 1, self.nz)
            z = self.h.zi(k)
            r = self.block(z, self.h.y)
            self.ysend(x, k).wait_recv()
            total = self.MINE[x, r].astype(F32) + self.R0[x, r].astype(F32) + self.R1[x, z].astype(F32)
            self.R1[x, z] = total.astype(BF)
            pl.when(k > 0)(lambda: self.zsend(x, k).start())

        loop(0, self.nz, on)

    def after_z(self, x):
        h = self.h
        loop(1, self.nz, lambda k: self.zcome(x, k).wait_recv())

        def add(k, acc):
            return acc + self.R2[x, h.zi(k)].astype(F32)

        total = lax.fori_loop(1, self.nz, add, self.R1[x, h.z].astype(F32))

        @pl.when(h.x != x)
        def _():
            self.R1[x, h.z] = total.astype(BF)
            self.xsend().start()

        @pl.when(h.x == x)
        def _():
            self.ACC[...] = total

    def result(self):
        self.xsend().wait_recv()
        return self.ACC[...] + self.R3[...].astype(F32)

    def sent(self):
        self.xsend().wait_send()
        self.sib(1).wait_send()
        for x in range(2):
            loop(0, self.nz, lambda k: self.ysend(x, k).wait_send())
            loop(1, self.nz, lambda k: self.zsend(x, k).wait_send())


def attend_back(QV, ST, DO, LV, GQKV, D, h, part, dh, seq, dead, base):
    rows = pl.ds(base, seq)
    q0, k0, v0 = h * dh, part + h * dh, 2 * part + h * dh
    queries = QV[rows, q0 : q0 + dh]
    keys = QV[rows, k0 : k0 + dh]
    values = QV[rows, v0 : v0 + dh]
    keys_t = keys.T
    d_o = DO[rows, h * dh : (h + 1) * dh]
    blocks = seq // 128
    gv = gk = 0.0
    for i0 in range(0, seq, TILE):
        q, do = queries[i0 : i0 + TILE], d_o[i0 : i0 + TILE]
        s = biased(dot(keys, q, 1, 1), ST, h, i0, dead)
        at = pl.ds(pl.multiple_of(base + i0, TILE), TILE)
        prob = jnp.exp(s - LV[h : h + 1, at])
        dprob = dot(values, do, 1, 1)
        weighted = prob * dprob
        delta = jnp.sum(weighted, axis=0, keepdims=True)
        gs = (weighted - prob * delta).astype(BF)
        gv += dot(prob.astype(BF), do)
        gk += dot(gs, q)
        gq = dot(keys_t, gs)
        GQKV[at, q0 : q0 + dh] = gq.astype(BF).T
        for j in range(blocks):
            c0 = 128 * (blocks - 1 - j) + i0
            D[h, :, c0 : c0 + TILE] += gs[128 * j : 128 * (j + 1)].astype(F32)
    GQKV[rows, k0 : k0 + dh] = gk.astype(BF)
    GQKV[rows, v0 : v0 + dh] = gv.astype(BF)


def backward_kernel(cfg, H, X, DY, W, QKV, O, LSE, OFF, gain1, gain2, onehot, lens, *refs):
    L, I, GQ, GK, GV, GO, GI, GF, SMALL = refs[:9]
    HV, XV, DYV, N2, N2T, DYT, U, GA, FF, GN, BV, CV, QV, OV, LV, OFFV, ST, D = refs[9:27]
    bufs, SR, SZ = refs[27:33], refs[33], refs[34]
    lsem, wsem, qsem, tsem, dsem, ssmall, rsmall = refs[35:42]
    sems = refs[42:50]
    ndp, nmp, fine, seq, heads_mp = cfg
    h = Place(ndp, nmp, fine)
    h.greet()
    n, width = HV.shape
    part = OV.shape[2]
    hid = U.shape[1]
    dh = part // heads_mp
    share = n // seq
    tiles = n // TILE
    GQKV, DO = U, GA
    packs = [Scatter(h, p, bufs, sems) for p in range(3)]
    PA, PI, PO = packs
    MINE = bufs[0]

    loads = [pltpu.make_async_copy(a, b, lsem.at[i]) for i, (a, b) in enumerate(((H, HV), (DY, DYV), (X, XV), (OFF, OFFV)))]
    for cp in loads:
        cp.start()

    def load_ff(m):
        slot = lax.rem(m, 2)
        return (
            pltpu.make_async_copy(W.at[1, m // 2, m % 2], BV.at[slot], wsem.at[0, slot]),
            pltpu.make_async_copy(W.at[2, m // 2, m % 2], CV.at[slot], wsem.at[1, slot]),
        )

    def load_attn(m):
        slot = lax.rem(m, 2)
        return (
            pltpu.make_async_copy(W.at[0, m // 2, m % 2], BV.at[slot], wsem.at[0, slot]),
            pltpu.make_async_copy(QKV.at[m], QV.at[slot], qsem.at[0, slot]),
            pltpu.make_async_copy(O.at[m], OV.at[slot], qsem.at[1, slot]),
            pltpu.make_async_copy(LSE.at[m], LV.at[slot], qsem.at[2, slot]),
        )

    def go(copies):
        for cp in copies:
            cp.start()

    def done(copies):
        for cp in copies:
            cp.wait()

    go(load_ff(0))
    SMALL[...] = jnp.zeros_like(SMALL)
    done(loads[:2])

    def prep(t):
        r = tile_rows(t, TILE)
        hid_in = HV[r, :]
        n2 = (hid_in * rsq(hid_in) * gain2[...].reshape(1, width)).astype(BF)
        N2[r, :] = n2
        N2T[:, r] = n2.T
        DYT[:, r] = DYV[r, :].T
        FF[r, :] = hid_in
        GN[r, :] = jnp.zeros((TILE, width), F32)

    loop(0, tiles, prep)

    def ff_group(m):
        slot = lax.rem(m, 2)
        done(load_ff(m))
        pl.when(m + 1 < nmp)(lambda: go(load_ff(m + 1)))

        def rowwise(t):
            r = tile_rows(t, TILE)
            b = BV[slot].reshape(width, hid)
            c = CV[slot].reshape(width, hid)
            a = dot(N2[r, :], b)
            gu = dot(DYV[r, :], c)
            u, slope = gelu_both(a)
            u = u.astype(BF)
            ga = (gu * slope).astype(BF)
            U[r, :] = u
            GA[r, :] = ga
            FF[r, :] += dot(u, c, 1, 1)
            GN[r, :] += dot(ga, b, 1, 1)

        loop(0, tiles, rowwise)

        @pl.when(m == 0)
        def _():
            h.met()

        @pl.when(m == 2)
        def _():
            PI.after_sib(0)
            PO.after_sib(0)

        PI.before_group(m)
        PO.before_group(m)
        to = PI.slot(m)

        def grads(t):
            r = tile_rows(t, TILE)
            MINE[1, to, r, :] = dot(N2T[r, :], GA[...]).astype(BF)
            MINE[2, to, r, :] = dot(DYT[r, :], U[...]).astype(BF)

        loop(0, width // TILE, grads)
        PI.after_group(m)
        PO.after_group(m)

    loop(0, nmp, ff_group)
    go(load_attn(0))
    done(loads[2:])

    def mid(t):
        r = tile_rows(t, TILE)
        hid_in = HV[r, :]
        r2 = rsq(hid_in)
        nh = hid_in * r2
        g = GN[r, :]
        SMALL[1:2, :] += jnp.sum(g * nh, axis=0, keepdims=True)
        e = g * gain2[...].reshape(1, width)
        gh = DYV[r, :].astype(F32) + r2 * (e - nh * jnp.mean(e * nh, axis=-1, keepdims=True))
        DYV[r, :] = FF[r, :].astype(BF)
        HV[r, :] = gh
        low = gh.astype(BF)
        N2[r, :] = low
        DYT[:, r] = low.T
        x = XV[r, :].astype(F32)
        N2T[:, r] = (x * rsq(x) * gain1[...].reshape(1, width)).astype(BF).T
        GN[r, :] = jnp.zeros((TILE, width), F32)

    loop(0, tiles, mid)
    sl = Swap(h, L, DYV, tsem, True)
    si = Swap(h, I, XV, dsem, True)

    ticks = {
        (0, 0, 0): lambda: PI.after_sib(1) or PO.after_sib(1) or sl.start(),
        (0, 1, 0): lambda: PI.after_y(0),
        (0, 1, 1): lambda: PO.after_y(0),
        (2, 0, 0): lambda: PI.after_y(1),
        (2, 0, 1): lambda: PO.after_y(1),
        (2, 0, 2): lambda: PA.after_sib(0),
        (2, 1, 0): lambda: PI.after_z(0) or PO.after_z(0),
        (3, 1, 0): lambda: PA.after_y(0),
    }

    def attn_group(m):
        slot = lax.rem(m, 2)
        done(load_attn(m))
        pl.when(m + 1 < nmp)(lambda: go(load_attn(m + 1)))
        toeplitz(OFFV.at[m], ST)
        D[...] = jnp.zeros_like(D)

        def project(t):
            r = tile_rows(t, TILE)
            w = BV[slot, :, :, :, 3 * part :].reshape(width, part)
            DO[r, :part] = dot(N2[r, :], w).astype(BF)

        loop(0, tiles, project)

        def pair(p):
            base = pl.multiple_of(p * seq, seq)
            off = jnp.where(lens[h.mp * share + p] < seq, -1e30, 0.0).astype(F32)
            for head in range(heads_mp):
                for (tm, tp, th), fn in ticks.items():
                    if th == head:
                        pl.when((m == tm) & (p == tp))(fn)
                attend_back(QV.at[slot], ST, DO, LV.at[slot], GQKV, D, head, part, dh, seq, off, base)

        loop(0, share, pair)
        PA.before_group(m)
        to = PA.slot(m)

        def grads(t):
            r = tile_rows(t, TILE)
            MINE[0, to, r, : 3 * part] = dot(N2T[r, :], GQKV[:, : 3 * part]).astype(BF)
            MINE[0, to, r, 3 * part :] = dot(DYT[r, :], OV[slot]).astype(BF)

        loop(0, width // TILE, grads)
        PA.after_group(m)

        def join(t):
            r = tile_rows(t, TILE)
            w = BV[slot, :, :, :, : 3 * part].reshape(width, 3 * part)
            GN[r, :] += dot(GQKV[r, : 3 * part], w, 1, 1)

        loop(0, tiles, join)
        sums = []
        for head in range(heads_mp):
            wide = jnp.concatenate([D[head], jnp.zeros((128, 128), F32)], 1)
            span = wide.shape[1]
            half = 64
            while half:
                wide = wide[:half] + pltpu.roll(wide[half:], span - half, 1)
                half //= 2
            sums.append(wide)
        sums = jnp.concatenate(sums + [jnp.zeros((8 - heads_mp, span), F32)], 0)
        at = pl.ds(pl.multiple_of(m * 128, 128), 128)
        SMALL[8:16, at] = dot(sums, onehot[...], 1, 1, HIGHEST)

    loop(0, nmp, attn_group)
    PA.after_sib(1)

    def last(t):
        r = tile_rows(t, TILE)
        x = XV[r, :].astype(F32)
        r1 = rsq(x)
        nx = x * r1
        g = GN[r, :]
        SMALL[0:1, :] += jnp.sum(g * nx, axis=0, keepdims=True)
        e = g * gain1[...].reshape(1, width)
        XV[r, :] = (HV[r, :] + r1 * (e - nx * jnp.mean(e * nx, axis=-1, keepdims=True))).astype(BF)

    loop(0, tiles, last)
    si.start()
    PI.after_z(1)
    PO.after_z(1)
    for i, who in enumerate((h.at(c=1 - h.c), h.at(x=1 - h.x), h.at(y=1 - h.y))):
        cp = remote(SMALL, SR.at[i], ssmall.at[i], rsmall.at[i], who)
        cp.start()
        cp.wait()
        SMALL[...] += SR[i]
    SZ[h.z] = SMALL[...]

    def zsmall(k, mine):
        z = h.zi(k)
        at = SZ.at[h.z if mine else z]
        return remote(at, at, ssmall.at[3 + z], rsmall.at[3 + (h.z if mine else z)], h.at(z=z))

    loop(1, h.nz, lambda k: zsmall(k, True).start())
    PA.after_y(1)
    loop(1, h.nz, lambda k: zsmall(k, False).wait_recv())
    SMALL[...] = lax.fori_loop(1, h.nz, lambda z, acc: acc + SZ[z], SZ[0])
    PA.after_z(0)
    GI[...] = PI.result()
    GF[...] = PO.result().T
    PA.after_z(1)
    ga = PA.result()
    GQ[...] = ga[:, :part]
    GK[...] = ga[:, part : 2 * part]
    GV[...] = ga[:, 2 * part : 3 * part]
    GO[...] = ga[:, 3 * part :].T
    for P_ in packs:
        P_.sent()
    loop(1, h.nz, lambda k: zsmall(k, True).wait_send())
    sl.come()
    sl.sent()
    si.come()
    si.sent()


def backward(H, X, DY, W, QKV, O, LSE, OFF, gain1, gain2, onehot, lens, shards, positions, ndp, nmp, fine, heads_mp):
    n, width = H.shape
    _, _, _, nz, _, rows, hid = W.shape
    part = O.shape[2]
    seq = positions * nmp
    share = n // seq
    any_ = pl.BlockSpec(memory_space=pl.ANY)
    vm = pl.BlockSpec(memory_space=pltpu.VMEM)
    dma = pltpu.SemaphoreType.DMA
    sds = jax.ShapeDtypeStruct
    bf = lambda *s: pltpu.VMEM(s, BF)
    fl = lambda *s: pltpu.VMEM(s, F32)
    act = sds((share * nmp, positions, width), BF)
    return pl.pallas_call(
        functools.partial(backward_kernel, (ndp, nmp, fine, seq, heads_mp)),
        out_shape=(act, act) + tuple(sds(s, F32) for s in shards) + (sds((16, width), F32),),
        in_specs=[any_] * 8 + [vm] * 3 + [pl.BlockSpec(memory_space=pltpu.SMEM)],
        out_specs=(any_, any_) + (vm,) * 7,
        scratch_shapes=[
            fl(n, width),
            bf(n, width),
            bf(n, width),
            bf(n, width),
            bf(width, n),
            bf(width, n),
            bf(n, hid),
            bf(n, hid),
            fl(n, width),
            fl(n, width),
            bf(2, nz, 2, rows, hid),
            bf(2, nz, 2, rows, hid),
            bf(2, n, 3 * part),
            bf(2, n, part),
            fl(2, 8, n),
            fl(nmp, 8, 2 * seq),
            fl(heads_mp, 128, 2 * seq - 128),
            fl(heads_mp, 128, 2 * seq - 128),
            bf(3, 3, width, hid),
            bf(3, 2, width, hid),
            bf(3, 2, nz, rows, hid),
            bf(3, 2, nz, rows, hid),
            bf(3, rows, hid),
            fl(3, rows, hid),
            fl(3, 16, width),
            fl(nz, 16, width),
            dma((4,)),
            dma((2, 2)),
            dma((3, 2)),
            dma((2, nmp, share)),
            dma((2, nmp, share)),
            dma((3 + nz,)),
            dma((3 + nz,)),
            dma((3, 2)),
            dma((3, 2)),
            dma((3, 2, nz)),
            dma((3, 2, nz)),
            dma((3, 2, nz)),
            dma((3, 2, nz)),
            dma((3, 1)),
            dma((3, 1)),
        ],
        compiler_params=pltpu.CompilerParams(collective_id=1, has_side_effects=True, vmem_limit_bytes=62 * MIB),
    )(H, X, DY, W, QKV, O, LSE, OFF, gain1, gain2, onehot, lens)


def body(tokens, cotangent, lengths, gain_attn, gain_ff, bias_table, w_query, w_key, w_value, w_out_attn, w_in_ff, w_out_ff):
    ndp, nmp = lax.axis_size("dp"), lax.axis_size("mp")
    positions = tokens.shape[1]
    seq = positions * nmp
    buckets, heads_mp = bias_table.shape
    fine = 16 // math.gcd(w_query.shape[0], 16)
    groups = [list(range(g, g + fine)) for g in range(0, ndp, fine)]

    def join(a, dim):
        return a if fine == 1 else lax.all_gather(a, "dp", axis=dim, tiled=True, axis_index_groups=groups)

    def split(a, dim):
        if fine == 1:
            return a
        return lax.psum_scatter(a, "dp", scatter_dimension=dim, tiled=True, axis_index_groups=groups)

    dims = (0, 0, 0, 1, 0, 1)
    ws = tuple(join(w, d) for w, d in zip((w_query, w_key, w_value, w_out_attn, w_in_ff, w_out_ff), dims))
    place = np.arange(2 * seq)
    place = np.where(place < 2 * seq - 128, seq - 128 - place, seq - 128 + 2 * seq - place)
    onehot = (bucket_of(place, buckets)[None] == np.arange(128)[:, None]).astype(np.float32)
    W, X, DY, OFF, H, QKV, O, LSE = forward(
        tokens, cotangent, ws, bias_table, onehot[:buckets], gain_attn, lengths, ndp, nmp, fine
    )
    layer, ing, *grads, small = backward(
        H, X, DY, W, QKV, O, LSE, OFF, gain_attn, gain_ff, onehot, lengths, [w.shape for w in ws],
        positions, ndp, nmp, fine, heads_mp,
    )
    if fine > 1:
        small = lax.psum(small, "dp", axis_index_groups=groups)
    gb = lax.dynamic_slice(small, (8, lax.axis_index("mp") * 128), (heads_mp, buckets)).T
    return (layer, ing, small[0], small[1], gb) + tuple(split(g, d) for g, d in zip(grads, dims))


def solution(mesh):
    act = P("dp", "mp", None)
    rows, cols = P("dp", "mp"), P("mp", "dp")
    return jax.shard_map(
        body,
        mesh=mesh,
        in_specs=(act, act, P("dp"), P(), P(), P(None, "mp"), rows, rows, rows, cols, rows, cols),
        out_specs=(act, act, P(), P(), P(None, "mp"), rows, rows, rows, cols, rows, cols),
        check_vma=False,
    )
```

```python
import functools
import math

import jax
import jax.numpy as jnp
import numpy as np
from jax import lax
from jax.experimental import pallas as pl
from jax.experimental.pallas import tpu as pltpu
from jax.sharding import PartitionSpec as P

BF = jnp.bfloat16
F32 = jnp.float32
MESH = pl.DeviceIdType.MESH
EPS = 1e-06
FAR = 128
HIGHEST = lax.Precision.HIGHEST
MIB = 2**20


def bucket_of(offset, count):
    half = count // 2
    upper = (offset > 0).astype(np.int64) * half
    distance = np.abs(offset)
    exact = half // 2
    scaled = np.log(np.maximum(distance, 1) / exact) / np.log(FAR / exact) * (half - exact)
    larger = np.minimum(exact + scaled.astype(np.int64), half - 1)
    return (upper + np.where(distance < exact, distance, larger)).astype(np.int32)

PLAN = {
    ("start", 0): ("C.Y0", "A.X0",),
    ("start", 1): ("A.plane2",),
    ("start", 2): ("B.Y0",),
    ("start", 3): ("B.Zs", "dy",),
    ("attend", 0): ("A.z2y",),
    ("attend", 2): ("A.ds", "C.Zs", "B.zy",),
    ("attend", 3): ("B.Xs",),
    ("attend", 4): ("C.zy", "B.ys", "C.Xs",),
    ("attend", 7): ("B.xd", "C.ys", "C.DX",),
    ("ff", 3): ("C.xd",),
    ("ff", 4): ("B.ds",),
    ("ff", 9): ("C.ds",),
    ("ff", 11): ("PO.sw0",),
    ("ff", 19): ("PO.yw0",),
    ("ff", 21): ("PO.sw1", "PI.xs0",),
    ("back", 0): ("lay", "PO.yw1", "PO.st1",),
    ("back", 1): ("PO.st0",),
    ("back", 2): ("PI.xs1", "PI.xw0", "PO.yt0",),
    ("back", 3): ("PA.st0", "PO.yt1",),
    ("back", 4): ("PI.xy0", "PA.st1", "PA.yt0",),
    ("back", 6): ("PI.xw1", "PO.zt0", "PA.yt1",),
    ("back", 7): ("PI.xy1", "PA.sw0",),
    ("end", 1): ("PA.yw0",),
    ("end", 3): ("PO.zw1", "PA.sw1",),
    ("end", 4): ("PI.zo1",),
    ("end", 5): ("PI.zo0", "PA.zw0", "PA.zt1", "PO.zt1", "PA.zt0", "PA.yw1", "PO.zw0", "PA.zw1",),
}
MODES = {"A": "plane", "B": "zxy", "C": "half"}
X_FIRST = {"PA": False, "PI": True, "PO": False}
A_BY_HOPS = True


class Place:
    def __init__(self, ndp, nmp, fine, rows):
        self.dp, self.mp = lax.axis_index("dp"), lax.axis_index("mp")
        self.x, self.c = self.mp // 2, self.mp % 2
        self.fine = fine
        self.z, self.y = self.dp // fine // 2, self.dp // fine % 2
        self.nz = ndp // fine // 2
        self.nmp, self.rows = nmp, rows

    def at(self, x=None, c=None, z=None, y=None):
        x = self.x if x is None else x
        c = self.c if c is None else c
        z = self.z if z is None else z
        y = self.y if y is None else y
        return ((z * 2 + y) * self.fine + self.dp % self.fine, x * 2 + c)

    def zi(self, k):
        return lax.rem(self.z + k, self.nz)

    def block(self, z, y, count=1):
        return pl.ds(pl.multiple_of((z * 2 + y) * self.rows, self.rows), count * self.rows)

    def greet(self):
        bar = pltpu.get_barrier_semaphore()

        def tell(who):
            pl.semaphore_signal(bar, inc=1, device_id=who, device_id_type=MESH)

        tell(self.at(c=1 - self.c))
        tell(self.at(x=1 - self.x))
        tell(self.at(x=1 - self.x, c=1 - self.c))
        tell(self.at(y=1 - self.y))
        loop(1, self.nz, lambda k: tell(self.at(z=self.zi(k))))

    def met(self):
        pl.semaphore_wait(pltpu.get_barrier_semaphore(), 4 + self.nz - 1)


def remote(src, dst, ssem, rsem, who):
    return pltpu.make_async_remote_copy(
        src_ref=src, dst_ref=dst, send_sem=ssem, recv_sem=rsem, device_id=who, device_id_type=MESH
    )


def loop(lo, hi, fn):
    def step(k, carry):
        fn(k)
        return carry

    lax.fori_loop(lo, hi, step, 0)


class Gather:
    def __init__(self, here, pack, mode, W, ssem, rsem):
        self.h, self.nz, self.mode = here, here.nz, mode
        self.W = W.at[pack]
        self.ss, self.rs = ssem.at[pack], rsem.at[pack]

    def at(self, x, c, z, y):
        return self.W.at[x, c, self.h.block(z, y)]

    def send(self, src, kind, idx, who, skind=None, sidx=None):
        skind = kind if skind is None else skind
        sidx = idx if sidx is None else sidx
        return remote(src, src, self.ss.at[skind, sidx], self.rs.at[kind, idx], who)

    def hop(self, b, step):
        h = self.h
        return self.send(self.at(h.x, h.c, b, h.y), 0, b, h.at(z=h.z + step), 0 if step > 0 else 7)

    def z(self, z, mine=True):
        h = self.h
        b = h.z if mine else z
        return self.send(self.at(h.x, h.c, b, h.y), 0, b, h.at(z=z), sidx=z)

    def y(self, z, mine=True):
        h = self.h
        return self.send(self.at(h.x, h.c, z, h.y if mine else 1 - h.y), 1, z, h.at(y=1 - h.y))

    def x(self, z, mine=True):
        h = self.h
        return self.send(self.at(h.x if mine else 1 - h.x, h.c, z, h.y), 2, z, h.at(x=1 - h.x))

    def diag_by_x(self, z):
        h = self.h
        return self.send(self.at(h.x, h.c, z, 1 - h.y), 3, z, h.at(x=1 - h.x))

    def diag_by_y(self, z):
        h = self.h
        return self.send(self.at(1 - h.x, h.c, z, h.y), 3, z, h.at(y=1 - h.y))

    def diag(self, z):
        h = self.h
        return self.send(self.at(1 - h.x, h.c, z, 1 - h.y), 3, z, h.at(x=1 - h.x))

    def z2(self, z, mine=True):
        h = self.h
        b = h.z if mine else z
        return self.send(self.at(1 - h.x, h.c, b, h.y), 4, b, h.at(z=z), sidx=z)

    def sib(self, half, z, mine=True):
        h = self.h
        block = self.W.at[h.x if half == 0 else 1 - h.x, h.c if mine else 1 - h.c, h.block(z, 0, 2)]
        return self.send(block, 5 + half, z, h.at(c=1 - h.c))

    def sib_wait(self, half):
        self.all(lambda z: self.sib(half, z, False).wait_recv())

    def all(self, fn):
        loop(0, self.nz, lambda k: fn(self.h.zi(k)))

    def others(self, fn):
        loop(1, self.nz, lambda k: fn(self.h.zi(k)))

    def by_x(self, z, fn):
        if self.mode == "half":
            pl.when(z % 2 == 0)(fn)

    def by_y(self, z, fn):
        if self.mode == "half":
            pl.when(z % 2 == 1)(fn)
        else:
            fn()

    def hops(self):
        h = self.h
        for step in (1, -1):
            pl.when((h.z + step >= 0) & (h.z + step < self.nz))(lambda: self.hop(h.z, step).start())
        self.y(h.z).start()

    def hops_on(self):
        h = self.h

        def on(d):
            for step in (1, -1):
                b = h.z - step * d

                @pl.when((b >= 0) & (b < self.nz))
                def _():
                    self.z(b, False).wait_recv()
                    pl.when((h.z + step >= 0) & (h.z + step < self.nz))(lambda: self.hop(b, step).start())
                    self.y(b).start()

        loop(1, self.nz, on)

    def hops_sent(self):
        h = self.h

        def on(b):
            pl.when((b <= h.z) & (h.z + 1 < self.nz))(lambda: self.hop(b, 1).wait_send())
            pl.when((b >= h.z) & (h.z >= 1))(lambda: self.hop(b, -1).wait_send())

        loop(0, self.nz, on)

    def steps(self):
        h = self.h

        def zy(z):
            self.z(z, False).wait_recv()
            self.y(z).start()

        def ys(z):
            self.y(z, False).wait_recv()
            self.sib(0, z).start()

        def z2y(z):
            self.z2(z, False).wait_recv()
            self.diag_by_y(z).start()

        def xd(z):
            self.x(z, False).wait_recv()
            self.by_y(z, lambda: self.diag_by_y(z).start())

        def ds(z):
            self.diag(z).wait_recv()
            self.sib(1, z).start()

        def plane2():
            self.x(h.z, False).wait_recv()
            self.others(lambda z: self.z2(z).start())
            self.diag_by_y(h.z).start()

        return {
            "Zs": lambda: self.others(lambda z: self.z(z).start()),
            "Y0": lambda: self.y(h.z).start(),
            "zy": lambda: self.others(zy),
            "ys": lambda: self.all(ys),
            "X0": lambda: self.x(h.z).start(),
            "plane2": plane2,
            "z2y": lambda: self.others(z2y),
            "Xs": lambda: self.all(lambda z: self.x(z).start()),
            "DX": lambda: self.all(lambda z: self.by_x(z, lambda: self.diag_by_x(z).start())),
            "xd": lambda: self.all(xd),
            "ds": lambda: self.all(ds),
        }

    def sent(self):
        self.all(lambda z: self.y(z).wait_send())
        self.all(lambda z: self.sib(0, z).wait_send())
        self.all(lambda z: self.sib(1, z).wait_send())
        if self.mode == "plane":
            self.x(self.h.z).wait_send()
            self.others(lambda z: self.z2(z).wait_send())
            self.all(lambda z: self.diag_by_y(z).wait_send())
        else:
            self.all(lambda z: self.x(z).wait_send())
            self.all(lambda z: self.by_x(z, lambda: self.diag_by_x(z).wait_send()))
            self.all(lambda z: self.by_y(z, lambda: self.diag_by_y(z).wait_send()))


class Swap:
    def __init__(self, here, whole, flat, sems, back):
        self.h, self.whole, self.flat, self.sems, self.back = here, whole, flat, sems, back
        self.positions = whole.shape[1]
        self.share = whole.shape[0] // here.nmp

    def views(self, s, outer, inner):
        at = pl.multiple_of((s * self.h.nmp + inner) * self.positions, self.positions)
        return self.whole.at[outer * self.share + s], self.flat.at[pl.ds(at, self.positions)]

    def copy(self, s, k, mine):
        h = self.h
        other = lax.rem(h.mp + (k if mine else h.nmp - k), h.nmp)
        sender, receiver = (h.mp, other) if mine else (other, h.mp)
        if self.back:
            dst, src = self.views(s, sender, receiver)
        else:
            src, dst = self.views(s, receiver, sender)
        if not mine:
            src = dst
        return remote(src, dst, self.sems.at[0, k, s], self.sems.at[1, k, s], (h.dp, other))

    def local(self, s):
        whole, flat = self.views(s, self.h.mp, self.h.mp)
        src, dst = (flat, whole) if self.back else (whole, flat)
        return pltpu.make_async_copy(src, dst, self.sems.at[0, 0, s])

    def start(self, s):
        for k in range(1, self.h.nmp):
            self.copy(s, k, True).start()
        self.local(s).start()

    def start_all(self):
        for s in range(self.share):
            self.start(s)

    def come(self):
        for s in range(self.share):
            for k in range(1, self.h.nmp):
                self.copy(s, k, False).wait_recv()
            self.local(s).wait()

    def sent(self):
        for s in range(self.share):
            for k in range(1, self.h.nmp):
                self.copy(s, k, True).wait_send()


class Scatter:
    def __init__(self, here, pack, x_first, mine, bufs, RES, sems):
        self.h, self.nz, self.x_first = here, here.nz, x_first
        self.MINE, self.SENT = mine
        self.R0, self.R1, self.R2, self.R3 = [b.at[pack] for b in bufs]
        self.RES = RES.at[pack]
        self.sems = [s.at[pack] for s in sems]
        self.block = here.block

    def half(self, own):
        return self.h.x if own else 1 - self.h.x

    def put(self, m, columns, value):
        @pl.when(m % 2 == self.h.c)
        def _():
            self.MINE[m // 2, :, columns] = value

        @pl.when(m % 2 != self.h.c)
        def _():
            self.SENT[:, columns] = value

    def two(self, x, r):
        return self.MINE[x, r].astype(F32) + self.R0[x, r].astype(F32)

    def sib(self, x):
        return remote(self.SENT, self.R0.at[x], self.sems[0].at[x], self.sems[1].at[x], self.h.at(c=1 - self.h.c))

    def ysend(self, x, z):
        h = self.h
        src = self.MINE.at[x, self.block(z, 1 - h.y)]
        return remote(src, self.R1.at[x, z], self.sems[2].at[x, z], self.sems[3].at[x, z], h.at(y=1 - h.y))

    def zsend(self, x, z):
        h = self.h
        return remote(self.R1.at[x, z], self.R2.at[x, h.z], self.sems[4].at[x, z], self.sems[5].at[x, h.z], h.at(z=z))

    def zcome(self, x, z):
        h = self.h
        return remote(self.R2.at[x, z], self.R2.at[x, z], self.sems[4].at[x, z], self.sems[5].at[x, z], h.at(z=z))

    def xsend(self):
        h = self.h
        return remote(self.R1.at[1 - h.x, h.z], self.R3, self.sems[6].at[0], self.sems[7].at[0], h.at(x=1 - h.x))

    def xall(self, z, y_is_own, mine=True):
        h = self.h
        i = 2 if y_is_own else 4
        to = h.x if mine else 1 - h.x
        src = self.MINE.at[1 - h.x, self.block(z, h.y if y_is_own else 1 - h.y)]
        dst = (self.R1 if y_is_own else self.R2).at[to, z]
        return remote(src, dst, self.sems[i].at[1 - h.x, z], self.sems[i + 1].at[to, z], h.at(x=1 - h.x))

    def after_group(self, m):
        pl.when(m % 2 != self.h.c)(lambda: self.sib(m // 2).start())

    def before_group(self, m, i):
        pl.when((m % 2 != self.h.c) & (i >= 2))(lambda: self.sib(1 - m // 2).wait_send())

    def sib_sent(self, own):
        self.sib(self.half(own)).wait_send()

    def each(self, fn):
        loop(1, self.nz + 1, lambda k: fn(self.h.zi(k)))

    def others(self, fn):
        loop(1, self.nz, lambda k: fn(self.h.zi(k)))

    def after_sib(self, own):
        x = self.half(own)
        self.sib(x).wait_recv()

        def on(z):
            r = self.block(z, 1 - self.h.y)
            self.MINE[x, r] = self.two(x, r).astype(BF)
            self.ysend(x, z).start()

        self.each(on)

    def after_y(self, own):
        x = self.half(own)

        def on(z):
            self.ysend(x, z).wait_recv()
            total = self.two(x, self.block(z, self.h.y)) + self.R1[x, z].astype(F32)
            self.R1[x, z] = total.astype(BF)
            pl.when(z != self.h.z)(lambda: self.zsend(x, z).start())

        self.each(on)

    def after_z(self, own):
        h, x = self.h, self.half(own)
        self.others(lambda z: self.zcome(x, z).wait_recv())

        def add(k, acc):
            return acc + self.R2[x, h.zi(k)].astype(F32)

        total = lax.fori_loop(1, self.nz, add, self.R1[x, h.z].astype(F32))
        if own:
            self.RES[...] = total
        else:
            self.R1[x, h.z] = total.astype(BF)
            self.xsend().start()

    def to_x(self):
        x = self.half(False)
        self.sib(x).wait_recv()

        def on(z):
            for y_is_own in (True, False):
                r = self.block(z, self.h.y if y_is_own else 1 - self.h.y)
                self.MINE[x, r] = self.two(x, r).astype(BF)
                self.xall(z, y_is_own).start()

        self.each(on)

    def after_x(self):
        x = self.half(True)
        self.sib(x).wait_recv()

        def on(z):
            r = self.block(z, 1 - self.h.y)
            self.xall(z, False, False).wait_recv()
            self.MINE[x, r] = (self.two(x, r) + self.R2[1 - x, z].astype(F32)).astype(BF)
            self.ysend(x, z).start()

        self.each(on)

    def after_x_and_y(self):
        x = self.half(True)

        def on(z):
            self.xall(z, True, False).wait_recv()
            self.ysend(x, z).wait_recv()
            total = self.two(x, self.block(z, self.h.y)) + self.R1[x, z].astype(F32) + self.R1[1 - x, z].astype(F32)
            self.R1[x, z] = total.astype(BF)
            pl.when(z != self.h.z)(lambda: self.zsend(x, z).start())

        self.each(on)

    def steps(self):
        out = {}
        if self.x_first:
            fns = {"xs": self.to_x, "xw": self.after_x, "xy": self.after_x_and_y, "zo": lambda: self.after_z(True)}
        else:
            fns = {}
            for tag, own in (("w", True), ("t", False)):
                fns["s" + tag] = functools.partial(self.after_sib, own)
                fns["y" + tag] = functools.partial(self.after_y, own)
                fns["z" + tag] = functools.partial(self.after_z, own)
        for name, fn in fns.items():
            for c in (0, 1):
                out[name + str(c)] = functools.partial(self.on_core, c, fn)
        return out

    def on_core(self, c, fn):
        pl.when(self.h.c == c)(fn)

    def result(self):
        if not self.x_first:
            self.xsend().wait_recv()
            self.RES[...] += self.R3[...].astype(F32)

    def sent(self):
        own, other = self.half(True), self.half(False)
        for x in (own,) if self.x_first else (own, other):
            self.each(lambda z: self.ysend(x, z).wait_send())
            self.others(lambda z: self.zsend(x, z).wait_send())
        if self.x_first:
            self.each(lambda z: self.xall(z, True).wait_send())
            self.each(lambda z: self.xall(z, False).wait_send())
        else:
            self.xsend().wait_send()


def dot(a, b, ca=1, cb=0, precision=None):
    return lax.dot_general(a, b, (((ca,), (cb,)), ((), ())), preferred_element_type=F32, precision=precision)


def tile_rows(i, size):
    return pl.ds(pl.multiple_of(i * size, size), size)


TILE = 256


def rsq(v):
    return lax.rsqrt(jnp.mean(v * v, axis=-1, keepdims=True) + EPS)


def toeplitz(offsets, ST):
    heads, span = ST.shape[0], ST.shape[2]
    for h in range(heads):
        row = jnp.broadcast_to(offsets[h : h + 1, :], (128, offsets.shape[1]))
        ST[h] = pltpu.roll(row, 0, 1, stride=1, stride_axis=0)[:, :span]


def biased(s, ST, h, dead):
    blocks = s.shape[0] // 128
    pieces = []
    for j in range(blocks):
        c0 = 128 * (blocks - 1 - j)
        piece = s[128 * j : 128 * (j + 1)] + ST[h, :, c0 : c0 + s.shape[1]]
        pieces.append(piece if j < blocks // 2 else piece + dead)
    return jnp.concatenate(pieces, 0)


def attend(QV, ST, h, part, dh, seq, dead, base, OV, LV):
    q0, k0, v0 = h * dh, part + h * dh, 2 * part + h * dh
    rows = pl.ds(base, seq)
    queries, keys, values = QV[rows, q0 : q0 + dh], QV[rows, k0 : k0 + dh], QV[rows, v0 : v0 + dh]
    s = biased(dot(keys, queries, 1, 1), ST, h, dead)
    top = jnp.max(s, axis=0, keepdims=True)
    e = jnp.exp(s - top)
    total = jnp.sum(e, axis=0, keepdims=True)
    prob = (e * (1.0 / total)).astype(BF)
    OV[rows, h * dh : (h + 1) * dh] = dot(prob, values, 0, 0).astype(BF)
    LV[h : h + 1, rows] = top + jnp.log(total)


GELU_C = float(np.sqrt(2.0 / np.pi))


def gelu_both(a):
    a2 = a * a
    t = jnp.tanh(a * (GELU_C + (GELU_C * 0.044715) * a2))
    half = 0.5 + 0.5 * t
    slope = half + (0.5 * a) * (1.0 - t * t) * (GELU_C + (3.0 * GELU_C * 0.044715) * a2)
    return a * half, slope


def attend_back(QV, ST, DO, LV, GQKV, D, h, part, dh, seq, dead, base):
    rows = pl.ds(base, seq)
    q0, k0, v0 = h * dh, part + h * dh, 2 * part + h * dh
    queries, keys, values = QV[rows, q0 : q0 + dh], QV[rows, k0 : k0 + dh], QV[rows, v0 : v0 + dh]
    d_o = DO[rows, h * dh : (h + 1) * dh]
    s = biased(dot(keys, queries, 1, 1), ST, h, dead)
    prob = jnp.exp(s - LV[h : h + 1, rows])
    dprob = dot(values, d_o, 1, 1)
    weighted = prob * dprob
    delta = jnp.sum(weighted, axis=0, keepdims=True)
    gs = (weighted - prob * delta).astype(BF)
    GQKV[rows, v0 : v0 + dh] = dot(prob.astype(BF), d_o).astype(BF)
    GQKV[rows, k0 : k0 + dh] = dot(gs, queries).astype(BF)
    GQKV[rows, q0 : q0 + dh] = dot(keys.T, gs).astype(BF).T
    blocks = seq // 128
    for d in range(1 - blocks, blocks):
        c0 = 128 * (blocks - 1 - d)
        acc = D[h, :, c0 : c0 + 128]
        for j in range(max(0, d), min(blocks, blocks + d)):
            acc += gs[128 * j : 128 * (j + 1), 128 * (j - d) : 128 * (j - d + 1)].astype(F32)
        D[h, :, c0 : c0 + 128] = acc


def layer_kernel(cfg, tok, cot, wq, wk, wv, wo, wi, wf_t, table_t, onehot, gain1, gain2, lens, *refs):
    ndp, nmp, fine, seq, heads_mp = cfg
    L, I, RES, SMALL, W, QKV, O, LSE = refs[:8]
    OWN, OFFV, XV, DYV, N2, N2T, DYT, U, GA, HV, FF, GN, BV, CV, QV, OV, LV, ST, D = refs[8:27]
    FFMINE, SENT = refs[27:29]
    bufs, SR, SZ = refs[29:33], refs[33], refs[34]
    ssem, rsem, xsem, dysem, lsem, isem, bsem, osem, wsem, qsem, ssmall, rsmall, csem = refs[35:48]
    sems = refs[48:56]
    rows, part = wq.shape
    h = Place(ndp, nmp, fine, rows)
    h.greet()
    n, width = XV.shape
    hid = U.shape[1]
    dh = part // heads_mp
    share = n // seq
    tiles = n // TILE
    nz = h.nz

    def gain(ref):
        return ref[...].reshape(1, width)

    def go(copies):
        for cp in copies:
            cp.start()

    def done(copies):
        for cp in copies:
            cp.wait()

    def run(section, at, static=None, period=1):
        for (name, slot), steps in PLAN.items():
            if name == section and (slot == at if static is None else slot % period in static):

                def fn(steps=steps):
                    for step in steps:
                        ACTIONS[step]()

                if static is None:
                    fn()
                else:
                    pl.when(at == slot)(fn)

    OWN[0, :, :part] = wq[...].astype(BF)
    OWN[0, :, part : 2 * part] = wk[...].astype(BF)
    OWN[0, :, 2 * part : 3 * part] = wv[...].astype(BF)
    OWN[0, :, 3 * part :] = wo[...].T.astype(BF)
    OWN[1] = wi[...].astype(BF)
    OWN[2] = wf_t[...].astype(BF)
    own = [pltpu.make_async_copy(OWN.at[p], W.at[p, h.x, h.c, h.block(h.z, h.y)], csem.at[p]) for p in range(3)]
    go(own)
    OFFV[h.mp] = jnp.zeros_like(OFFV[0])
    OFFV[h.mp, :heads_mp] = dot(table_t[...], onehot[: table_t.shape[1], :], 1, 0, HIGHEST)

    def offs(k, mine=True):
        other = lax.rem(h.mp + (k if mine else nmp - k), nmp)
        at = OFFV.at[h.mp if mine else other]
        return remote(at, at, bsem.at[0, k], bsem.at[1, k], (h.dp, other))

    A, B, C = [Gather(h, p, MODES[name], W, ssem, rsem) for p, name in enumerate("ABC")]
    mines = (CV, SENT.at[0]), (FFMINE.at[0], SENT.at[0]), (FFMINE.at[1], SENT.at[1])
    PA, PI, PO = [
        Scatter(h, p, X_FIRST[name], mines[p], bufs, RES, sems) for p, name in enumerate(("PA", "PI", "PO"))
    ]
    sx = Swap(h, tok, XV, xsem, False)
    sd = Swap(h, cot, DYV, dysem, False)
    sl = Swap(h, L, DYV, lsem, True)
    si = Swap(h, I, XV, isem, True)

    ACTIONS = {"dy": sd.start_all, "lay": sl.start_all}
    for name, part_of in (("A", A), ("B", B), ("C", C), ("PA", PA), ("PI", PI), ("PO", PO)):
        ACTIONS.update({name + "." + step: fn for step, fn in part_of.steps().items()})

    done(own)
    h.met()
    if A_BY_HOPS:
        A.hops()
    else:
        ACTIONS["A.Zs"]()
        ACTIONS["A.Y0"]()
    sx.start_all()
    for k in range(1, nmp):
        offs(k).start()
    run("start", 0)
    if A_BY_HOPS:
        A.hops_on()
    else:
        ACTIONS["A.zy"]()
    run("start", 1)
    ACTIONS["A.ys"]()
    run("start", 2)
    sx.come()
    run("start", 3)
    A.sib_wait(0)

    def group(i):
        return lax.rem(2 * h.x + i, nmp)

    def load(p, i, m, V, sem):
        slot = lax.rem(i, 2)
        return pltpu.make_async_copy(W.at[p, m // 2, m % 2], V.at[slot], sem.at[slot])

    def load_a(i):
        return load(0, i, group(i), BV, wsem.at[0])

    def store(i):
        m, slot = group(i), lax.rem(i, 2)
        return (
            pltpu.make_async_copy(QV.at[slot], QKV.at[m], osem.at[0, slot]),
            pltpu.make_async_copy(OV.at[slot], O.at[m], osem.at[1, slot]),
            pltpu.make_async_copy(LV.at[slot], LSE.at[m], osem.at[2, slot]),
        )

    load_a(0).start()
    for k in range(1, nmp):
        offs(k, False).wait_recv()

    def norm(t):
        r = tile_rows(t, TILE)
        x = XV[r, :].astype(F32)
        N2[r, :] = (x * rsq(x) * gain(gain1)).astype(BF)
        HV[r, :] = x

    loop(0, tiles, norm)

    def attn_group(i):
        slot = lax.rem(i, 2)
        m = group(i)

        @pl.when(i == 2)
        def _():
            A.sib_wait(1)
            load_a(2).start()

        load_a(i).wait()
        pl.when((i == 0) | (i == 2))(lambda: load_a(i + 1).start())
        pl.when(i >= 2)(lambda: done(store(i - 2)))
        toeplitz(OFFV.at[m], ST)

        QV[slot] = dot(N2[...], BV[slot, :, : 3 * part]).astype(BF)

        def pair(p):
            base = pl.multiple_of(p * seq, seq)
            off = jnp.where(lens[h.mp * share + p] < seq, -1e30, 0.0).astype(F32)
            run("attend", i * share + p, range(1))
            for head in range(heads_mp):
                attend(QV.at[slot], ST, head, part, dh, seq, off, base, OV.at[slot], LV.at[slot])

        loop(0, share, pair)

        HV[...] += dot(OV[slot], BV[slot, :, 3 * part :], 1, 1)
        go(store(i))

    loop(0, nmp, attn_group)

    run("between", 0)

    def load_ff(i):
        m = group(i)
        return load(1, i, m, BV, wsem.at[0]), load(2, i, m, CV, wsem.at[1])

    sd.come()
    SMALL[...] = jnp.zeros_like(SMALL)

    def prep(t):
        r = tile_rows(t, TILE)
        hidden = HV[r, :]
        n2 = (hidden * rsq(hidden) * gain(gain2)).astype(BF)
        N2[r, :] = n2
        N2T[:, r] = n2.T
        DYT[:, r] = DYV[r, :].T
        FF[r, :] = hidden
        GN[r, :] = jnp.zeros((TILE, width), F32)

    loop(0, tiles, prep)
    run("between", 1)
    B.sib_wait(0)
    C.sib_wait(0)
    go(load_ff(0))

    steps = tiles + 2

    def ff_group(i):
        slot = lax.rem(i, 2)
        m = group(i)
        done(load_ff(i))
        pl.when((i == 0) | (i == 2))(lambda: go(load_ff(i + 1)))

        def rowwise(t):
            run("ff", i * steps + t, range(tiles), steps)
            r = tile_rows(t, TILE)
            b = BV[slot]
            c = CV[slot]
            a = dot(N2[r, :], b)
            gu = dot(DYV[r, :], c)
            u, slope = gelu_both(a)
            u = u.astype(BF)
            ga = (gu * slope).astype(BF)
            U[r, :] = u
            GA[r, :] = ga
            FF[r, :] += dot(u, c, 1, 1)
            GN[r, :] += dot(ga, b, 1, 1)

        loop(0, tiles, rowwise)
        PI.before_group(m, i)
        PO.before_group(m, i)

        run("ff", i * steps + tiles, (tiles,), steps)
        PI.put(m, slice(None), dot(N2T[...], GA[...]).astype(BF))
        run("ff", i * steps + tiles + 1, (tiles + 1,), steps)
        PO.put(m, slice(None), dot(DYT[...], U[...]).astype(BF))
        PI.after_group(m)
        PO.after_group(m)

        @pl.when(i == 1)
        def _():
            run("between", 2)
            B.sib_wait(1)
            C.sib_wait(1)
            go(load_ff(2))

    loop(0, nmp, ff_group)

    def back_group(i):
        return lax.rem(2 * (1 - h.x) + i, nmp)

    def load_attn(i):
        m, slot = back_group(i), lax.rem(i, 2)
        return (
            load(0, i, m, BV, wsem.at[0]),
            pltpu.make_async_copy(QKV.at[m], QV.at[slot], qsem.at[0, slot]),
            pltpu.make_async_copy(O.at[m], OV.at[slot], qsem.at[1, slot]),
            pltpu.make_async_copy(LSE.at[m], LV.at[slot], qsem.at[2, slot]),
        )

    for i in (nmp - 2, nmp - 1):
        done(store(i))
    go(load_attn(0))
    run("between", 3)

    def mid(t):
        r = tile_rows(t, TILE)
        hidden = HV[r, :]
        r2 = rsq(hidden)
        nh = hidden * r2
        g = GN[r, :]
        SMALL[1:2, :] += jnp.sum(g * nh, axis=0, keepdims=True)
        e = g * gain(gain2)
        gh = DYV[r, :].astype(F32) + r2 * (e - nh * jnp.mean(e * nh, axis=-1, keepdims=True))
        DYV[r, :] = FF[r, :].astype(BF)
        HV[r, :] = gh
        low = gh.astype(BF)
        N2[r, :] = low
        DYT[:, r] = low.T
        x = XV[r, :].astype(F32)
        N2T[:, r] = (x * rsq(x) * gain(gain1)).astype(BF).T
        GN[r, :] = jnp.zeros((TILE, width), F32)
        U[r, 3 * part :] = jnp.zeros((TILE, hid - 3 * part), BF)

    loop(0, tiles, mid)

    GQKV, DO = U, GA
    wide = -(-3 * part // 128) * 128

    def last(p, t):
        r = pl.ds(pl.multiple_of(p * seq + t * TILE, TILE), TILE)
        x = XV[r, :].astype(F32)
        r1 = rsq(x)
        nx = x * r1
        g = GN[r, :]
        SMALL[0:1, :] += jnp.sum(g * nx, axis=0, keepdims=True)
        e = g * gain(gain1)
        XV[r, :] = (HV[r, :] + r1 * (e - nx * jnp.mean(e * nx, axis=-1, keepdims=True))).astype(BF)


    def attn_back_group(i):
        slot = lax.rem(i, 2)
        m = back_group(i)
        done(load_attn(i))
        pl.when(i + 1 < nmp)(lambda: go(load_attn(i + 1)))
        toeplitz(OFFV.at[m], ST)
        D[...] = jnp.zeros_like(D)

        DO[:, :part] = dot(N2[...], BV[slot, :, 3 * part :]).astype(BF)

        def join(p):
            r = tile_rows(p, seq)
            GN[r, :] += dot(GQKV[r, :wide], BV[slot, :, :wide], 1, 1)

            @pl.when(i == nmp - 1)
            def _():
                loop(0, seq // TILE, functools.partial(last, p))
                si.start(p)

        def pair(p):
            pl.when(p > 0)(lambda: join(p - 1))
            base = pl.multiple_of(p * seq, seq)
            off = jnp.where(lens[h.mp * share + p] < seq, -1e30, 0.0).astype(F32)
            run("back", i * share + p, range(1))
            for head in range(heads_mp):
                attend_back(QV.at[slot], ST, DO, LV.at[slot], GQKV, D, head, part, dh, seq, off, base)

        loop(0, share, pair)
        PA.before_group(m, i)
        pl.when((m % 2 != h.c) & (i < 2))(lambda: PI.sib_sent(False))

        PA.put(m, slice(0, 3 * part), dot(N2T[...], GQKV[:, : 3 * part]).astype(BF))
        PA.put(m, slice(3 * part, hid), dot(DYT[...], OV[slot]).astype(BF))
        PA.after_group(m)
        join(share - 1)
        sums = []
        for head in range(heads_mp):
            strip = jnp.concatenate([D[head], jnp.zeros((128, 128), F32)], 1)
            span = strip.shape[1]
            half = 64
            while half:
                strip = strip[:half] + pltpu.roll(strip[half:], span - half, 1)
                half //= 2
            sums.append(strip)
        sums = jnp.concatenate(sums + [jnp.zeros((8 - heads_mp, span), F32)], 0)
        at = pl.ds(pl.multiple_of(m * 128, 128), 128)
        SMALL[8:16, at] = dot(sums, onehot[...], 1, 1, HIGHEST)

    loop(0, nmp, attn_back_group)
    run("end", 0)

    small = [
        remote(SMALL, SR.at[i], ssmall.at[i], rsmall.at[i], who)
        for i, who in enumerate((h.at(c=1 - h.c), h.at(x=1 - h.x), h.at(y=1 - h.y)))
    ]

    def small_step(i):
        small[i].wait()
        SMALL[...] += SR[i]

    small[0].start()
    run("end", 1)
    small_step(0)
    small[1].start()
    run("end", 2)
    small_step(1)
    small[2].start()
    run("end", 3)
    small_step(2)
    SZ[h.z] = SMALL[...]

    def small_z(k, mine):
        z = h.zi(k)
        b = h.z if mine else z
        return remote(SZ.at[b], SZ.at[b], ssmall.at[3 + z], rsmall.at[3 + b], h.at(z=z))

    loop(1, nz, lambda k: small_z(k, True).start())
    run("end", 4)
    loop(1, nz, lambda k: small_z(k, False).wait_recv())
    SMALL[...] = lax.fori_loop(1, nz, lambda z, acc: acc + SZ[z], SZ[0])
    run("end", 5)
    for T in (PA, PI, PO):
        T.result()
        T.sent()
    PA.sib_sent(True)
    PO.sib_sent(False)
    loop(1, nz, lambda k: small_z(k, True).wait_send())
    if A_BY_HOPS:
        A.hops_sent()
    else:
        A.others(lambda z: A.z(z).wait_send())
    for T in (B, C):
        T.others(lambda z: T.z(z).wait_send())
    for T in (A, B, C):
        T.sent()
    for k in range(1, nmp):
        offs(k).wait_send()
    sx.sent()
    sd.sent()
    sl.come()
    sl.sent()
    si.come()
    si.sent()


def layer(tok, cot, ws, table_t, onehot, gain1, gain2, lens, ndp, nmp, fine):
    pairs, positions, width = tok.shape
    rows, part = ws[0].shape
    hid = ws[4].shape[1]
    heads_mp = table_t.shape[0]
    seq = positions * nmp
    share = pairs // nmp
    n = share * seq
    nz = ndp // fine // 2
    any_ = pl.BlockSpec(memory_space=pl.ANY)
    vm = pl.BlockSpec(memory_space=pltpu.VMEM)
    dma = pltpu.SemaphoreType.DMA
    sds = jax.ShapeDtypeStruct
    bf = lambda *s: pltpu.VMEM(s, BF)
    fl = lambda *s: pltpu.VMEM(s, F32)
    act = sds((pairs, positions, width), BF)
    return pl.pallas_call(
        functools.partial(layer_kernel, (ndp, nmp, fine, seq, heads_mp)),
        out_shape=(act, act)
        + (
            sds((3, rows, hid), F32),
            sds((16, width), F32),
            sds((3, nmp // 2, 2, width, hid), BF),
            sds((nmp, n, 3 * part), BF),
            sds((nmp, n, part), BF),
            sds((nmp, 8, n), F32),
        ),
        in_specs=[any_, any_] + [vm] * 10 + [pl.BlockSpec(memory_space=pltpu.SMEM)],
        out_specs=(any_, any_) + (vm,) * 2 + (any_,) * 4,
        scratch_shapes=[
            bf(3, rows, hid),
            fl(nmp, 8, 2 * seq),
            bf(n, width),
            bf(n, width),
            bf(n, width),
            bf(width, n),
            bf(width, n),
            bf(n, hid),
            bf(n, hid),
            fl(n, width),
            fl(n, width),
            fl(n, width),
            bf(2, width, hid),
            bf(2, width, hid),
            bf(2, n, 3 * part),
            bf(2, n, part),
            fl(2, 8, n),
            fl(heads_mp, 128, 2 * seq - 128),
            fl(heads_mp, 128, 2 * seq - 128),
            bf(2, 2, width, hid),
            bf(2, width, hid),
            bf(3, 2, width, hid),
            bf(3, 2, nz, rows, hid),
            bf(3, 2, nz, rows, hid),
            bf(3, rows, hid),
            fl(3, 16, width),
            fl(nz, 16, width),
            dma((3, 8, nz)),
            dma((3, 8, nz)),
        ]
        + [dma((2, nmp, share))] * 4
        + [dma((2, nmp)), dma((3, 2)), dma((2, 2)), dma((3, 2)), dma((3 + nz,)), dma((3 + nz,)), dma((3,))]
        + [dma((3, 2))] * 2
        + [dma((3, 2, nz))] * 4
        + [dma((3, 1))] * 2,
        compiler_params=pltpu.CompilerParams(collective_id=0, has_side_effects=True, vmem_limit_bytes=63 * MIB),
    )(tok, cot, *ws, table_t, onehot, gain1, gain2, lens)


def finish_kernel(heads_mp, L, I, RES, SMALL, L2, I2, GQ, GK, GV, GO, GI, GF, G1, G2, GB, buf, sem):
    come = [pltpu.make_async_copy(a, buf.at[i], sem.at[0, i]) for i, a in enumerate((L, I))]
    go = [pltpu.make_async_copy(buf.at[i], a, sem.at[1, i]) for i, a in enumerate((L2, I2))]
    for cp in come:
        cp.start()
    for before, after in zip(come, go):
        before.wait()
        after.start()
    part = GQ.shape[1]
    GQ[...] = RES[0, :, :part]
    GK[...] = RES[0, :, part : 2 * part]
    GV[...] = RES[0, :, 2 * part : 3 * part]
    GO[...] = RES[0, :, 3 * part :].T
    GI[...] = RES[1]
    GF[...] = RES[2]
    G1[...] = SMALL[0, :]
    G2[...] = SMALL[1, :]
    at = pl.ds(pl.multiple_of(lax.axis_index("mp") * 128, 128), 128)
    GB[...] = SMALL[8:16, at][:heads_mp, : GB.shape[1]]
    for cp in go:
        cp.wait()


def finish(L, I, RES, SMALL, part, heads_mp, buckets):
    _, rows, hid = RES.shape
    width = SMALL.shape[1]
    any_ = pl.BlockSpec(memory_space=pl.ANY)
    vm = pl.BlockSpec(memory_space=pltpu.VMEM)
    sds = jax.ShapeDtypeStruct
    f32 = [(rows, part)] * 3 + [(part, rows), (rows, hid), (rows, hid), (width,), (width,), (heads_mp, buckets)]
    return pl.pallas_call(
        functools.partial(finish_kernel, heads_mp),
        out_shape=(sds(L.shape, BF), sds(I.shape, BF)) + tuple(sds(s, F32) for s in f32),
        in_specs=[any_, any_, vm, vm],
        out_specs=(any_, any_) + (vm,) * len(f32),
        scratch_shapes=[pltpu.VMEM((2,) + L.shape, BF), pltpu.SemaphoreType.DMA((2, 2))],
    )(L, I, RES, SMALL)


def body(tokens, cotangent, lengths, gain_attn, gain_ff, bias_table, w_query, w_key, w_value, w_out_attn, w_in_ff, w_out_ff):
    ndp, nmp = lax.axis_size("dp"), lax.axis_size("mp")
    seq = tokens.shape[1] * nmp
    buckets, heads_mp = bias_table.shape
    fine = 16 // math.gcd(w_query.shape[0], 16)
    groups = [list(range(g, g + fine)) for g in range(0, ndp, fine)]

    def join(a, dim):
        return a if fine == 1 else lax.all_gather(a, "dp", axis=dim, tiled=True, axis_index_groups=groups)

    def split(a, dim):
        if fine == 1:
            return a
        return lax.psum_scatter(a, "dp", scatter_dimension=dim, tiled=True, axis_index_groups=groups)

    dims = (0, 0, 0, 1, 0, 0)
    ws = tuple(join(w, d) for w, d in zip((w_query, w_key, w_value, w_out_attn, w_in_ff, w_out_ff.T), dims))
    place = np.arange(2 * seq)
    place = np.where(place < 2 * seq - 128, seq - 128 - place, seq - 128 + 2 * seq - place)
    onehot = (bucket_of(place, buckets)[None] == np.arange(128)[:, None]).astype(np.float32)
    out, ing, res, small = layer(
        tokens, cotangent, ws, bias_table.T, onehot, gain_attn, gain_ff, lengths, ndp, nmp, fine
    )[:4]
    if fine > 1:
        small = lax.psum(small, "dp", axis_index_groups=groups)
    out, ing, *grads, g1, g2, gb = finish(out, ing, res, small, w_query.shape[1], heads_mp, buckets)
    gq, gk, gv, go, gi, gf = (split(g, d) for g, d in zip(grads, dims))
    return out, ing, g1, g2, gb.T, gq, gk, gv, go, gi, gf.T


def solution(mesh):
    act = P("dp", "mp", None)
    rows, cols = P("dp", "mp"), P("mp", "dp")
    return jax.shard_map(
        body,
        mesh=mesh,
        in_specs=(act, act, P("dp"), P(), P(), P(None, "mp"), rows, rows, rows, cols, rows, cols),
        out_specs=(act, act, P(), P(), P(None, "mp"), rows, rows, rows, cols, rows, cols),
        check_vma=False,
    )
```

```python
import functools
import math

import jax
import jax.numpy as jnp
import numpy as np
from jax import lax
from jax.experimental import pallas as pl
from jax.experimental.pallas import tpu as pltpu
from jax.sharding import PartitionSpec as P

BF = jnp.bfloat16
F32 = jnp.float32
MESH = pl.DeviceIdType.MESH
EPS = 1e-06
FAR = 128
HIGHEST = lax.Precision.HIGHEST
MIB = 2**20


def bucket_of(offset, count):
    half = count // 2
    upper = (offset > 0).astype(np.int64) * half
    distance = np.abs(offset)
    exact = half // 2
    scaled = np.log(np.maximum(distance, 1) / exact) / np.log(FAR / exact) * (half - exact)
    larger = np.minimum(exact + scaled.astype(np.int64), half - 1)
    return (upper + np.where(distance < exact, distance, larger)).astype(np.int32)

PLAN = {
    ("start", 0): ("C.Y0",),
    ("start", 1): ("A.Xs", "B.Zs", "B.Y0",),
    ("start", 2): ("B.X0", "C.Zs",),
    ("start", 3): ("A.DX",),
    ("attend", 0): ("A.xd",),
    ("attend", 1): ("dy", "B.zy",),
    ("attend", 2): ("B.plane2",),
    ("attend", 3): ("A.ds",),
    ("attend", 4): ("C.zy",),
    ("attend", 6): ("C.Xs",),
    ("attend", 7): ("B.ys",),
    ("between", 0): ("B.z2y", "C.ys",),
    ("ff", 4): ("C.DX", "B.ds",),
    ("ff", 5): ("C.xd",),
    ("ff", 10): ("C.ds",),
    ("ff", 11): ("PO.sw0",),
    ("ff", 19): ("PO.sw1",),
    ("ff", 20): ("PO.yw0",),
    ("between", 3): ("PI.xs0", "PO.st0",),
    ("back", 0): ("PO.yw1", "PI.xs1",),
    ("back", 1): ("PO.st1", "PO.yt0",),
    ("back", 2): ("PO.yt1",),
    ("back", 3): ("PO.zt0", "PI.xw0",),
    ("back", 4): ("PI.xw1", "PA.st0", "lay",),
    ("back", 5): ("PI.xy0", "PO.zw1", "PA.st1",),
    ("back", 6): ("PA.yt0",),
    ("back", 7): ("PA.sw0", "PI.xy1", "PA.yt1", "PI.zo0",),
    ("end", 0): ("PO.zw0",),
    ("end", 1): ("PO.zt1",),
    ("end", 2): ("PI.zo1",),
    ("end", 3): ("PA.yw0", "PA.zt1",),
    ("end", 5): ("PA.zt0", "PA.zw0", "PA.sw1", "PA.yw1", "PA.zw1",),
}
MODES = {"A": "half", "B": "plane", "C": "half"}
X_FIRST = {"PA": False, "PI": True, "PO": False}
A_BY_HOPS = True


class Place:
    def __init__(self, ndp, nmp, fine, rows):
        self.dp, self.mp = lax.axis_index("dp"), lax.axis_index("mp")
        self.x, self.c = self.mp // 2, self.mp % 2
        self.fine = fine
        self.z, self.y = self.dp // fine // 2, self.dp // fine % 2
        self.nz = ndp // fine // 2
        self.nmp, self.rows = nmp, rows

    def at(self, x=None, c=None, z=None, y=None):
        x = self.x if x is None else x
        c = self.c if c is None else c
        z = self.z if z is None else z
        y = self.y if y is None else y
        return ((z * 2 + y) * self.fine + self.dp % self.fine, x * 2 + c)

    def zi(self, k):
        return lax.rem(self.z + k, self.nz)

    def block(self, z, y, count=1):
        return pl.ds(pl.multiple_of((z * 2 + y) * self.rows, self.rows), count * self.rows)

    def greet(self):
        bar = pltpu.get_barrier_semaphore()

        def tell(who):
            pl.semaphore_signal(bar, inc=1, device_id=who, device_id_type=MESH)

        tell(self.at(c=1 - self.c))
        tell(self.at(x=1 - self.x))
        tell(self.at(x=1 - self.x, c=1 - self.c))
        tell(self.at(y=1 - self.y))
        loop(1, self.nz, lambda k: tell(self.at(z=self.zi(k))))

    def met(self):
        pl.semaphore_wait(pltpu.get_barrier_semaphore(), 4 + self.nz - 1)


def remote(src, dst, ssem, rsem, who):
    return pltpu.make_async_remote_copy(
        src_ref=src, dst_ref=dst, send_sem=ssem, recv_sem=rsem, device_id=who, device_id_type=MESH
    )


def loop(lo, hi, fn):
    def step(k, carry):
        fn(k)
        return carry

    lax.fori_loop(lo, hi, step, 0)


class Gather:
    def __init__(self, here, pack, mode, W, ssem, rsem):
        self.h, self.nz, self.mode = here, here.nz, mode
        self.W = W.at[pack]
        self.ss, self.rs = ssem.at[pack], rsem.at[pack]

    def at(self, x, c, z, y):
        return self.W.at[x, c, self.h.block(z, y)]

    def send(self, src, kind, idx, who, skind=None, sidx=0):
        skind = kind if skind is None else skind
        return remote(src, src, self.ss.at[skind, sidx], self.rs.at[kind, idx], who)

    def wait_sent(self, kind, blocks):
        src = self.W.at[0, 0, self.h.block(0, 0, blocks)]
        remote(src, src, self.ss.at[kind, 0], self.rs.at[kind, 0], self.h.at(c=1 - self.h.c)).wait_send()

    def hop(self, b, step):
        h = self.h
        return self.send(self.at(h.x, h.c, b, h.y), 0, b, h.at(z=h.z + step), 0 if step > 0 else 7, b)

    def z(self, z, mine=True):
        h = self.h
        b = h.z if mine else z
        return self.send(self.at(h.x, h.c, b, h.y), 0, b, h.at(z=z))

    def y(self, z, mine=True):
        h = self.h
        return self.send(self.at(h.x, h.c, z, h.y if mine else 1 - h.y), 1, z, h.at(y=1 - h.y))

    def x(self, z, mine=True):
        h = self.h
        return self.send(self.at(h.x if mine else 1 - h.x, h.c, z, h.y), 2, z, h.at(x=1 - h.x))

    def diag_by_x(self, z):
        h = self.h
        return self.send(self.at(h.x, h.c, z, 1 - h.y), 3, z, h.at(x=1 - h.x))

    def diag_by_y(self, z):
        h = self.h
        return self.send(self.at(1 - h.x, h.c, z, h.y), 3, z, h.at(y=1 - h.y))

    def diag(self, z):
        h = self.h
        return self.send(self.at(1 - h.x, h.c, z, 1 - h.y), 3, z, h.at(x=1 - h.x))

    def z2(self, z, mine=True):
        h = self.h
        b = h.z if mine else z
        return self.send(self.at(1 - h.x, h.c, b, h.y), 4, b, h.at(z=z))

    def sib(self, half, z, mine=True):
        h = self.h
        block = self.W.at[h.x if half == 0 else 1 - h.x, h.c if mine else 1 - h.c, h.block(z, 0, 2)]
        return self.send(block, 5 + half, z, h.at(c=1 - h.c))

    def sib_wait(self, half):
        self.all(lambda z: self.sib(half, z, False).wait_recv())

    def all(self, fn):
        loop(0, self.nz, lambda k: fn(self.h.zi(k)))

    def others(self, fn):
        loop(1, self.nz, lambda k: fn(self.h.zi(k)))

    def by_x(self, z, fn):
        if self.mode == "half":
            pl.when(z % 2 == 0)(fn)

    def by_y(self, z, fn):
        if self.mode == "half":
            pl.when(z % 2 == 1)(fn)
        else:
            fn()

    def hops(self):
        h = self.h
        for step in (1, -1):
            pl.when((h.z + step >= 0) & (h.z + step < self.nz))(lambda: self.hop(h.z, step).start())
        self.y(h.z).start()

    def hops_on(self):
        h = self.h

        def on(d):
            for step in (1, -1):
                b = h.z - step * d

                @pl.when((b >= 0) & (b < self.nz))
                def _():
                    self.z(b, False).wait_recv()
                    pl.when((h.z + step >= 0) & (h.z + step < self.nz))(lambda: self.hop(b, step).start())
                    self.y(b).start()

        loop(1, self.nz, on)

    def hops_sent(self):
        h = self.h

        def on(b):
            pl.when((b <= h.z) & (h.z + 1 < self.nz))(lambda: self.hop(b, 1).wait_send())
            pl.when((b >= h.z) & (h.z >= 1))(lambda: self.hop(b, -1).wait_send())

        loop(0, self.nz, on)

    def steps(self):
        h = self.h

        def zy(z):
            self.z(z, False).wait_recv()
            self.y(z).start()

        def ys(z):
            self.y(z, False).wait_recv()
            self.sib(0, z).start()

        def z2y(z):
            self.z2(z, False).wait_recv()
            self.diag_by_y(z).start()

        def xd(z):
            self.x(z, False).wait_recv()
            self.by_y(z, lambda: self.diag_by_y(z).start())

        def ds(z):
            self.diag(z).wait_recv()
            self.sib(1, z).start()

        def plane2():
            self.x(h.z, False).wait_recv()
            self.others(lambda z: self.z2(z).start())
            self.diag_by_y(h.z).start()

        return {
            "Zs": lambda: self.others(lambda z: self.z(z).start()),
            "Y0": lambda: self.y(h.z).start(),
            "zy": lambda: self.others(zy),
            "ys": lambda: self.all(ys),
            "X0": lambda: self.x(h.z).start(),
            "plane2": plane2,
            "z2y": lambda: self.others(z2y),
            "Xs": lambda: self.all(lambda z: self.x(z).start()),
            "DX": lambda: self.all(lambda z: self.by_x(z, lambda: self.diag_by_x(z).start())),
            "xd": lambda: self.all(xd),
            "ds": lambda: self.all(ds),
        }

    def sent(self, by_hops=False):
        nz = self.nz
        if by_hops:
            self.hops_sent()
        else:
            self.wait_sent(0, nz - 1)
        self.wait_sent(1, nz)
        self.wait_sent(2, 1 if self.mode == "plane" else nz)
        self.wait_sent(3, nz)
        if self.mode == "plane":
            self.wait_sent(4, nz - 1)
        self.wait_sent(5, 2 * nz)
        self.wait_sent(6, 2 * nz)


class Swap:
    def __init__(self, here, whole, flat, sems, back):
        self.h, self.whole, self.flat, self.sems, self.back = here, whole, flat, sems, back
        self.positions = whole.shape[1]
        self.share = whole.shape[0] // here.nmp

    def views(self, s, outer, inner):
        at = pl.multiple_of((s * self.h.nmp + inner) * self.positions, self.positions)
        return self.whole.at[outer * self.share + s], self.flat.at[pl.ds(at, self.positions)]

    def copy(self, s, k, mine):
        h = self.h
        other = lax.rem(h.mp + (k if mine else h.nmp - k), h.nmp)
        sender, receiver = (h.mp, other) if mine else (other, h.mp)
        if self.back:
            dst, src = self.views(s, sender, receiver)
        else:
            src, dst = self.views(s, receiver, sender)
        if not mine:
            src = dst
        return remote(src, dst, self.sems.at[0, k, s], self.sems.at[1, k, s], (h.dp, other))

    def local(self, s):
        whole, flat = self.views(s, self.h.mp, self.h.mp)
        src, dst = (flat, whole) if self.back else (whole, flat)
        return pltpu.make_async_copy(src, dst, self.sems.at[0, 0, s])

    def start(self, s):
        for k in range(1, self.h.nmp):
            self.copy(s, k, True).start()
        self.local(s).start()

    def start_all(self):
        for s in range(self.share):
            self.start(s)

    def come(self):
        for s in range(self.share):
            for k in range(1, self.h.nmp):
                self.copy(s, k, False).wait_recv()
            self.local(s).wait()

    def sent(self):
        for s in range(self.share):
            for k in range(1, self.h.nmp):
                self.copy(s, k, True).wait_send()


class Scatter:
    def __init__(self, here, pack, x_first, mine, bufs, RES, sems):
        self.h, self.nz, self.x_first = here, here.nz, x_first
        self.MINE, self.SENT = mine
        self.R0, self.R1, self.R2, self.R3 = [b.at[pack] for b in bufs]
        self.RES = RES.at[pack]
        self.sems = [s.at[pack] for s in sems]
        self.block = here.block

    def half(self, own):
        return self.h.x if own else 1 - self.h.x

    def put(self, m, columns, value):
        @pl.when(m % 2 == self.h.c)
        def _():
            self.MINE[m // 2, :, columns] = value

        @pl.when(m % 2 != self.h.c)
        def _():
            self.SENT[:, columns] = value

    def two(self, x, r):
        return self.MINE[x, r].astype(F32) + self.R0[x, r].astype(F32)

    def sib(self, x):
        return remote(self.SENT, self.R0.at[x], self.sems[0].at[x], self.sems[1].at[x], self.h.at(c=1 - self.h.c))

    def ysend(self, x, z):
        h = self.h
        src = self.MINE.at[x, self.block(z, 1 - h.y)]
        return remote(src, self.R1.at[x, z], self.sems[2].at[x, 0], self.sems[3].at[x, z], h.at(y=1 - h.y))

    def zsend(self, x, z):
        h = self.h
        return remote(self.R1.at[x, z], self.R2.at[x, h.z], self.sems[4].at[x, 0], self.sems[5].at[x, h.z], h.at(z=z))

    def zcome(self, x, z):
        h = self.h
        return remote(self.R2.at[x, z], self.R2.at[x, z], self.sems[4].at[x, 0], self.sems[5].at[x, z], h.at(z=z))

    def xsend(self):
        h = self.h
        return remote(self.R1.at[1 - h.x, h.z], self.R3, self.sems[6].at[0], self.sems[7].at[0], h.at(x=1 - h.x))

    def xall(self, z, y_is_own, mine=True):
        h = self.h
        i = 2 if y_is_own else 4
        to = h.x if mine else 1 - h.x
        src = self.MINE.at[1 - h.x, self.block(z, h.y if y_is_own else 1 - h.y)]
        dst = (self.R1 if y_is_own else self.R2).at[to, z]
        return remote(src, dst, self.sems[i].at[1 - h.x, 0], self.sems[i + 1].at[to, z], h.at(x=1 - h.x))

    def after_group(self, m):
        pl.when(m % 2 != self.h.c)(lambda: self.sib(m // 2).start())

    def before_group(self, m, i):
        pl.when((m % 2 != self.h.c) & (i >= 2))(lambda: self.sib(1 - m // 2).wait_send())

    def sib_sent(self, own):
        self.sib(self.half(own)).wait_send()

    def each(self, fn):
        loop(1, self.nz + 1, lambda k: fn(self.h.zi(k)))

    def others(self, fn):
        loop(1, self.nz, lambda k: fn(self.h.zi(k)))

    def after_sib(self, own):
        x = self.half(own)
        self.sib(x).wait_recv()

        def on(z):
            r = self.block(z, 1 - self.h.y)
            self.MINE[x, r] = self.two(x, r).astype(BF)
            self.ysend(x, z).start()

        self.each(on)

    def after_y(self, own):
        x = self.half(own)

        def on(z):
            self.ysend(x, z).wait_recv()
            total = self.two(x, self.block(z, self.h.y)) + self.R1[x, z].astype(F32)
            self.R1[x, z] = total.astype(BF)
            pl.when(z != self.h.z)(lambda: self.zsend(x, z).start())

        self.each(on)

    def after_z(self, own):
        h, x = self.h, self.half(own)
        self.others(lambda z: self.zcome(x, z).wait_recv())

        def add(k, acc):
            return acc + self.R2[x, h.zi(k)].astype(F32)

        total = lax.fori_loop(1, self.nz, add, self.R1[x, h.z].astype(F32))
        if own:
            self.RES[...] = total
        else:
            self.R1[x, h.z] = total.astype(BF)
            self.xsend().start()

    def to_x(self):
        x = self.half(False)
        self.sib(x).wait_recv()

        def on(z):
            for y_is_own in (True, False):
                r = self.block(z, self.h.y if y_is_own else 1 - self.h.y)
                self.MINE[x, r] = self.two(x, r).astype(BF)
                self.xall(z, y_is_own).start()

        self.each(on)

    def after_x(self):
        x = self.half(True)
        self.sib(x).wait_recv()

        def on(z):
            r = self.block(z, 1 - self.h.y)
            self.xall(z, False, False).wait_recv()
            self.MINE[x, r] = (self.two(x, r) + self.R2[1 - x, z].astype(F32)).astype(BF)
            self.ysend(x, z).start()

        self.each(on)

    def after_x_and_y(self):
        x = self.half(True)

        def on(z):
            self.xall(z, True, False).wait_recv()
            self.ysend(x, z).wait_recv()
            total = self.two(x, self.block(z, self.h.y)) + self.R1[x, z].astype(F32) + self.R1[1 - x, z].astype(F32)
            self.R1[x, z] = total.astype(BF)
            pl.when(z != self.h.z)(lambda: self.zsend(x, z).start())

        self.each(on)

    def steps(self):
        out = {}
        if self.x_first:
            fns = {"xs": self.to_x, "xw": self.after_x, "xy": self.after_x_and_y, "zo": lambda: self.after_z(True)}
        else:
            fns = {}
            for tag, own in (("w", True), ("t", False)):
                fns["s" + tag] = functools.partial(self.after_sib, own)
                fns["y" + tag] = functools.partial(self.after_y, own)
                fns["z" + tag] = functools.partial(self.after_z, own)
        for name, fn in fns.items():
            for c in (0, 1):
                out[name + str(c)] = functools.partial(self.on_core, c, fn)
        return out

    def on_core(self, c, fn):
        pl.when(self.h.c == c)(fn)

    def result(self):
        if not self.x_first:
            self.xsend().wait_recv()
            self.RES[...] += self.R3[...].astype(F32)

    def wait_sent(self, i, x, blocks):
        src = self.R1.at[x, pl.ds(0, blocks)]
        remote(src, src, self.sems[i].at[x, 0], self.sems[i + 1].at[x, 0], self.h.at(c=1 - self.h.c)).wait_send()

    def sent(self):
        own, other = self.half(True), self.half(False)
        self.wait_sent(2, own, self.nz)
        self.wait_sent(4, own, self.nz - 1)
        self.wait_sent(2, other, self.nz)
        if self.x_first:
            self.wait_sent(4, other, self.nz)
        else:
            self.wait_sent(4, other, self.nz - 1)
            self.xsend().wait_send()


def dot(a, b, ca=1, cb=0, precision=None):
    return lax.dot_general(a, b, (((ca,), (cb,)), ((), ())), preferred_element_type=F32, precision=precision)


def tile_rows(i, size):
    return pl.ds(pl.multiple_of(i * size, size), size)


TILE = 256


def rsq(v):
    return lax.rsqrt(jnp.mean(v * v, axis=-1, keepdims=True) + EPS)


def toeplitz(offsets, ST):
    heads, span = ST.shape[0], ST.shape[2]
    for h in range(heads):
        row = jnp.broadcast_to(offsets[h : h + 1, :], (128, offsets.shape[1]))
        ST[h] = pltpu.roll(row, 0, 1, stride=1, stride_axis=0)[:, :span]


def biased(s, ST, h, dead):
    blocks = s.shape[0] // 128
    pieces = []
    for j in range(blocks):
        c0 = 128 * (blocks - 1 - j)
        piece = s[128 * j : 128 * (j + 1)] + ST[h, :, c0 : c0 + s.shape[1]]
        pieces.append(piece if j < blocks // 2 else piece + dead)
    return jnp.concatenate(pieces, 0)


def attend(QV, ST, h, part, dh, seq, dead, base, OV, LV):
    q0, k0, v0 = h * dh, part + h * dh, 2 * part + h * dh
    rows = pl.ds(base, seq)
    queries, keys, values = QV[rows, q0 : q0 + dh], QV[rows, k0 : k0 + dh], QV[rows, v0 : v0 + dh]
    s = biased(dot(keys, queries, 1, 1), ST, h, dead)
    top = jnp.max(s, axis=0, keepdims=True)
    e = jnp.exp(s - top)
    total = jnp.sum(e, axis=0, keepdims=True)
    prob = (e * (1.0 / total)).astype(BF)
    OV[rows, h * dh : (h + 1) * dh] = dot(prob, values, 0, 0).astype(BF)
    LV[h : h + 1, rows] = top + jnp.log(total)


GELU_C = float(np.sqrt(2.0 / np.pi))


def gelu_both(a):
    a2 = a * a
    t = jnp.tanh(a * (GELU_C + (GELU_C * 0.044715) * a2))
    half = 0.5 + 0.5 * t
    slope = half + (0.5 * a) * (1.0 - t * t) * (GELU_C + (3.0 * GELU_C * 0.044715) * a2)
    return a * half, slope


def attend_back(QV, ST, DO, LV, DL, GQKV, D, h, part, dh, seq, dead, base):
    rows = pl.ds(base, seq)
    q0, k0, v0 = h * dh, part + h * dh, 2 * part + h * dh
    queries, keys, values = QV[rows, q0 : q0 + dh], QV[rows, k0 : k0 + dh], QV[rows, v0 : v0 + dh]
    d_o = DO[rows, h * dh : (h + 1) * dh]
    s = biased(dot(keys, queries, 1, 1), ST, h, dead)
    prob = jnp.exp(s - LV[h : h + 1, rows])
    dprob = dot(values, d_o, 1, 1)
    gs = (prob * (dprob - DL[h : h + 1, rows])).astype(BF)
    GQKV[rows, v0 : v0 + dh] = dot(prob.astype(BF), d_o).astype(BF)
    GQKV[rows, k0 : k0 + dh] = dot(gs, queries).astype(BF)
    GQKV[rows, q0 : q0 + dh] = dot(keys.T, gs).astype(BF).T
    blocks = seq // 128
    for d in range(1 - blocks, blocks):
        c0 = 128 * (blocks - 1 - d)
        acc = D[h, :, c0 : c0 + 128]
        for j in range(max(0, d), min(blocks, blocks + d)):
            acc += gs[128 * j : 128 * (j + 1), 128 * (j - d) : 128 * (j - d + 1)].astype(F32)
        D[h, :, c0 : c0 + 128] = acc


def layer_kernel(cfg, tok, cot, wq, wk, wv, wo, wi, wf_t, table_t, onehot, gain1, gain2, lens, *refs):
    ndp, nmp, fine, seq, heads_mp = cfg
    L, I, RES, SMALL, W, QKV, O, LSE = refs[:8]
    OWN, OFFV, XV, DYV, N2, N2T, DYT, U, GA, HV, FF, GN, BV, CV, QV, OV, LV, DL, ST, D = refs[8:28]
    FFMINE, SENT = refs[28:30]
    bufs, SR, SZ = refs[30:34], refs[34], refs[35]
    ssem, rsem, xsem, dysem, lsem, isem, bsem, osem, wsem, qsem, ssmall, rsmall, csem = refs[36:49]
    sems = refs[49:57]
    rows, part = wq.shape
    h = Place(ndp, nmp, fine, rows)
    h.greet()
    n, width = XV.shape
    hid = U.shape[1]
    dh = part // heads_mp
    share = n // seq
    tiles = n // TILE
    nz = h.nz

    def gain(ref):
        return ref[...].reshape(1, width)

    def go(copies):
        for cp in copies:
            cp.start()

    def done(copies):
        for cp in copies:
            cp.wait()

    def run(section, at, static=None, period=1):
        for (name, slot), steps in PLAN.items():
            if name == section and (slot == at if static is None else slot % period in static):

                def fn(steps=steps):
                    for step in steps:
                        ACTIONS[step]()

                if static is None:
                    fn()
                else:
                    pl.when(at == slot)(fn)

    OWN[0, :, :part] = wq[...].astype(BF)
    OWN[0, :, part : 2 * part] = wk[...].astype(BF)
    OWN[0, :, 2 * part : 3 * part] = wv[...].astype(BF)
    OWN[0, :, 3 * part :] = wo[...].T.astype(BF)
    OWN[1] = wi[...].astype(BF)
    OWN[2] = wf_t[...].astype(BF)
    own = [pltpu.make_async_copy(OWN.at[p], W.at[p, h.x, h.c, h.block(h.z, h.y)], csem.at[p]) for p in range(3)]
    go(own)
    OFFV[h.mp] = jnp.zeros_like(OFFV[0])
    OFFV[h.mp, :heads_mp] = dot(table_t[...], onehot[: table_t.shape[1], :], 1, 0, HIGHEST)

    def offs(k, mine=True):
        other = lax.rem(h.mp + (k if mine else nmp - k), nmp)
        at = OFFV.at[h.mp if mine else other]
        return remote(at, at, bsem.at[0, k], bsem.at[1, k], (h.dp, other))

    A, B, C = [Gather(h, p, MODES[name], W, ssem, rsem) for p, name in enumerate("ABC")]
    mines = (CV, SENT.at[0]), (FFMINE.at[0], SENT.at[0]), (FFMINE.at[1], SENT.at[1])
    PA, PI, PO = [
        Scatter(h, p, X_FIRST[name], mines[p], bufs, RES, sems) for p, name in enumerate(("PA", "PI", "PO"))
    ]
    sx = Swap(h, tok, XV, xsem, False)
    sd = Swap(h, cot, DYV, dysem, False)
    sl = Swap(h, L, DYV, lsem, True)
    si = Swap(h, I, XV, isem, True)

    ACTIONS = {"dy": sd.start_all, "lay": sl.start_all}
    for name, part_of in (("A", A), ("B", B), ("C", C), ("PA", PA), ("PI", PI), ("PO", PO)):
        ACTIONS.update({name + "." + step: fn for step, fn in part_of.steps().items()})

    done(own)
    h.met()
    if A_BY_HOPS:
        A.hops()
    else:
        ACTIONS["A.Zs"]()
        ACTIONS["A.Y0"]()
    run("first", 0)
    sx.start_all()
    for k in range(1, nmp):
        offs(k).start()
    run("start", 0)
    if A_BY_HOPS:
        A.hops_on()
    else:
        ACTIONS["A.zy"]()
    run("start", 1)
    ACTIONS["A.ys"]()
    run("start", 2)
    sx.come()
    run("start", 3)

    def norm(t):
        r = tile_rows(t, TILE)
        x = XV[r, :].astype(F32)
        N2[r, :] = (x * rsq(x) * gain(gain1)).astype(BF)
        HV[r, :] = x

    loop(0, tiles, norm)
    A.sib_wait(0)

    def group(i):
        return lax.rem(2 * h.x + i, nmp)

    def load(p, i, m, V, sem):
        slot = lax.rem(i, 2)
        return pltpu.make_async_copy(W.at[p, m // 2, m % 2], V.at[slot], sem.at[slot])

    def load_a(i):
        return load(0, i, group(i), BV, wsem.at[0])

    def store(i):
        m, slot = group(i), lax.rem(i, 2)
        return (
            pltpu.make_async_copy(QV.at[slot], QKV.at[m], osem.at[0, slot]),
            pltpu.make_async_copy(OV.at[slot], O.at[m], osem.at[1, slot]),
            pltpu.make_async_copy(LV.at[slot], LSE.at[m], osem.at[2, slot]),
        )

    load_a(0).start()
    for k in range(1, nmp):
        offs(k, False).wait_recv()

    def attn_group(i):
        slot = lax.rem(i, 2)
        m = group(i)

        @pl.when(i == 2)
        def _():
            A.sib_wait(1)
            load_a(2).start()

        toeplitz(OFFV.at[m], ST)
        pl.when(i >= 2)(lambda: done(store(i - 2)))
        load_a(i).wait()
        pl.when((i == 0) | (i == 2))(lambda: load_a(i + 1).start())

        QV[slot] = dot(N2[...], BV[slot, :, : 3 * part]).astype(BF)

        def pair(p):
            base = pl.multiple_of(p * seq, seq)
            off = jnp.where(lens[h.mp * share + p] < seq, -1e30, 0.0).astype(F32)
            run("attend", i * share + p, range(1))
            for head in range(heads_mp):
                attend(QV.at[slot], ST, head, part, dh, seq, off, base, OV.at[slot], LV.at[slot])

        loop(0, share, pair)

        HV[...] += dot(OV[slot], BV[slot, :, 3 * part :], 1, 1)
        go(store(i))

    loop(0, nmp, attn_group)

    run("between", 0)

    def load_ff(i):
        m = group(i)
        return load(1, i, m, BV, wsem.at[0]), load(2, i, m, CV, wsem.at[1])

    sd.come()
    SMALL[...] = jnp.zeros_like(SMALL)

    def prep(t):
        r = tile_rows(t, TILE)
        hidden = HV[r, :]
        n2 = (hidden * rsq(hidden) * gain(gain2)).astype(BF)
        N2[r, :] = n2
        N2T[:, r] = n2.T
        DYT[:, r] = DYV[r, :].T
        FF[r, :] = hidden
        GN[r, :] = jnp.zeros((TILE, width), F32)

    loop(0, tiles, prep)
    run("between", 1)
    B.sib_wait(0)
    C.sib_wait(0)
    go(load_ff(0))

    steps = tiles + 2

    def ff_group(i):
        slot = lax.rem(i, 2)
        m = group(i)
        done(load_ff(i))
        pl.when((i == 0) | (i == 2))(lambda: go(load_ff(i + 1)))

        def rowwise(t):
            run("ff", i * steps + t, range(tiles), steps)
            r = tile_rows(t, TILE)
            b = BV[slot]
            c = CV[slot]
            a = dot(N2[r, :], b)
            gu = dot(DYV[r, :], c)
            u, slope = gelu_both(a)
            u = u.astype(BF)
            ga = (gu * slope).astype(BF)
            U[r, :] = u
            GA[r, :] = ga
            FF[r, :] += dot(u, c, 1, 1)
            GN[r, :] += dot(ga, b, 1, 1)

        loop(0, tiles, rowwise)
        PI.before_group(m, i)
        PO.before_group(m, i)

        run("ff", i * steps + tiles, (tiles,), steps)
        PI.put(m, slice(None), dot(N2T[...], GA[...]).astype(BF))
        run("ff", i * steps + tiles + 1, (tiles + 1,), steps)
        PO.put(m, slice(None), dot(DYT[...], U[...]).astype(BF))
        PI.after_group(m)
        PO.after_group(m)

        @pl.when(i == 1)
        def _():
            run("between", 2)
            B.sib_wait(1)
            C.sib_wait(1)
            go(load_ff(2))

    loop(0, nmp, ff_group)

    def back_group(i):
        return lax.rem(2 * (1 - h.x) + i, nmp)

    def load_attn(i):
        m, slot = back_group(i), lax.rem(i, 2)
        return (
            load(0, i, m, BV, wsem.at[0]),
            pltpu.make_async_copy(QKV.at[m], QV.at[slot], qsem.at[0, slot]),
            pltpu.make_async_copy(O.at[m], OV.at[slot], qsem.at[1, slot]),
            pltpu.make_async_copy(LSE.at[m], LV.at[slot], qsem.at[2, slot]),
        )

    for i in (nmp - 2, nmp - 1):
        done(store(i))
    go(load_attn(0))
    run("between", 3)

    def mid(t):
        r = tile_rows(t, TILE)
        hidden = HV[r, :]
        r2 = rsq(hidden)
        nh = hidden * r2
        g = GN[r, :]
        SMALL[1:2, :] += jnp.sum(g * nh, axis=0, keepdims=True)
        e = g * gain(gain2)
        gh = DYV[r, :].astype(F32) + r2 * (e - nh * jnp.mean(e * nh, axis=-1, keepdims=True))
        DYV[r, :] = FF[r, :].astype(BF)
        HV[r, :] = gh
        low = gh.astype(BF)
        N2[r, :] = low
        DYT[:, r] = low.T
        x = XV[r, :].astype(F32)
        N2T[:, r] = (x * rsq(x) * gain(gain1)).astype(BF).T
        GN[r, :] = jnp.zeros((TILE, width), F32)
        U[r, 3 * part :] = jnp.zeros((TILE, hid - 3 * part), BF)

    loop(0, tiles, mid)

    GQKV, DO = U, GA
    wide = -(-3 * part // 128) * 128

    def last(p, t):
        r = pl.ds(pl.multiple_of(p * seq + t * TILE, TILE), TILE)
        x = XV[r, :].astype(F32)
        r1 = rsq(x)
        nx = x * r1
        g = GN[r, :]
        SMALL[0:1, :] += jnp.sum(g * nx, axis=0, keepdims=True)
        e = g * gain(gain1)
        XV[r, :] = (HV[r, :] + r1 * (e - nx * jnp.mean(e * nx, axis=-1, keepdims=True))).astype(BF)


    head_of = (lax.broadcasted_iota(jnp.int32, (8, part), 1) // dh == lax.broadcasted_iota(jnp.int32, (8, part), 0)).astype(F32)

    def attn_back_group(i):
        slot = lax.rem(i, 2)
        m = back_group(i)
        toeplitz(OFFV.at[m], ST)
        D[...] = jnp.zeros_like(D)
        done(load_attn(i))
        pl.when(i + 1 < nmp)(lambda: go(load_attn(i + 1)))

        d_o = dot(N2[...], BV[slot, :, 3 * part :]).astype(BF)
        DO[:, :part] = d_o
        DL[...] = dot(head_of, OV[slot].astype(F32) * d_o.astype(F32), 1, 1, HIGHEST)

        def join(p):
            r = tile_rows(p, seq)
            GN[r, :] += dot(GQKV[r, :wide], BV[slot, :, :wide], 1, 1)

            @pl.when(i == nmp - 1)
            def _():
                loop(0, seq // TILE, functools.partial(last, p))
                pl.when(p + 1 < share)(lambda: si.start(p))

        def pair(p):
            pl.when(p > 0)(lambda: join(p - 1))
            base = pl.multiple_of(p * seq, seq)
            off = jnp.where(lens[h.mp * share + p] < seq, -1e30, 0.0).astype(F32)
            run("back", i * share + p, range(1))
            for head in range(heads_mp):
                attend_back(QV.at[slot], ST, DO, LV.at[slot], DL, GQKV, D, head, part, dh, seq, off, base)

        loop(0, share, pair)
        PA.before_group(m, i)
        pl.when((m % 2 != h.c) & (i < 2))(lambda: PI.sib_sent(False))

        PA.put(m, slice(0, 3 * part), dot(N2T[...], GQKV[:, : 3 * part]).astype(BF))
        PA.put(m, slice(3 * part, hid), dot(DYT[...], OV[slot]).astype(BF))
        PA.after_group(m)
        join(share - 1)
        sums = []
        for head in range(heads_mp):
            strip = jnp.concatenate([D[head], jnp.zeros((128, 128), F32)], 1)
            span = strip.shape[1]
            half = 64
            while half:
                strip = strip[:half] + pltpu.roll(strip[half:], span - half, 1)
                half //= 2
            sums.append(strip)
        sums = jnp.concatenate(sums + [jnp.zeros((8 - heads_mp, span), F32)], 0)
        at = pl.ds(pl.multiple_of(m * 128, 128), 128)
        SMALL[8:16, at] = dot(sums, onehot[...], 1, 1, HIGHEST)

    loop(0, nmp, attn_back_group)
    run("end", 0)

    small = [
        remote(SMALL, SR.at[i], ssmall.at[i], rsmall.at[i], who)
        for i, who in enumerate((h.at(c=1 - h.c), h.at(x=1 - h.x), h.at(y=1 - h.y), h.at(c=1 - h.c)))
    ]

    def small_z(k, mine):
        z = h.zi(k)
        b = h.z if mine else z
        return remote(SZ.at[b], SZ.at[b], ssmall.at[4 + z], rsmall.at[4 + b], h.at(z=z))

    def small_step(i):
        small[i].wait()
        SMALL[...] += SR[i]

    def on_core_0(fn):
        pl.when(h.c == 0)(fn)

    small[0].start()
    small_step(0)
    on_core_0(lambda: small[1].start())
    si.start(share - 1)
    run("end", 1)

    @on_core_0
    def _():
        small_step(1)
        small[2].start()

    run("end", 2)

    @on_core_0
    def _():
        small_step(2)
        SZ[h.z] = SMALL[...]
        loop(1, nz, lambda k: small_z(k, True).start())

    run("end", 3)

    @on_core_0
    def _():
        loop(1, nz, lambda k: small_z(k, False).wait_recv())
        SMALL[...] = lax.fori_loop(1, nz, lambda z, acc: acc + SZ[z], SZ[0])
        small[3].start()

    run("end", 4)

    @pl.when(h.c == 1)
    def _():
        small[3].wait_recv()
        SMALL[...] = SR[3]

    run("end", 5)
    for T in (PA, PI, PO):
        T.result()
        T.sent()
    PA.sib_sent(True)
    PO.sib_sent(False)

    @on_core_0
    def _():
        loop(1, nz, lambda k: small_z(k, True).wait_send())
        small[3].wait_send()

    A.sent(A_BY_HOPS)
    B.sent()
    C.sent()
    for k in range(1, nmp):
        offs(k).wait_send()
    sx.sent()
    sd.sent()
    sl.come()
    sl.sent()
    si.come()
    si.sent()


def layer(tok, cot, ws, table_t, onehot, gain1, gain2, lens, ndp, nmp, fine):
    pairs, positions, width = tok.shape
    rows, part = ws[0].shape
    hid = ws[4].shape[1]
    heads_mp = table_t.shape[0]
    seq = positions * nmp
    share = pairs // nmp
    n = share * seq
    nz = ndp // fine // 2
    any_ = pl.BlockSpec(memory_space=pl.ANY)
    vm = pl.BlockSpec(memory_space=pltpu.VMEM)
    dma = pltpu.SemaphoreType.DMA
    sds = jax.ShapeDtypeStruct
    bf = lambda *s: pltpu.VMEM(s, BF)
    fl = lambda *s: pltpu.VMEM(s, F32)
    act = sds((pairs, positions, width), BF)
    return pl.pallas_call(
        functools.partial(layer_kernel, (ndp, nmp, fine, seq, heads_mp)),
        out_shape=(act, act)
        + (
            sds((3, rows, hid), F32),
            sds((16, width), F32),
            sds((3, nmp // 2, 2, width, hid), BF),
            sds((nmp, n, 3 * part), BF),
            sds((nmp, n, part), BF),
            sds((nmp, 8, n), F32),
        ),
        in_specs=[any_, any_] + [vm] * 10 + [pl.BlockSpec(memory_space=pltpu.SMEM)],
        out_specs=(any_, any_) + (vm,) * 2 + (any_,) * 4,
        scratch_shapes=[
            bf(3, rows, hid),
            fl(nmp, 8, 2 * seq),
            bf(n, width),
            bf(n, width),
            bf(n, width),
            bf(width, n),
            bf(width, n),
            bf(n, hid),
            bf(n, hid),
            fl(n, width),
            fl(n, width),
            fl(n, width),
            bf(2, width, hid),
            bf(2, width, hid),
            bf(2, n, 3 * part),
            bf(2, n, part),
            fl(2, 8, n),
            fl(8, n),
            fl(heads_mp, 128, 2 * seq - 128),
            fl(heads_mp, 128, 2 * seq - 128),
            bf(2, 2, width, hid),
            bf(2, width, hid),
            bf(3, 2, width, hid),
            bf(3, 2, nz, rows, hid),
            bf(3, 2, nz, rows, hid),
            bf(3, rows, hid),
            fl(4, 16, width),
            fl(nz, 16, width),
            dma((3, 8, nz)),
            dma((3, 8, nz)),
        ]
        + [dma((2, nmp, share))] * 4
        + [dma((2, nmp)), dma((3, 2)), dma((2, 2)), dma((3, 2)), dma((4 + nz,)), dma((4 + nz,)), dma((3,))]
        + [dma((3, 2))] * 2
        + [dma((3, 2, nz))] * 4
        + [dma((3, 1))] * 2,
        compiler_params=pltpu.CompilerParams(collective_id=0, has_side_effects=True, vmem_limit_bytes=63 * MIB),
    )(tok, cot, *ws, table_t, onehot, gain1, gain2, lens)


def finish_kernel(heads_mp, L, I, RES_, SMALL_, L2, I2, GQ, GK, GV, GO, GI, GF, G1, G2, GB, buf, RES, SMALL, sem):
    come = [
        pltpu.make_async_copy(a, b, sem.at[0, i])
        for i, (a, b) in enumerate(((L, buf.at[0]), (I, buf.at[1]), (RES_, RES), (SMALL_, SMALL)))
    ]
    go = [pltpu.make_async_copy(buf.at[i], a, sem.at[1, i]) for i, a in enumerate((L2, I2))]
    for cp in come:
        cp.start()
    for before, after in zip(come, go):
        before.wait()
        after.start()
    come[2].wait()
    come[3].wait()
    part = GQ.shape[1]
    GQ[...] = RES[0, :, :part]
    GK[...] = RES[0, :, part : 2 * part]
    GV[...] = RES[0, :, 2 * part : 3 * part]
    GO[...] = RES[0, :, 3 * part :].T
    GI[...] = RES[1]
    GF[...] = RES[2]
    G1[...] = SMALL[0, :]
    G2[...] = SMALL[1, :]
    at = pl.ds(pl.multiple_of(lax.axis_index("mp") * 128, 128), 128)
    GB[...] = SMALL[8:16, at][:heads_mp, : GB.shape[1]]
    for cp in go:
        cp.wait()


def finish(L, I, RES, SMALL, part, heads_mp, buckets):
    _, rows, hid = RES.shape
    width = SMALL.shape[1]
    any_ = pl.BlockSpec(memory_space=pl.ANY)
    vm = pl.BlockSpec(memory_space=pltpu.VMEM)
    sds = jax.ShapeDtypeStruct
    f32 = [(rows, part)] * 3 + [(part, rows), (rows, hid), (rows, hid), (width,), (width,), (heads_mp, buckets)]
    return pl.pallas_call(
        functools.partial(finish_kernel, heads_mp),
        out_shape=(sds(L.shape, BF), sds(I.shape, BF)) + tuple(sds(s, F32) for s in f32),
        in_specs=[any_] * 4,
        out_specs=(any_, any_) + (vm,) * len(f32),
        scratch_shapes=[
            pltpu.VMEM((2,) + L.shape, BF),
            pltpu.VMEM(RES.shape, F32),
            pltpu.VMEM(SMALL.shape, F32),
            pltpu.SemaphoreType.DMA((2, 4)),
        ],
    )(L, I, RES, SMALL)


def body(tokens, cotangent, lengths, gain_attn, gain_ff, bias_table, w_query, w_key, w_value, w_out_attn, w_in_ff, w_out_ff):
    ndp, nmp = lax.axis_size("dp"), lax.axis_size("mp")
    seq = tokens.shape[1] * nmp
    buckets, heads_mp = bias_table.shape
    fine = 16 // math.gcd(w_query.shape[0], 16)
    groups = [list(range(g, g + fine)) for g in range(0, ndp, fine)]

    def join(a, dim):
        return a if fine == 1 else lax.all_gather(a, "dp", axis=dim, tiled=True, axis_index_groups=groups)

    def split(a, dim):
        if fine == 1:
            return a
        return lax.psum_scatter(a, "dp", scatter_dimension=dim, tiled=True, axis_index_groups=groups)

    dims = (0, 0, 0, 1, 0, 0)
    ws = tuple(join(w, d) for w, d in zip((w_query, w_key, w_value, w_out_attn, w_in_ff, w_out_ff.T), dims))
    place = np.arange(2 * seq)
    place = np.where(place < 2 * seq - 128, seq - 128 - place, seq - 128 + 2 * seq - place)
    onehot = (bucket_of(place, buckets)[None] == np.arange(128)[:, None]).astype(np.float32)
    out, ing, res, small = layer(
        tokens, cotangent, ws, bias_table.T, onehot, gain_attn, gain_ff, lengths, ndp, nmp, fine
    )[:4]
    if fine > 1:
        small = lax.psum(small, "dp", axis_index_groups=groups)
    out, ing, *grads, g1, g2, gb = finish(out, ing, res, small, w_query.shape[1], heads_mp, buckets)
    gq, gk, gv, go, gi, gf = (split(g, d) for g, d in zip(grads, dims))
    return out, ing, g1, g2, gb.T, gq, gk, gv, go, gi, gf.T


def solution(mesh):
    act = P("dp", "mp", None)
    rows, cols = P("dp", "mp"), P("mp", "dp")
    return jax.shard_map(
        body,
        mesh=mesh,
        in_specs=(act, act, P("dp"), P(), P(), P(None, "mp"), rows, rows, rows, cols, rows, cols),
        out_specs=(act, act, P(), P(), P(None, "mp"), rows, rows, rows, cols, rows, cols),
        check_vma=False,
    )
```

```python
import functools
import math

import jax
import jax.numpy as jnp
import numpy as np
from jax import lax
from jax.experimental import pallas as pl
from jax.experimental.pallas import tpu as pltpu
from jax.sharding import PartitionSpec as P

BF = jnp.bfloat16
F32 = jnp.float32
MESH = pl.DeviceIdType.MESH
EPS = 1e-06
FAR = 128
HIGHEST = lax.Precision.HIGHEST
MIB = 2**20


def bucket_of(offset, count):
    half = count // 2
    upper = (offset > 0).astype(np.int64) * half
    distance = np.abs(offset)
    exact = half // 2
    scaled = np.log(np.maximum(distance, 1) / exact) / np.log(FAR / exact) * (half - exact)
    larger = np.minimum(exact + scaled.astype(np.int64), half - 1)
    return (upper + np.where(distance < exact, distance, larger)).astype(np.int32)

PLAN = {
    ("first", 0): ("B.Y0",),
    ("start", 1): ("B.Zs", "A.Xs",),
    ("start", 2): ("A.DX", "C.Zs",),
    ("start", 3): ("C.Y0",),
    ("attend", 0): ("C.X0",),
    ("attend", 1): ("A.xd",),
    ("attend", 2): ("B.zy", "dy", "A.ds",),
    ("attend", 4): ("C.zy", "C.plane2",),
    ("attend", 6): ("B.ys", "B.Xs",),
    ("between", 0): ("C.ys",),
    ("ff", 0): ("C.z2y",),
    ("ff", 6): ("B.DX", "B.xd",),
    ("ff", 8): ("C.ds",),
    ("ff", 11): ("B.ds", "PO.sw0",),
    ("ff", 15): ("PO.sw1",),
    ("ff", 21): ("PO.yw1",),
    ("ff", 23): ("PO.st0",),
    ("between", 3): ("PI.xs0", "PO.yw0",),
    ("back", 0): ("PO.st1",),
    ("back", 1): ("PI.xs1", "PO.yt0", "lay",),
    ("back", 2): ("PO.yt1", "PI.xw0", "PA.st0",),
    ("back", 4): ("PA.st1", "PI.xy0",),
    ("back", 5): ("PA.yt0", "PI.xw1", "PO.zt0",),
    ("back", 6): ("PA.sw0", "PA.yt1",),
    ("back", 7): ("PA.zt0", "PI.xy1",),
    ("end", 0): ("PA.zt1", "PO.zt1", "PA.yw0",),
    ("end", 3): ("PA.zw0", "PA.sw1", "PA.yw1",),
    ("end", 4): ("PI.zo1", "PO.zw1", "PO.zw0",),
    ("end", 5): ("PI.zo0", "PA.zw1",),
}
MODES = {"A": "half", "B": "half", "C": "plane"}
X_FIRST = {"PA": False, "PI": True, "PO": False}
A_BY_HOPS = True


class Place:
    def __init__(self, ndp, nmp, fine, rows):
        self.dp, self.mp = lax.axis_index("dp"), lax.axis_index("mp")
        self.x, self.c = self.mp // 2, self.mp % 2
        self.fine = fine
        self.z, self.y = self.dp // fine // 2, self.dp // fine % 2
        self.nz = ndp // fine // 2
        self.nmp, self.rows = nmp, rows

    def at(self, x=None, c=None, z=None, y=None):
        x = self.x if x is None else x
        c = self.c if c is None else c
        z = self.z if z is None else z
        y = self.y if y is None else y
        return ((z * 2 + y) * self.fine + self.dp % self.fine, x * 2 + c)

    def zi(self, k):
        return lax.rem(self.z + k, self.nz)

    def block(self, z, y, count=1):
        return pl.ds(pl.multiple_of((z * 2 + y) * self.rows, self.rows), count * self.rows)

    def greet(self):
        bar = pltpu.get_barrier_semaphore()

        def tell(who):
            pl.semaphore_signal(bar, inc=1, device_id=who, device_id_type=MESH)

        tell(self.at(c=1 - self.c))
        tell(self.at(x=1 - self.x))
        tell(self.at(x=1 - self.x, c=1 - self.c))
        tell(self.at(y=1 - self.y))
        loop(1, self.nz, lambda k: tell(self.at(z=self.zi(k))))

    def met(self):
        pl.semaphore_wait(pltpu.get_barrier_semaphore(), 4 + self.nz - 1)


def remote(src, dst, ssem, rsem, who):
    return pltpu.make_async_remote_copy(
        src_ref=src, dst_ref=dst, send_sem=ssem, recv_sem=rsem, device_id=who, device_id_type=MESH
    )


def loop(lo, hi, fn):
    def step(k, carry):
        fn(k)
        return carry

    lax.fori_loop(lo, hi, step, 0)


class Gather:
    def __init__(self, here, pack, mode, W, ssem, rsem):
        self.h, self.nz, self.mode = here, here.nz, mode
        self.W = W.at[pack]
        self.ss, self.rs = ssem.at[pack], rsem.at[pack]

    def at(self, x, c, z, y):
        return self.W.at[x, c, self.h.block(z, y)]

    def send(self, src, kind, idx, who, skind=None, sidx=0):
        skind = kind if skind is None else skind
        return remote(src, src, self.ss.at[skind, sidx], self.rs.at[kind, idx], who)

    def wait_sent(self, kind, blocks):
        src = self.W.at[0, 0, self.h.block(0, 0, blocks)]
        remote(src, src, self.ss.at[kind, 0], self.rs.at[kind, 0], self.h.at(c=1 - self.h.c)).wait_send()

    def hop(self, b, step):
        h = self.h
        return self.send(self.at(h.x, h.c, b, h.y), 0, b, h.at(z=h.z + step), 0 if step > 0 else 7, b)

    def z(self, z, mine=True):
        h = self.h
        b = h.z if mine else z
        return self.send(self.at(h.x, h.c, b, h.y), 0, b, h.at(z=z))

    def y(self, z, mine=True):
        h = self.h
        return self.send(self.at(h.x, h.c, z, h.y if mine else 1 - h.y), 1, z, h.at(y=1 - h.y))

    def x(self, z, mine=True):
        h = self.h
        return self.send(self.at(h.x if mine else 1 - h.x, h.c, z, h.y), 2, z, h.at(x=1 - h.x))

    def diag_by_x(self, z):
        h = self.h
        return self.send(self.at(h.x, h.c, z, 1 - h.y), 3, z, h.at(x=1 - h.x))

    def diag_by_y(self, z):
        h = self.h
        return self.send(self.at(1 - h.x, h.c, z, h.y), 3, z, h.at(y=1 - h.y))

    def diag(self, z):
        h = self.h
        return self.send(self.at(1 - h.x, h.c, z, 1 - h.y), 3, z, h.at(x=1 - h.x))

    def z2(self, z, mine=True):
        h = self.h
        b = h.z if mine else z
        return self.send(self.at(1 - h.x, h.c, b, h.y), 4, b, h.at(z=z))

    def sib(self, half, z, mine=True):
        h = self.h
        block = self.W.at[h.x if half == 0 else 1 - h.x, h.c if mine else 1 - h.c, h.block(z, 0, 2)]
        return self.send(block, 5 + half, z, h.at(c=1 - h.c))

    def sib_wait(self, half):
        self.all(lambda z: self.sib(half, z, False).wait_recv())

    def all(self, fn):
        loop(0, self.nz, lambda k: fn(self.h.zi(k)))

    def others(self, fn):
        loop(1, self.nz, lambda k: fn(self.h.zi(k)))

    def by_x(self, z, fn):
        if self.mode == "half":
            pl.when(z % 2 == 0)(fn)

    def by_y(self, z, fn):
        if self.mode == "half":
            pl.when(z % 2 == 1)(fn)
        else:
            fn()

    def hops(self):
        h = self.h
        for step in (1, -1):
            pl.when((h.z + step >= 0) & (h.z + step < self.nz))(lambda: self.hop(h.z, step).start())
        self.y(h.z).start()

    def hops_on(self):
        h = self.h

        def on(d):
            for step in (1, -1):
                b = h.z - step * d

                @pl.when((b >= 0) & (b < self.nz))
                def _():
                    self.z(b, False).wait_recv()
                    pl.when((h.z + step >= 0) & (h.z + step < self.nz))(lambda: self.hop(b, step).start())
                    self.y(b).start()

        loop(1, self.nz, on)

    def hops_sent(self):
        h = self.h

        def on(b):
            pl.when((b <= h.z) & (h.z + 1 < self.nz))(lambda: self.hop(b, 1).wait_send())
            pl.when((b >= h.z) & (h.z >= 1))(lambda: self.hop(b, -1).wait_send())

        loop(0, self.nz, on)

    def steps(self):
        h = self.h

        def zy(z):
            self.z(z, False).wait_recv()
            self.y(z).start()

        def ys(z):
            self.y(z, False).wait_recv()
            self.sib(0, z).start()

        def z2y(z):
            self.z2(z, False).wait_recv()
            self.diag_by_y(z).start()

        def xd(z):
            self.x(z, False).wait_recv()
            self.by_y(z, lambda: self.diag_by_y(z).start())

        def ds(z):
            self.diag(z).wait_recv()
            self.sib(1, z).start()

        def plane2():
            self.x(h.z, False).wait_recv()
            self.others(lambda z: self.z2(z).start())
            self.diag_by_y(h.z).start()

        return {
            "Zs": lambda: self.others(lambda z: self.z(z).start()),
            "Y0": lambda: self.y(h.z).start(),
            "zy": lambda: self.others(zy),
            "ys": lambda: self.all(ys),
            "X0": lambda: self.x(h.z).start(),
            "plane2": plane2,
            "z2y": lambda: self.others(z2y),
            "Xs": lambda: self.all(lambda z: self.x(z).start()),
            "DX": lambda: self.all(lambda z: self.by_x(z, lambda: self.diag_by_x(z).start())),
            "xd": lambda: self.all(xd),
            "ds": lambda: self.all(ds),
        }

    def sent(self, by_hops=False):
        nz = self.nz
        if by_hops:
            self.hops_sent()
        else:
            self.wait_sent(0, nz - 1)
        self.wait_sent(1, nz)
        self.wait_sent(2, 1 if self.mode == "plane" else nz)
        self.wait_sent(3, nz)
        if self.mode == "plane":
            self.wait_sent(4, nz - 1)
        self.wait_sent(5, 2 * nz)
        self.wait_sent(6, 2 * nz)


class Swap:
    def __init__(self, here, whole, flat, sems, back):
        self.h, self.whole, self.flat, self.sems, self.back = here, whole, flat, sems, back
        self.positions = whole.shape[1]
        self.share = whole.shape[0] // here.nmp

    def views(self, s, outer, inner):
        at = pl.multiple_of((s * self.h.nmp + inner) * self.positions, self.positions)
        return self.whole.at[outer * self.share + s], self.flat.at[pl.ds(at, self.positions)]

    def copy(self, s, k, mine):
        h = self.h
        other = lax.rem(h.mp + (k if mine else h.nmp - k), h.nmp)
        sender, receiver = (h.mp, other) if mine else (other, h.mp)
        if self.back:
            dst, src = self.views(s, sender, receiver)
        else:
            src, dst = self.views(s, receiver, sender)
        if not mine:
            src = dst
        return remote(src, dst, self.sems.at[0, k, s], self.sems.at[1, k, s], (h.dp, other))

    def local(self, s):
        whole, flat = self.views(s, self.h.mp, self.h.mp)
        src, dst = (flat, whole) if self.back else (whole, flat)
        return pltpu.make_async_copy(src, dst, self.sems.at[0, 0, s])

    def start(self, s):
        for k in range(1, self.h.nmp):
            self.copy(s, k, True).start()
        self.local(s).start()

    def start_all(self):
        for s in range(self.share):
            self.start(s)

    def come(self):
        for s in range(self.share):
            for k in range(1, self.h.nmp):
                self.copy(s, k, False).wait_recv()
            self.local(s).wait()

    def sent(self):
        for s in range(self.share):
            for k in range(1, self.h.nmp):
                self.copy(s, k, True).wait_send()


class Scatter:
    def __init__(self, here, pack, x_first, mine, bufs, RES, sems):
        self.h, self.nz, self.x_first = here, here.nz, x_first
        self.MINE, self.SENT = mine
        self.R0, self.R1, self.R2, self.R3 = [b.at[pack] for b in bufs]
        self.RES = RES.at[pack]
        self.sems = [s.at[pack] for s in sems]
        self.block = here.block

    def half(self, own):
        return self.h.x if own else 1 - self.h.x

    def put(self, m, columns, value):
        @pl.when(m % 2 == self.h.c)
        def _():
            self.MINE[m // 2, :, columns] = value

        @pl.when(m % 2 != self.h.c)
        def _():
            self.SENT[:, columns] = value

    def two(self, x, r):
        return self.MINE[x, r].astype(F32) + self.R0[x, r].astype(F32)

    def sib(self, x):
        return remote(self.SENT, self.R0.at[x], self.sems[0].at[x], self.sems[1].at[x], self.h.at(c=1 - self.h.c))

    def ysend(self, x, z):
        h = self.h
        src = self.MINE.at[x, self.block(z, 1 - h.y)]
        return remote(src, self.R1.at[x, z], self.sems[2].at[x, 0], self.sems[3].at[x, z], h.at(y=1 - h.y))

    def zsend(self, x, z):
        h = self.h
        return remote(self.R1.at[x, z], self.R2.at[x, h.z], self.sems[4].at[x, 0], self.sems[5].at[x, h.z], h.at(z=z))

    def zcome(self, x, z):
        h = self.h
        return remote(self.R2.at[x, z], self.R2.at[x, z], self.sems[4].at[x, 0], self.sems[5].at[x, z], h.at(z=z))

    def xsend(self):
        h = self.h
        return remote(self.R1.at[1 - h.x, h.z], self.R3, self.sems[6].at[0], self.sems[7].at[0], h.at(x=1 - h.x))

    def xall(self, z, y_is_own, mine=True):
        h = self.h
        i = 2 if y_is_own else 4
        to = h.x if mine else 1 - h.x
        src = self.MINE.at[1 - h.x, self.block(z, h.y if y_is_own else 1 - h.y)]
        dst = (self.R1 if y_is_own else self.R2).at[to, z]
        return remote(src, dst, self.sems[i].at[1 - h.x, 0], self.sems[i + 1].at[to, z], h.at(x=1 - h.x))

    def after_group(self, m):
        pl.when(m % 2 != self.h.c)(lambda: self.sib(m // 2).start())

    def before_group(self, m, i):
        pl.when((m % 2 != self.h.c) & (i >= 2))(lambda: self.sib(1 - m // 2).wait_send())

    def sib_sent(self, own):
        self.sib(self.half(own)).wait_send()

    def each(self, fn):
        loop(1, self.nz + 1, lambda k: fn(self.h.zi(k)))

    def others(self, fn):
        loop(1, self.nz, lambda k: fn(self.h.zi(k)))

    def after_sib(self, own):
        x = self.half(own)
        self.sib(x).wait_recv()

        def on(z):
            r = self.block(z, 1 - self.h.y)
            self.MINE[x, r] = self.two(x, r).astype(BF)
            self.ysend(x, z).start()

        self.each(on)

    def after_y(self, own):
        x = self.half(own)

        def on(z):
            self.ysend(x, z).wait_recv()
            total = self.two(x, self.block(z, self.h.y)) + self.R1[x, z].astype(F32)
            self.R1[x, z] = total.astype(BF)
            pl.when(z != self.h.z)(lambda: self.zsend(x, z).start())

        self.each(on)

    def after_z(self, own):
        h, x = self.h, self.half(own)
        self.others(lambda z: self.zcome(x, z).wait_recv())

        def add(k, acc):
            return acc + self.R2[x, h.zi(k)].astype(F32)

        total = lax.fori_loop(1, self.nz, add, self.R1[x, h.z].astype(F32))
        if own:
            self.RES[...] = total
        else:
            self.R1[x, h.z] = total.astype(BF)
            self.xsend().start()

    def to_x(self):
        x = self.half(False)
        self.sib(x).wait_recv()

        def on(z):
            for y_is_own in (True, False):
                r = self.block(z, self.h.y if y_is_own else 1 - self.h.y)
                self.MINE[x, r] = self.two(x, r).astype(BF)
                self.xall(z, y_is_own).start()

        self.each(on)

    def after_x(self):
        x = self.half(True)
        self.sib(x).wait_recv()

        def on(z):
            r = self.block(z, 1 - self.h.y)
            self.xall(z, False, False).wait_recv()
            self.MINE[x, r] = (self.two(x, r) + self.R2[1 - x, z].astype(F32)).astype(BF)
            self.ysend(x, z).start()

        self.each(on)

    def after_x_and_y(self):
        x = self.half(True)

        def on(z):
            self.xall(z, True, False).wait_recv()
            self.ysend(x, z).wait_recv()
            total = self.two(x, self.block(z, self.h.y)) + self.R1[x, z].astype(F32) + self.R1[1 - x, z].astype(F32)
            self.R1[x, z] = total.astype(BF)
            pl.when(z != self.h.z)(lambda: self.zsend(x, z).start())

        self.each(on)

    def steps(self):
        out = {}
        if self.x_first:
            fns = {"xs": self.to_x, "xw": self.after_x, "xy": self.after_x_and_y, "zo": lambda: self.after_z(True)}
        else:
            fns = {}
            for tag, own in (("w", True), ("t", False)):
                fns["s" + tag] = functools.partial(self.after_sib, own)
                fns["y" + tag] = functools.partial(self.after_y, own)
                fns["z" + tag] = functools.partial(self.after_z, own)
        for name, fn in fns.items():
            for c in (0, 1):
                out[name + str(c)] = functools.partial(self.on_core, c, fn)
        return out

    def on_core(self, c, fn):
        pl.when(self.h.c == c)(fn)

    def result(self):
        if not self.x_first:
            self.xsend().wait_recv()
            self.RES[...] += self.R3[...].astype(F32)

    def wait_sent(self, i, x, blocks):
        src = self.R1.at[x, pl.ds(0, blocks)]
        remote(src, src, self.sems[i].at[x, 0], self.sems[i + 1].at[x, 0], self.h.at(c=1 - self.h.c)).wait_send()

    def sent(self):
        own, other = self.half(True), self.half(False)
        self.wait_sent(2, own, self.nz)
        self.wait_sent(4, own, self.nz - 1)
        self.wait_sent(2, other, self.nz)
        if self.x_first:
            self.wait_sent(4, other, self.nz)
        else:
            self.wait_sent(4, other, self.nz - 1)
            self.xsend().wait_send()


def dot(a, b, ca=1, cb=0, precision=None):
    return lax.dot_general(a, b, (((ca,), (cb,)), ((), ())), preferred_element_type=F32, precision=precision)


def tile_rows(i, size):
    return pl.ds(pl.multiple_of(i * size, size), size)


TILE = 256


def rsq(v):
    return lax.rsqrt(jnp.mean(v * v, axis=-1, keepdims=True) + EPS)


def toeplitz(offsets, ST):
    heads, span = ST.shape[0], ST.shape[2]
    for h in range(heads):
        row = jnp.broadcast_to(offsets[h : h + 1, :], (128, offsets.shape[1]))
        ST[h] = pltpu.roll(row, 0, 1, stride=1, stride_axis=0)[:, :span]


def biased(s, ST, h, dead):
    blocks = s.shape[0] // 128
    pieces = []
    for j in range(blocks):
        c0 = 128 * (blocks - 1 - j)
        piece = s[128 * j : 128 * (j + 1)] + ST[h, :, c0 : c0 + s.shape[1]]
        pieces.append(piece if j < blocks // 2 else piece + dead)
    return jnp.concatenate(pieces, 0)


def attend(QV, ST, h, part, dh, seq, dead, base, OV, LV):
    q0, k0, v0 = h * dh, part + h * dh, 2 * part + h * dh
    rows = pl.ds(base, seq)
    queries, keys, values = QV[rows, q0 : q0 + dh], QV[rows, k0 : k0 + dh], QV[rows, v0 : v0 + dh]
    s = biased(dot(keys, queries, 1, 1), ST, h, dead)
    top = jnp.max(s, axis=0, keepdims=True)
    e = jnp.exp(s - top)
    total = jnp.sum(e, axis=0, keepdims=True)
    prob = (e * (1.0 / total)).astype(BF)
    OV[rows, h * dh : (h + 1) * dh] = dot(prob, values, 0, 0).astype(BF)
    LV[h : h + 1, rows] = top + jnp.log(total)


GELU_C = float(np.sqrt(2.0 / np.pi))


def gelu_both(a):
    a2 = a * a
    t = jnp.tanh(a * (GELU_C + (GELU_C * 0.044715) * a2))
    half = 0.5 + 0.5 * t
    slope = half + (0.5 * a) * (1.0 - t * t) * (GELU_C + (3.0 * GELU_C * 0.044715) * a2)
    return a * half, slope


def attend_back(QV, ST, DO, LV, DL, GQKV, D, h, part, dh, seq, dead, base):
    rows = pl.ds(base, seq)
    q0, k0, v0 = h * dh, part + h * dh, 2 * part + h * dh
    queries, keys, values = QV[rows, q0 : q0 + dh], QV[rows, k0 : k0 + dh], QV[rows, v0 : v0 + dh]
    d_o = DO[rows, h * dh : (h + 1) * dh]
    s = biased(dot(keys, queries, 1, 1), ST, h, dead)
    prob = jnp.exp(s - LV[h : h + 1, rows])
    dprob = dot(values, d_o, 1, 1)
    gs = (prob * (dprob - DL[h : h + 1, rows])).astype(BF)
    GQKV[rows, v0 : v0 + dh] = dot(prob.astype(BF), d_o).astype(BF)
    GQKV[rows, k0 : k0 + dh] = dot(gs, queries).astype(BF)
    GQKV[rows, q0 : q0 + dh] = dot(keys.T, gs).astype(BF).T
    blocks = seq // 128
    for d in range(1 - blocks, blocks):
        c0 = 128 * (blocks - 1 - d)
        acc = D[h, :, c0 : c0 + 128]
        for j in range(max(0, d), min(blocks, blocks + d)):
            acc += gs[128 * j : 128 * (j + 1), 128 * (j - d) : 128 * (j - d + 1)].astype(F32)
        D[h, :, c0 : c0 + 128] = acc


def layer_kernel(cfg, tok, cot, wq, wk, wv, wo, wi, wf_t, table_t, onehot, gain1, gain2, lens, *refs):
    ndp, nmp, fine, seq, heads_mp = cfg
    L, I, RES, SMALL, W, QKV, O, LSE = refs[:8]
    OWN, OFFV, XV, DYV, N2, N2T, DYT, U, GA, HV, FF, GN, BV, CV, QV, OV, LV, DL, ST, D = refs[8:28]
    FFMINE, SENT = refs[28:30]
    bufs, SR, SZ = refs[30:34], refs[34], refs[35]
    ssem, rsem, xsem, dysem, lsem, isem, bsem, osem, wsem, qsem, ssmall, rsmall, csem = refs[36:49]
    sems = refs[49:57]
    rows, part = wq.shape
    h = Place(ndp, nmp, fine, rows)
    h.greet()
    n, width = XV.shape
    hid = U.shape[1]
    dh = part // heads_mp
    share = n // seq
    tiles = n // TILE
    nz = h.nz

    def gain(ref):
        return ref[...].reshape(1, width)

    def go(copies):
        for cp in copies:
            cp.start()

    def done(copies):
        for cp in copies:
            cp.wait()

    def run(section, at, static=None, period=1):
        for (name, slot), steps in PLAN.items():
            if name == section and (slot == at if static is None else slot % period in static):

                def fn(steps=steps):
                    for step in steps:
                        ACTIONS[step]()

                if static is None:
                    fn()
                else:
                    pl.when(at == slot)(fn)

    OWN[0, :, :part] = wq[...].astype(BF)
    OWN[0, :, part : 2 * part] = wk[...].astype(BF)
    OWN[0, :, 2 * part : 3 * part] = wv[...].astype(BF)
    OWN[0, :, 3 * part :] = wo[...].T.astype(BF)
    OWN[1] = wi[...].astype(BF)
    OWN[2] = wf_t[...].astype(BF)
    own = [pltpu.make_async_copy(OWN.at[p], W.at[p, h.x, h.c, h.block(h.z, h.y)], csem.at[p]) for p in range(3)]
    go(own)
    OFFV[h.mp] = jnp.zeros_like(OFFV[0])
    OFFV[h.mp, :heads_mp] = dot(table_t[...], onehot[: table_t.shape[1], :], 1, 0, HIGHEST)

    def offs(k, mine=True):
        other = lax.rem(h.mp + (k if mine else nmp - k), nmp)
        at = OFFV.at[h.mp if mine else other]
        return remote(at, at, bsem.at[0, k], bsem.at[1, k], (h.dp, other))

    A, B, C = [Gather(h, p, MODES[name], W, ssem, rsem) for p, name in enumerate("ABC")]
    mines = (CV, SENT.at[0]), (FFMINE.at[0], SENT.at[0]), (FFMINE.at[1], SENT.at[1])
    PA, PI, PO = [
        Scatter(h, p, X_FIRST[name], mines[p], bufs, RES, sems) for p, name in enumerate(("PA", "PI", "PO"))
    ]
    sx = Swap(h, tok, XV, xsem, False)
    sd = Swap(h, cot, DYV, dysem, False)
    sl = Swap(h, L, DYV, lsem, True)
    si = Swap(h, I, XV, isem, True)

    ACTIONS = {"dy": sd.start_all, "lay": sl.start_all}
    for name, part_of in (("A", A), ("B", B), ("C", C), ("PA", PA), ("PI", PI), ("PO", PO)):
        ACTIONS.update({name + "." + step: fn for step, fn in part_of.steps().items()})

    done(own)
    h.met()
    if A_BY_HOPS:
        A.hops()
    else:
        ACTIONS["A.Zs"]()
        ACTIONS["A.Y0"]()
    run("first", 0)
    sx.start_all()
    for k in range(1, nmp):
        offs(k).start()
    run("start", 0)
    if A_BY_HOPS:
        A.hops_on()
    else:
        ACTIONS["A.zy"]()
    run("start", 1)
    ACTIONS["A.ys"]()
    run("start", 2)
    sx.come()
    run("start", 3)

    def norm(t):
        r = tile_rows(t, TILE)
        x = XV[r, :].astype(F32)
        N2[r, :] = (x * rsq(x) * gain(gain1)).astype(BF)
        HV[r, :] = x

    loop(0, tiles, norm)
    A.sib_wait(0)

    def group(i):
        return lax.rem(2 * h.x + i, nmp)

    def load(p, i, m, V, sem):
        slot = lax.rem(i, 2)
        return pltpu.make_async_copy(W.at[p, m // 2, m % 2], V.at[slot], sem.at[slot])

    def load_a(i):
        return load(0, i, group(i), BV, wsem.at[0])

    def store(i):
        m, slot = group(i), lax.rem(i, 2)
        return (
            pltpu.make_async_copy(QV.at[slot], QKV.at[m], osem.at[0, slot]),
            pltpu.make_async_copy(OV.at[slot], O.at[m], osem.at[1, slot]),
            pltpu.make_async_copy(LV.at[slot], LSE.at[m], osem.at[2, slot]),
        )

    load_a(0).start()
    for k in range(1, nmp):
        offs(k, False).wait_recv()

    def attn_group(i):
        slot = lax.rem(i, 2)
        m = group(i)

        @pl.when(i == 2)
        def _():
            A.sib_wait(1)
            load_a(2).start()

        toeplitz(OFFV.at[m], ST)
        pl.when(i >= 2)(lambda: done(store(i - 2)))
        load_a(i).wait()
        pl.when((i == 0) | (i == 2))(lambda: load_a(i + 1).start())

        QV[slot] = dot(N2[...], BV[slot, :, : 3 * part]).astype(BF)

        def pair(p):
            base = pl.multiple_of(p * seq, seq)
            off = jnp.where(lens[h.mp * share + p] < seq, -1e30, 0.0).astype(F32)
            run("attend", i * share + p, range(1))
            for head in range(heads_mp):
                attend(QV.at[slot], ST, head, part, dh, seq, off, base, OV.at[slot], LV.at[slot])

        loop(0, share, pair)

        HV[...] += dot(OV[slot], BV[slot, :, 3 * part :], 1, 1)
        go(store(i))

    loop(0, nmp, attn_group)

    run("between", 0)

    def load_ff(i):
        m = group(i)
        return load(1, i, m, BV, wsem.at[0]), load(2, i, m, CV, wsem.at[1])

    sd.come()
    SMALL[...] = jnp.zeros_like(SMALL)

    def prep(t):
        r = tile_rows(t, TILE)
        hidden = HV[r, :]
        n2 = (hidden * rsq(hidden) * gain(gain2)).astype(BF)
        N2[r, :] = n2
        N2T[:, r] = n2.T
        DYT[:, r] = DYV[r, :].T
        FF[r, :] = hidden
        GN[r, :] = jnp.zeros((TILE, width), F32)

    loop(0, tiles, prep)
    run("between", 1)
    B.sib_wait(0)
    C.sib_wait(0)
    go(load_ff(0))

    steps = tiles + 2

    def ff_group(i):
        slot = lax.rem(i, 2)
        m = group(i)
        done(load_ff(i))
        pl.when((i == 0) | (i == 2))(lambda: go(load_ff(i + 1)))

        def rowwise(t):
            run("ff", i * steps + t, range(tiles), steps)
            r = tile_rows(t, TILE)
            b = BV[slot]
            c = CV[slot]
            a = dot(N2[r, :], b)
            gu = dot(DYV[r, :], c)
            u, slope = gelu_both(a)
            u = u.astype(BF)
            ga = (gu * slope).astype(BF)
            U[r, :] = u
            GA[r, :] = ga
            FF[r, :] += dot(u, c, 1, 1)
            GN[r, :] += dot(ga, b, 1, 1)

        loop(0, tiles, rowwise)
        PI.before_group(m, i)
        PO.before_group(m, i)

        run("ff", i * steps + tiles, (tiles,), steps)
        PI.put(m, slice(None), dot(N2T[...], GA[...]).astype(BF))
        run("ff", i * steps + tiles + 1, (tiles + 1,), steps)
        PO.put(m, slice(None), dot(DYT[...], U[...]).astype(BF))
        PI.after_group(m)
        PO.after_group(m)

        @pl.when(i == 1)
        def _():
            run("between", 2)
            B.sib_wait(1)
            C.sib_wait(1)
            go(load_ff(2))

    loop(0, nmp, ff_group)

    def back_group(i):
        return lax.rem(2 * (1 - h.x) + i, nmp)

    def load_attn(i):
        m, slot = back_group(i), lax.rem(i, 2)
        return (
            load(0, i, m, BV, wsem.at[0]),
            pltpu.make_async_copy(QKV.at[m], QV.at[slot], qsem.at[0, slot]),
            pltpu.make_async_copy(O.at[m], OV.at[slot], qsem.at[1, slot]),
            pltpu.make_async_copy(LSE.at[m], LV.at[slot], qsem.at[2, slot]),
        )

    for i in (nmp - 2, nmp - 1):
        done(store(i))
    go(load_attn(0))
    run("between", 3)

    def mid(t):
        r = tile_rows(t, TILE)
        hidden = HV[r, :]
        r2 = rsq(hidden)
        nh = hidden * r2
        g = GN[r, :]
        SMALL[1:2, :] += jnp.sum(g * nh, axis=0, keepdims=True)
        e = g * gain(gain2)
        gh = DYV[r, :].astype(F32) + r2 * (e - nh * jnp.mean(e * nh, axis=-1, keepdims=True))
        DYV[r, :] = FF[r, :].astype(BF)
        HV[r, :] = gh
        low = gh.astype(BF)
        N2[r, :] = low
        DYT[:, r] = low.T
        x = XV[r, :].astype(F32)
        N2T[:, r] = (x * rsq(x) * gain(gain1)).astype(BF).T
        GN[r, :] = jnp.zeros((TILE, width), F32)
        U[r, 3 * part :] = jnp.zeros((TILE, hid - 3 * part), BF)

    loop(0, tiles, mid)

    GQKV, DO = U, GA
    wide = -(-3 * part // 128) * 128

    def last(p, t):
        r = pl.ds(pl.multiple_of(p * seq + t * TILE, TILE), TILE)
        x = XV[r, :].astype(F32)
        r1 = rsq(x)
        nx = x * r1
        g = GN[r, :]
        SMALL[0:1, :] += jnp.sum(g * nx, axis=0, keepdims=True)
        e = g * gain(gain1)
        XV[r, :] = (HV[r, :] + r1 * (e - nx * jnp.mean(e * nx, axis=-1, keepdims=True))).astype(BF)


    head_of = (lax.broadcasted_iota(jnp.int32, (8, part), 1) // dh == lax.broadcasted_iota(jnp.int32, (8, part), 0)).astype(F32)

    def attn_back_group(i):
        slot = lax.rem(i, 2)
        m = back_group(i)
        toeplitz(OFFV.at[m], ST)
        D[...] = jnp.zeros_like(D)
        done(load_attn(i))
        pl.when(i + 1 < nmp)(lambda: go(load_attn(i + 1)))

        d_o = dot(N2[...], BV[slot, :, 3 * part :]).astype(BF)
        DO[:, :part] = d_o
        DL[...] = dot(head_of, OV[slot].astype(F32) * d_o.astype(F32), 1, 1, HIGHEST)

        def join(p):
            r = tile_rows(p, seq)
            GN[r, :] += dot(GQKV[r, :wide], BV[slot, :, :wide], 1, 1)

            @pl.when(i == nmp - 1)
            def _():
                loop(0, seq // TILE, functools.partial(last, p))
                pl.when(p + 1 < share)(lambda: si.start(p))

        def pair(p):
            pl.when(p > 0)(lambda: join(p - 1))
            base = pl.multiple_of(p * seq, seq)
            off = jnp.where(lens[h.mp * share + p] < seq, -1e30, 0.0).astype(F32)
            run("back", i * share + p, range(1))
            for head in range(heads_mp):
                attend_back(QV.at[slot], ST, DO, LV.at[slot], DL, GQKV, D, head, part, dh, seq, off, base)

        loop(0, share, pair)
        PA.before_group(m, i)
        pl.when((m % 2 != h.c) & (i < 2))(lambda: PI.sib_sent(False))

        PA.put(m, slice(0, 3 * part), dot(N2T[...], GQKV[:, : 3 * part]).astype(BF))
        PA.put(m, slice(3 * part, hid), dot(DYT[...], OV[slot]).astype(BF))
        PA.after_group(m)
        join(share - 1)
        sums = []
        for head in range(heads_mp):
            strip = jnp.concatenate([D[head], jnp.zeros((128, 128), F32)], 1)
            span = strip.shape[1]
            half = 64
            while half:
                strip = strip[:half] + pltpu.roll(strip[half:], span - half, 1)
                half //= 2
            sums.append(strip)
        sums = jnp.concatenate(sums + [jnp.zeros((8 - heads_mp, span), F32)], 0)
        at = pl.ds(pl.multiple_of(m * 128, 128), 128)
        SMALL[8:16, at] = dot(sums, onehot[...], 1, 1, HIGHEST)

    loop(0, nmp, attn_back_group)
    run("end", 0)

    small = [
        remote(SMALL, SR.at[i], ssmall.at[i], rsmall.at[i], who)
        for i, who in enumerate((h.at(c=1 - h.c), h.at(x=1 - h.x), h.at(y=1 - h.y), h.at(c=1 - h.c)))
    ]

    def small_z(k, mine):
        z = h.zi(k)
        b = h.z if mine else z
        return remote(SZ.at[b], SZ.at[b], ssmall.at[4 + z], rsmall.at[4 + b], h.at(z=z))

    def small_step(i):
        small[i].wait()
        SMALL[...] += SR[i]

    def on_core_0(fn):
        pl.when(h.c == 0)(fn)

    small[0].start()
    small_step(0)
    on_core_0(lambda: small[1].start())
    si.start(share - 1)
    run("end", 1)

    @on_core_0
    def _():
        small_step(1)
        small[2].start()

    run("end", 2)

    @on_core_0
    def _():
        small_step(2)
        SZ[h.z] = SMALL[...]
        loop(1, nz, lambda k: small_z(k, True).start())

    run("end", 3)

    @on_core_0
    def _():
        loop(1, nz, lambda k: small_z(k, False).wait_recv())
        SMALL[...] = lax.fori_loop(1, nz, lambda z, acc: acc + SZ[z], SZ[0])
        small[3].start()

    run("end", 4)

    @pl.when(h.c == 1)
    def _():
        small[3].wait_recv()
        SMALL[...] = SR[3]

    run("end", 5)
    for T in (PA, PI, PO):
        T.result()
        T.sent()
    PA.sib_sent(True)
    PO.sib_sent(False)

    @on_core_0
    def _():
        loop(1, nz, lambda k: small_z(k, True).wait_send())
        small[3].wait_send()

    A.sent(A_BY_HOPS)
    B.sent()
    C.sent()
    for k in range(1, nmp):
        offs(k).wait_send()
    sx.sent()
    sd.sent()
    sl.come()
    sl.sent()
    si.come()
    si.sent()


def layer(tok, cot, ws, table_t, onehot, gain1, gain2, lens, ndp, nmp, fine):
    pairs, positions, width = tok.shape
    rows, part = ws[0].shape
    hid = ws[4].shape[1]
    heads_mp = table_t.shape[0]
    seq = positions * nmp
    share = pairs // nmp
    n = share * seq
    nz = ndp // fine // 2
    any_ = pl.BlockSpec(memory_space=pl.ANY)
    vm = pl.BlockSpec(memory_space=pltpu.VMEM)
    dma = pltpu.SemaphoreType.DMA
    sds = jax.ShapeDtypeStruct
    bf = lambda *s: pltpu.VMEM(s, BF)
    fl = lambda *s: pltpu.VMEM(s, F32)
    act = sds((pairs, positions, width), BF)
    return pl.pallas_call(
        functools.partial(layer_kernel, (ndp, nmp, fine, seq, heads_mp)),
        out_shape=(act, act)
        + (
            sds((3, rows, hid), F32),
            sds((16, width), F32),
            sds((3, nmp // 2, 2, width, hid), BF),
            sds((nmp, n, 3 * part), BF),
            sds((nmp, n, part), BF),
            sds((nmp, 8, n), F32),
        ),
        in_specs=[any_, any_] + [vm] * 10 + [pl.BlockSpec(memory_space=pltpu.SMEM)],
        out_specs=(any_, any_) + (vm,) * 2 + (any_,) * 4,
        scratch_shapes=[
            bf(3, rows, hid),
            fl(nmp, 8, 2 * seq),
            bf(n, width),
            bf(n, width),
            bf(n, width),
            bf(width, n),
            bf(width, n),
            bf(n, hid),
            bf(n, hid),
            fl(n, width),
            fl(n, width),
            fl(n, width),
            bf(2, width, hid),
            bf(2, width, hid),
            bf(2, n, 3 * part),
            bf(2, n, part),
            fl(2, 8, n),
            fl(8, n),
            fl(heads_mp, 128, 2 * seq - 128),
            fl(heads_mp, 128, 2 * seq - 128),
            bf(2, 2, width, hid),
            bf(2, width, hid),
            bf(3, 2, width, hid),
            bf(3, 2, nz, rows, hid),
            bf(3, 2, nz, rows, hid),
            bf(3, rows, hid),
            fl(4, 16, width),
            fl(nz, 16, width),
            dma((3, 8, nz)),
            dma((3, 8, nz)),
        ]
        + [dma((2, nmp, share))] * 4
        + [dma((2, nmp)), dma((3, 2)), dma((2, 2)), dma((3, 2)), dma((4 + nz,)), dma((4 + nz,)), dma((3,))]
        + [dma((3, 2))] * 2
        + [dma((3, 2, nz))] * 4
        + [dma((3, 1))] * 2,
        compiler_params=pltpu.CompilerParams(collective_id=0, has_side_effects=True, vmem_limit_bytes=63 * MIB),
    )(tok, cot, *ws, table_t, onehot, gain1, gain2, lens)


def finish_kernel(heads_mp, L, I, RES_, SMALL_, L2, I2, GQ, GK, GV, GO, GI, GF, G1, G2, GB, buf, RES, SMALL, sem):
    come = [
        pltpu.make_async_copy(a, b, sem.at[0, i])
        for i, (a, b) in enumerate(((L, buf.at[0]), (I, buf.at[1]), (RES_, RES), (SMALL_, SMALL)))
    ]
    go = [pltpu.make_async_copy(buf.at[i], a, sem.at[1, i]) for i, a in enumerate((L2, I2))]
    for cp in come:
        cp.start()
    for before, after in zip(come, go):
        before.wait()
        after.start()
    come[2].wait()
    come[3].wait()
    part = GQ.shape[1]
    GQ[...] = RES[0, :, :part]
    GK[...] = RES[0, :, part : 2 * part]
    GV[...] = RES[0, :, 2 * part : 3 * part]
    GO[...] = RES[0, :, 3 * part :].T
    GI[...] = RES[1]
    GF[...] = RES[2]
    G1[...] = SMALL[0, :]
    G2[...] = SMALL[1, :]
    at = pl.ds(pl.multiple_of(lax.axis_index("mp") * 128, 128), 128)
    GB[...] = SMALL[8:16, at][:heads_mp, : GB.shape[1]]
    for cp in go:
        cp.wait()


def finish(L, I, RES, SMALL, part, heads_mp, buckets):
    _, rows, hid = RES.shape
    width = SMALL.shape[1]
    any_ = pl.BlockSpec(memory_space=pl.ANY)
    vm = pl.BlockSpec(memory_space=pltpu.VMEM)
    sds = jax.ShapeDtypeStruct
    f32 = [(rows, part)] * 3 + [(part, rows), (rows, hid), (rows, hid), (width,), (width,), (heads_mp, buckets)]
    return pl.pallas_call(
        functools.partial(finish_kernel, heads_mp),
        out_shape=(sds(L.shape, BF), sds(I.shape, BF)) + tuple(sds(s, F32) for s in f32),
        in_specs=[any_] * 4,
        out_specs=(any_, any_) + (vm,) * len(f32),
        scratch_shapes=[
            pltpu.VMEM((2,) + L.shape, BF),
            pltpu.VMEM(RES.shape, F32),
            pltpu.VMEM(SMALL.shape, F32),
            pltpu.SemaphoreType.DMA((2, 4)),
        ],
    )(L, I, RES, SMALL)


def body(tokens, cotangent, lengths, gain_attn, gain_ff, bias_table, w_query, w_key, w_value, w_out_attn, w_in_ff, w_out_ff):
    ndp, nmp = lax.axis_size("dp"), lax.axis_size("mp")
    seq = tokens.shape[1] * nmp
    buckets, heads_mp = bias_table.shape
    fine = 16 // math.gcd(w_query.shape[0], 16)
    groups = [list(range(g, g + fine)) for g in range(0, ndp, fine)]

    def join(a, dim):
        return a if fine == 1 else lax.all_gather(a, "dp", axis=dim, tiled=True, axis_index_groups=groups)

    def split(a, dim):
        if fine == 1:
            return a
        return lax.psum_scatter(a, "dp", scatter_dimension=dim, tiled=True, axis_index_groups=groups)

    dims = (0, 0, 0, 1, 0, 0)
    ws = tuple(join(w, d) for w, d in zip((w_query, w_key, w_value, w_out_attn, w_in_ff, w_out_ff.T), dims))
    place = np.arange(2 * seq)
    place = np.where(place < 2 * seq - 128, seq - 128 - place, seq - 128 + 2 * seq - place)
    onehot = (bucket_of(place, buckets)[None] == np.arange(128)[:, None]).astype(np.float32)
    out, ing, res, small = layer(
        tokens, cotangent, ws, bias_table.T, onehot, gain_attn, gain_ff, lengths, ndp, nmp, fine
    )[:4]
    if fine > 1:
        small = lax.psum(small, "dp", axis_index_groups=groups)
    out, ing, *grads, g1, g2, gb = finish(out, ing, res, small, w_query.shape[1], heads_mp, buckets)
    gq, gk, gv, go, gi, gf = (split(g, d) for g, d in zip(grads, dims))
    return out, ing, g1, g2, gb.T, gq, gk, gv, go, gi, gf.T


def solution(mesh):
    act = P("dp", "mp", None)
    rows, cols = P("dp", "mp"), P("mp", "dp")
    return jax.shard_map(
        body,
        mesh=mesh,
        in_specs=(act, act, P("dp"), P(), P(), P(None, "mp"), rows, rows, rows, cols, rows, cols),
        out_specs=(act, act, P(), P(), P(None, "mp"), rows, rows, rows, cols, rows, cols),
        check_vma=False,
    )
```

```python
import functools
import math

import jax
import jax.numpy as jnp
import numpy as np
from jax import lax
from jax.experimental import pallas as pl
from jax.experimental.pallas import tpu as pltpu
from jax.sharding import PartitionSpec as P

BF = jnp.bfloat16
F32 = jnp.float32
MESH = pl.DeviceIdType.MESH
EPS = 1e-06
FAR = 128
HIGHEST = lax.Precision.HIGHEST
MIB = 2**20


def bucket_of(offset, count):
    half = count // 2
    upper = (offset > 0).astype(np.int64) * half
    distance = np.abs(offset)
    exact = half // 2
    scaled = np.log(np.maximum(distance, 1) / exact) / np.log(FAR / exact) * (half - exact)
    larger = np.minimum(exact + scaled.astype(np.int64), half - 1)
    return (upper + np.where(distance < exact, distance, larger)).astype(np.int32)

PLAN = {
    ("first", 0): ("B.Y0",),
    ("start", 1): ("B.Zs", "A.Xs",),
    ("start", 2): ("A.DX", "C.Zs",),
    ("start", 3): ("C.Y0",),
    ("attend", 0): ("C.X0",),
    ("attend", 1): ("A.xd",),
    ("attend", 2): ("B.zy", "dy", "A.ds",),
    ("attend", 4): ("C.zy", "C.plane2",),
    ("attend", 6): ("B.ys", "B.Xs",),
    ("between", 0): ("C.ys",),
    ("ff", 0): ("C.z2y",),
    ("ff", 6): ("B.DX", "B.xd",),
    ("ff", 8): ("C.ds",),
    ("ff", 11): ("B.ds", "PO.sw0",),
    ("ff", 15): ("PO.sw1",),
    ("ff", 21): ("PO.yw1",),
    ("ff", 23): ("PO.st0",),
    ("between", 3): ("PI.xs0", "PO.yw0",),
    ("back", 0): ("PO.st1",),
    ("back", 1): ("PI.xs1", "PO.yt0", "lay",),
    ("back", 2): ("PO.yt1", "PI.xw0", "PA.st0",),
    ("back", 4): ("PA.st1", "PI.xy0",),
    ("back", 5): ("PA.yt0", "PI.xw1", "PO.zt0",),
    ("back", 6): ("PA.sw0", "PA.yt1",),
    ("back", 7): ("PA.zt0", "PI.xy1",),
    ("end", 0): ("PA.zt1", "PO.zt1", "PA.yw0",),
    ("end", 3): ("PA.zw0", "PA.sw1", "PA.yw1",),
    ("end", 4): ("PI.zo1", "PO.zw1", "PO.zw0",),
    ("end", 5): ("PI.zo0", "PA.zw1",),
}
MODES = {"A": "half", "B": "half", "C": "plane"}
X_FIRST = {"PA": False, "PI": True, "PO": False}
A_BY_HOPS = True


class Place:
    def __init__(self, ndp, nmp, fine, rows):
        self.dp, self.mp = lax.axis_index("dp"), lax.axis_index("mp")
        self.x, self.c = self.mp // 2, self.mp % 2
        self.fine = fine
        self.z, self.y = self.dp // fine // 2, self.dp // fine % 2
        self.nz = ndp // fine // 2
        self.nmp, self.rows = nmp, rows

    def at(self, x=None, c=None, z=None, y=None):
        x = self.x if x is None else x
        c = self.c if c is None else c
        z = self.z if z is None else z
        y = self.y if y is None else y
        return ((z * 2 + y) * self.fine + self.dp % self.fine, x * 2 + c)

    def zi(self, k):
        return lax.rem(self.z + k, self.nz)

    def block(self, z, y, count=1):
        return pl.ds(pl.multiple_of((z * 2 + y) * self.rows, self.rows), count * self.rows)

    def greet(self):
        bar = pltpu.get_barrier_semaphore()

        def tell(who):
            pl.semaphore_signal(bar, inc=1, device_id=who, device_id_type=MESH)

        tell(self.at(c=1 - self.c))
        tell(self.at(x=1 - self.x))
        tell(self.at(x=1 - self.x, c=1 - self.c))
        tell(self.at(y=1 - self.y))
        loop(1, self.nz, lambda k: tell(self.at(z=self.zi(k))))

    def met(self):
        pl.semaphore_wait(pltpu.get_barrier_semaphore(), 4 + self.nz - 1)


def remote(src, dst, ssem, rsem, who):
    return pltpu.make_async_remote_copy(
        src_ref=src, dst_ref=dst, send_sem=ssem, recv_sem=rsem, device_id=who, device_id_type=MESH
    )


def loop(lo, hi, fn):
    def step(k, carry):
        fn(k)
        return carry

    lax.fori_loop(lo, hi, step, 0)


class Gather:
    def __init__(self, here, pack, mode, W, ssem, rsem):
        self.h, self.nz, self.mode = here, here.nz, mode
        self.W = W.at[pack]
        self.ss, self.rs = ssem.at[pack], rsem.at[pack]

    def at(self, x, c, z, y):
        return self.W.at[x, c, self.h.block(z, y)]

    def send(self, src, kind, idx, who, skind=None, sidx=0):
        skind = kind if skind is None else skind
        return remote(src, src, self.ss.at[skind, sidx], self.rs.at[kind, idx], who)

    def wait_sent(self, kind, blocks):
        src = self.W.at[0, 0, self.h.block(0, 0, blocks)]
        remote(src, src, self.ss.at[kind, 0], self.rs.at[kind, 0], self.h.at(c=1 - self.h.c)).wait_send()

    def hop(self, b, step):
        h = self.h
        return self.send(self.at(h.x, h.c, b, h.y), 0, b, h.at(z=h.z + step), 0 if step > 0 else 7, b)

    def z(self, z, mine=True):
        h = self.h
        b = h.z if mine else z
        return self.send(self.at(h.x, h.c, b, h.y), 0, b, h.at(z=z))

    def y(self, z, mine=True):
        h = self.h
        return self.send(self.at(h.x, h.c, z, h.y if mine else 1 - h.y), 1, z, h.at(y=1 - h.y))

    def x(self, z, mine=True):
        h = self.h
        return self.send(self.at(h.x if mine else 1 - h.x, h.c, z, h.y), 2, z, h.at(x=1 - h.x))

    def diag_by_x(self, z):
        h = self.h
        return self.send(self.at(h.x, h.c, z, 1 - h.y), 3, z, h.at(x=1 - h.x))

    def diag_by_y(self, z):
        h = self.h
        return self.send(self.at(1 - h.x, h.c, z, h.y), 3, z, h.at(y=1 - h.y))

    def diag(self, z):
        h = self.h
        return self.send(self.at(1 - h.x, h.c, z, 1 - h.y), 3, z, h.at(x=1 - h.x))

    def z2(self, z, mine=True):
        h = self.h
        b = h.z if mine else z
        return self.send(self.at(1 - h.x, h.c, b, h.y), 4, b, h.at(z=z))

    def sib(self, half, z, mine=True):
        h = self.h
        block = self.W.at[h.x if half == 0 else 1 - h.x, h.c if mine else 1 - h.c, h.block(z, 0, 2)]
        return self.send(block, 5 + half, z, h.at(c=1 - h.c))

    def sib_wait(self, half):
        self.all(lambda z: self.sib(half, z, False).wait_recv())

    def all(self, fn):
        loop(0, self.nz, lambda k: fn(self.h.zi(k)))

    def others(self, fn):
        loop(1, self.nz, lambda k: fn(self.h.zi(k)))

    def by_x(self, z, fn):
        if self.mode == "half":
            pl.when(z % 2 == 0)(fn)

    def by_y(self, z, fn):
        if self.mode == "half":
            pl.when(z % 2 == 1)(fn)
        else:
            fn()

    def hops(self):
        h = self.h
        for step in (1, -1):
            pl.when((h.z + step >= 0) & (h.z + step < self.nz))(lambda: self.hop(h.z, step).start())
        self.y(h.z).start()

    def hops_on(self):
        h = self.h

        def on(d):
            for step in (1, -1):
                b = h.z - step * d

                @pl.when((b >= 0) & (b < self.nz))
                def _():
                    self.z(b, False).wait_recv()
                    pl.when((h.z + step >= 0) & (h.z + step < self.nz))(lambda: self.hop(b, step).start())
                    self.y(b).start()

        loop(1, self.nz, on)

    def hops_sent(self):
        h = self.h

        def on(b):
            pl.when((b <= h.z) & (h.z + 1 < self.nz))(lambda: self.hop(b, 1).wait_send())
            pl.when((b >= h.z) & (h.z >= 1))(lambda: self.hop(b, -1).wait_send())

        loop(0, self.nz, on)

    def steps(self):
        h = self.h

        def zy(z):
            self.z(z, False).wait_recv()
            self.y(z).start()

        def ys(z):
            self.y(z, False).wait_recv()
            self.sib(0, z).start()

        def z2y(z):
            self.z2(z, False).wait_recv()
            self.diag_by_y(z).start()

        def xd(z):
            self.x(z, False).wait_recv()
            self.by_y(z, lambda: self.diag_by_y(z).start())

        def ds(z):
            self.diag(z).wait_recv()
            self.sib(1, z).start()

        def plane2():
            self.x(h.z, False).wait_recv()
            self.others(lambda z: self.z2(z).start())
            self.diag_by_y(h.z).start()

        return {
            "Zs": lambda: self.others(lambda z: self.z(z).start()),
            "Y0": lambda: self.y(h.z).start(),
            "zy": lambda: self.others(zy),
            "ys": lambda: self.all(ys),
            "X0": lambda: self.x(h.z).start(),
            "plane2": plane2,
            "z2y": lambda: self.others(z2y),
            "Xs": lambda: self.all(lambda z: self.x(z).start()),
            "DX": lambda: self.all(lambda z: self.by_x(z, lambda: self.diag_by_x(z).start())),
            "xd": lambda: self.all(xd),
            "ds": lambda: self.all(ds),
        }

    def sent(self, by_hops=False):
        nz = self.nz
        if by_hops:
            self.hops_sent()
        else:
            self.wait_sent(0, nz - 1)
        self.wait_sent(1, nz)
        self.wait_sent(2, 1 if self.mode == "plane" else nz)
        self.wait_sent(3, nz)
        if self.mode == "plane":
            self.wait_sent(4, nz - 1)
        self.wait_sent(5, 2 * nz)
        self.wait_sent(6, 2 * nz)


class Swap:
    def __init__(self, here, whole, flat, sems, back):
        self.h, self.whole, self.flat, self.sems, self.back = here, whole, flat, sems, back
        self.positions = whole.shape[1]
        self.share = whole.shape[0] // here.nmp

    def views(self, s, outer, inner):
        at = pl.multiple_of((s * self.h.nmp + inner) * self.positions, self.positions)
        return self.whole.at[outer * self.share + s], self.flat.at[pl.ds(at, self.positions)]

    def copy(self, s, k, mine):
        h = self.h
        other = lax.rem(h.mp + (k if mine else h.nmp - k), h.nmp)
        sender, receiver = (h.mp, other) if mine else (other, h.mp)
        if self.back:
            dst, src = self.views(s, sender, receiver)
        else:
            src, dst = self.views(s, receiver, sender)
        if not mine:
            src = dst
        return remote(src, dst, self.sems.at[0, k, s], self.sems.at[1, k, s], (h.dp, other))

    def local(self, s):
        whole, flat = self.views(s, self.h.mp, self.h.mp)
        src, dst = (flat, whole) if self.back else (whole, flat)
        return pltpu.make_async_copy(src, dst, self.sems.at[0, 0, s])

    def start(self, s):
        for k in range(1, self.h.nmp):
            self.copy(s, k, True).start()
        self.local(s).start()

    def start_all(self):
        for s in range(self.share):
            self.start(s)

    def come(self):
        for s in range(self.share):
            for k in range(1, self.h.nmp):
                self.copy(s, k, False).wait_recv()
            self.local(s).wait()

    def sent(self):
        for s in range(self.share):
            for k in range(1, self.h.nmp):
                self.copy(s, k, True).wait_send()


class Scatter:
    def __init__(self, here, pack, x_first, mine, bufs, RES, sems):
        self.h, self.nz, self.x_first = here, here.nz, x_first
        self.MINE, self.SENT = mine
        self.R0, self.R1, self.R2, self.R3 = [b.at[pack] for b in bufs]
        self.RES = RES.at[pack]
        self.sems = [s.at[pack] for s in sems]
        self.block = here.block

    def half(self, own):
        return self.h.x if own else 1 - self.h.x

    def put(self, m, columns, value):
        @pl.when(m % 2 == self.h.c)
        def _():
            self.MINE[m // 2, :, columns] = value

        @pl.when(m % 2 != self.h.c)
        def _():
            self.SENT[:, columns] = value

    def two(self, x, r):
        return self.MINE[x, r].astype(F32) + self.R0[x, r].astype(F32)

    def sib(self, x):
        return remote(self.SENT, self.R0.at[x], self.sems[0].at[x], self.sems[1].at[x], self.h.at(c=1 - self.h.c))

    def ysend(self, x, z):
        h = self.h
        src = self.MINE.at[x, self.block(z, 1 - h.y)]
        return remote(src, self.R1.at[x, z], self.sems[2].at[x, 0], self.sems[3].at[x, z], h.at(y=1 - h.y))

    def zsend(self, x, z):
        h = self.h
        return remote(self.R1.at[x, z], self.R2.at[x, h.z], self.sems[4].at[x, 0], self.sems[5].at[x, h.z], h.at(z=z))

    def zcome(self, x, z):
        h = self.h
        return remote(self.R2.at[x, z], self.R2.at[x, z], self.sems[4].at[x, 0], self.sems[5].at[x, z], h.at(z=z))

    def xsend(self):
        h = self.h
        return remote(self.R1.at[1 - h.x, h.z], self.R3, self.sems[6].at[0], self.sems[7].at[0], h.at(x=1 - h.x))

    def xall(self, z, y_is_own, mine=True):
        h = self.h
        i = 2 if y_is_own else 4
        to = h.x if mine else 1 - h.x
        src = self.MINE.at[1 - h.x, self.block(z, h.y if y_is_own else 1 - h.y)]
        dst = (self.R1 if y_is_own else self.R2).at[to, z]
        return remote(src, dst, self.sems[i].at[1 - h.x, 0], self.sems[i + 1].at[to, z], h.at(x=1 - h.x))

    def after_group(self, m):
        pl.when(m % 2 != self.h.c)(lambda: self.sib(m // 2).start())

    def before_group(self, m, i):
        pl.when((m % 2 != self.h.c) & (i >= 2))(lambda: self.sib(1 - m // 2).wait_send())

    def sib_sent(self, own):
        self.sib(self.half(own)).wait_send()

    def each(self, fn):
        loop(1, self.nz + 1, lambda k: fn(self.h.zi(k)))

    def others(self, fn):
        loop(1, self.nz, lambda k: fn(self.h.zi(k)))

    def after_sib(self, own):
        x = self.half(own)
        self.sib(x).wait_recv()

        def on(z):
            r = self.block(z, 1 - self.h.y)
            self.MINE[x, r] = self.two(x, r).astype(BF)
            self.ysend(x, z).start()

        self.each(on)

    def after_y(self, own):
        x = self.half(own)

        def on(z):
            self.ysend(x, z).wait_recv()
            total = self.two(x, self.block(z, self.h.y)) + self.R1[x, z].astype(F32)
            self.R1[x, z] = total.astype(BF)
            pl.when(z != self.h.z)(lambda: self.zsend(x, z).start())

        self.each(on)

    def after_z(self, own):
        h, x = self.h, self.half(own)
        self.others(lambda z: self.zcome(x, z).wait_recv())

        def add(k, acc):
            return acc + self.R2[x, h.zi(k)].astype(F32)

        total = lax.fori_loop(1, self.nz, add, self.R1[x, h.z].astype(F32))
        if own:
            self.RES[...] = total
        else:
            self.R1[x, h.z] = total.astype(BF)
            self.xsend().start()

    def to_x(self):
        x = self.half(False)
        self.sib(x).wait_recv()

        def on(z):
            for y_is_own in (True, False):
                r = self.block(z, self.h.y if y_is_own else 1 - self.h.y)
                self.MINE[x, r] = self.two(x, r).astype(BF)
                self.xall(z, y_is_own).start()

        self.each(on)

    def after_x(self):
        x = self.half(True)
        self.sib(x).wait_recv()

        def on(z):
            r = self.block(z, 1 - self.h.y)
            self.xall(z, False, False).wait_recv()
            self.MINE[x, r] = (self.two(x, r) + self.R2[1 - x, z].astype(F32)).astype(BF)
            self.ysend(x, z).start()

        self.each(on)

    def after_x_and_y(self):
        x = self.half(True)

        def on(z):
            self.xall(z, True, False).wait_recv()
            self.ysend(x, z).wait_recv()
            total = self.two(x, self.block(z, self.h.y)) + self.R1[x, z].astype(F32) + self.R1[1 - x, z].astype(F32)
            self.R1[x, z] = total.astype(BF)
            pl.when(z != self.h.z)(lambda: self.zsend(x, z).start())

        self.each(on)

    def steps(self):
        out = {}
        if self.x_first:
            fns = {"xs": self.to_x, "xw": self.after_x, "xy": self.after_x_and_y, "zo": lambda: self.after_z(True)}
        else:
            fns = {}
            for tag, own in (("w", True), ("t", False)):
                fns["s" + tag] = functools.partial(self.after_sib, own)
                fns["y" + tag] = functools.partial(self.after_y, own)
                fns["z" + tag] = functools.partial(self.after_z, own)
        for name, fn in fns.items():
            for c in (0, 1):
                out[name + str(c)] = functools.partial(self.on_core, c, fn)
        return out

    def on_core(self, c, fn):
        pl.when(self.h.c == c)(fn)

    def result(self):
        if not self.x_first:
            self.xsend().wait_recv()
            self.RES[...] += self.R3[...].astype(F32)

    def wait_sent(self, i, x, blocks):
        src = self.R1.at[x, pl.ds(0, blocks)]
        remote(src, src, self.sems[i].at[x, 0], self.sems[i + 1].at[x, 0], self.h.at(c=1 - self.h.c)).wait_send()

    def sent(self):
        own, other = self.half(True), self.half(False)
        self.wait_sent(2, own, self.nz)
        self.wait_sent(4, own, self.nz - 1)
        self.wait_sent(2, other, self.nz)
        if self.x_first:
            self.wait_sent(4, other, self.nz)
        else:
            self.wait_sent(4, other, self.nz - 1)
            self.xsend().wait_send()


def dot(a, b, ca=1, cb=0, precision=None):
    return lax.dot_general(a, b, (((ca,), (cb,)), ((), ())), preferred_element_type=F32, precision=precision)


def tile_rows(i, size):
    return pl.ds(pl.multiple_of(i * size, size), size)


TILE = 256


def rsq(v):
    return lax.rsqrt(jnp.mean(v * v, axis=-1, keepdims=True) + EPS)


def toeplitz(offsets, ST):
    heads, span = ST.shape[0], ST.shape[2]
    for h in range(heads):
        row = jnp.broadcast_to(offsets[h : h + 1, :], (128, offsets.shape[1]))
        ST[h] = pltpu.roll(row, 0, 1, stride=1, stride_axis=0)[:, :span]


def biased(s, ST, h, dead):
    blocks = s.shape[0] // 128
    pieces = []
    for j in range(blocks):
        c0 = 128 * (blocks - 1 - j)
        piece = s[128 * j : 128 * (j + 1)] + ST[h, :, c0 : c0 + s.shape[1]]
        pieces.append(piece if j < blocks // 2 else piece + dead)
    return jnp.concatenate(pieces, 0)


def attend(QV, ST, h, part, dh, seq, dead, base, OV, LV):
    q0, k0, v0 = h * dh, part + h * dh, 2 * part + h * dh
    rows = pl.ds(base, seq)
    queries, keys, values = QV[rows, q0 : q0 + dh], QV[rows, k0 : k0 + dh], QV[rows, v0 : v0 + dh]
    s = biased(dot(keys, queries, 1, 1), ST, h, dead)
    top = jnp.max(s, axis=0, keepdims=True)
    e = jnp.exp(s - top)
    total = jnp.sum(e, axis=0, keepdims=True)
    prob = (e * (1.0 / total)).astype(BF)
    OV[rows, h * dh : (h + 1) * dh] = dot(prob, values, 0, 0).astype(BF)
    LV[h : h + 1, rows] = top + jnp.log(total)


GELU_C = float(np.sqrt(2.0 / np.pi))


def gelu_both(a):
    a2 = a * a
    t = jnp.tanh(a * (GELU_C + (GELU_C * 0.044715) * a2))
    half = 0.5 + 0.5 * t
    slope = half + (0.5 * a) * (1.0 - t * t) * (GELU_C + (3.0 * GELU_C * 0.044715) * a2)
    return a * half, slope


def attend_back(QV, ST, DO, LV, DL, GQKV, D, h, part, dh, seq, dead, base):
    rows = pl.ds(base, seq)
    q0, k0, v0 = h * dh, part + h * dh, 2 * part + h * dh
    queries, keys, values = QV[rows, q0 : q0 + dh], QV[rows, k0 : k0 + dh], QV[rows, v0 : v0 + dh]
    d_o = DO[rows, h * dh : (h + 1) * dh]
    s = biased(dot(keys, queries, 1, 1), ST, h, dead)
    prob = jnp.exp(s - LV[h : h + 1, rows])
    dprob = dot(values, d_o, 1, 1)
    gs = (prob * (dprob - DL[h : h + 1, rows])).astype(BF)
    GQKV[rows, v0 : v0 + dh] = dot(prob.astype(BF), d_o).astype(BF)
    GQKV[rows, k0 : k0 + dh] = dot(gs, queries).astype(BF)
    GQKV[rows, q0 : q0 + dh] = dot(keys.T, gs).astype(BF).T
    blocks = seq // 128
    for d in range(1 - blocks, blocks):
        c0 = 128 * (blocks - 1 - d)
        acc = D[h, :, c0 : c0 + 128]
        for j in range(max(0, d), min(blocks, blocks + d)):
            acc += gs[128 * j : 128 * (j + 1), 128 * (j - d) : 128 * (j - d + 1)].astype(F32)
        D[h, :, c0 : c0 + 128] = acc


def layer_kernel(cfg, tok, cot, wq, wk, wv, wo, wi, wf_t, table_t, onehot, gain1, gain2, lens, *refs):
    ndp, nmp, fine, seq, heads_mp = cfg
    L, I, RES, SMALL, W, QKV, O, LSE = refs[:8]
    OWN, OFFV, XV, DYV, N2, N2T, DYT, U, GA, HV, FF, GN, BV, CV, QV, OV, LV, DL, ST, D = refs[8:28]
    FFMINE, SENT = refs[28:30]
    bufs, SR, SZ = refs[30:34], refs[34], refs[35]
    ssem, rsem, xsem, dysem, lsem, isem, bsem, osem, wsem, qsem, ssmall, rsmall, csem = refs[36:49]
    sems = refs[49:57]
    rows, part = wq.shape
    h = Place(ndp, nmp, fine, rows)
    h.greet()
    n, width = XV.shape
    hid = U.shape[1]
    dh = part // heads_mp
    share = n // seq
    tiles = n // TILE
    nz = h.nz

    def gain(ref):
        return ref[...].reshape(1, width)

    def go(copies):
        for cp in copies:
            cp.start()

    def done(copies):
        for cp in copies:
            cp.wait()

    def run(section, at, static=None, period=1):
        for (name, slot), steps in PLAN.items():
            if name == section and (slot == at if static is None else slot % period in static):

                def fn(steps=steps):
                    for step in steps:
                        ACTIONS[step]()

                if static is None:
                    fn()
                else:
                    pl.when(at == slot)(fn)

    OWN[0, :, :part] = wq[...].astype(BF)
    OWN[0, :, part : 2 * part] = wk[...].astype(BF)
    OWN[0, :, 2 * part : 3 * part] = wv[...].astype(BF)
    OWN[0, :, 3 * part :] = wo[...].T.astype(BF)
    OWN[1] = wi[...].astype(BF)
    OWN[2] = wf_t[...].astype(BF)
    own = [pltpu.make_async_copy(OWN.at[p], W.at[p, h.x, h.c, h.block(h.z, h.y)], csem.at[p]) for p in range(3)]
    go(own)
    OFFV[h.mp] = jnp.zeros_like(OFFV[0])
    OFFV[h.mp, :heads_mp] = dot(table_t[...], onehot[: table_t.shape[1], :], 1, 0, HIGHEST)

    def offs(k, mine=True):
        other = lax.rem(h.mp + (k if mine else nmp - k), nmp)
        at = OFFV.at[h.mp if mine else other]
        return remote(at, at, bsem.at[0, k], bsem.at[1, k], (h.dp, other))

    A, B, C = [Gather(h, p, MODES[name], W, ssem, rsem) for p, name in enumerate("ABC")]
    mines = (CV, SENT.at[0]), (FFMINE.at[0], SENT.at[0]), (FFMINE.at[1], SENT.at[1])
    PA, PI, PO = [
        Scatter(h, p, X_FIRST[name], mines[p], bufs, RES, sems) for p, name in enumerate(("PA", "PI", "PO"))
    ]
    sx = Swap(h, tok, XV, xsem, False)
    sd = Swap(h, cot, DYV, dysem, False)
    sl = Swap(h, L, DYV, lsem, True)
    si = Swap(h, I, XV, isem, True)

    ACTIONS = {"dy": sd.start_all, "lay": sl.start_all}
    for name, part_of in (("A", A), ("B", B), ("C", C), ("PA", PA), ("PI", PI), ("PO", PO)):
        ACTIONS.update({name + "." + step: fn for step, fn in part_of.steps().items()})

    done(own)
    h.met()
    if A_BY_HOPS:
        A.hops()
    else:
        ACTIONS["A.Zs"]()
        ACTIONS["A.Y0"]()
    run("first", 0)
    sx.start_all()
    for k in range(1, nmp):
        offs(k).start()
    run("start", 0)
    if A_BY_HOPS:
        A.hops_on()
    else:
        ACTIONS["A.zy"]()
    run("start", 1)
    ACTIONS["A.ys"]()
    run("start", 2)
    sx.come()
    run("start", 3)

    def norm(t):
        r = tile_rows(t, TILE)
        x = XV[r, :].astype(F32)
        N2[r, :] = (x * rsq(x) * gain(gain1)).astype(BF)
        HV[r, :] = x

    loop(0, tiles, norm)
    A.sib_wait(0)

    def group(i):
        return lax.rem(2 * h.x + i, nmp)

    def load(p, i, m, V, sem):
        slot = lax.rem(i, 2)
        return pltpu.make_async_copy(W.at[p, m // 2, m % 2], V.at[slot], sem.at[slot])

    def load_a(i):
        return load(0, i, group(i), BV, wsem.at[0])

    def store(i):
        m, slot = group(i), lax.rem(i, 2)
        return (
            pltpu.make_async_copy(QV.at[slot], QKV.at[m], osem.at[0, slot]),
            pltpu.make_async_copy(OV.at[slot], O.at[m], osem.at[1, slot]),
            pltpu.make_async_copy(LV.at[slot], LSE.at[m], osem.at[2, slot]),
        )

    load_a(0).start()
    for k in range(1, nmp):
        offs(k, False).wait_recv()

    def attn_group(i):
        slot = lax.rem(i, 2)
        m = group(i)

        @pl.when(i == 2)
        def _():
            A.sib_wait(1)
            load_a(2).start()

        toeplitz(OFFV.at[m], ST)
        pl.when(i >= 2)(lambda: done(store(i - 2)))
        load_a(i).wait()
        pl.when((i == 0) | (i == 2))(lambda: load_a(i + 1).start())

        QV[slot] = dot(N2[...], BV[slot, :, : 3 * part]).astype(BF)

        def pair(p):
            base = pl.multiple_of(p * seq, seq)
            off = jnp.where(lens[h.mp * share + p] < seq, -1e30, 0.0).astype(F32)
            run("attend", i * share + p, range(1))
            for head in range(heads_mp):
                attend(QV.at[slot], ST, head, part, dh, seq, off, base, OV.at[slot], LV.at[slot])

        loop(0, share, pair)

        HV[...] += dot(OV[slot], BV[slot, :, 3 * part :], 1, 1)
        go(store(i))

    loop(0, nmp, attn_group)

    run("between", 0)

    def load_ff(i):
        m = group(i)
        return load(1, i, m, BV, wsem.at[0]), load(2, i, m, CV, wsem.at[1])

    sd.come()
    SMALL[...] = jnp.zeros_like(SMALL)

    def prep(t):
        r = tile_rows(t, TILE)
        hidden = HV[r, :]
        n2 = (hidden * rsq(hidden) * gain(gain2)).astype(BF)
        N2[r, :] = n2
        N2T[:, r] = n2.T
        DYT[:, r] = DYV[r, :].T
        FF[r, :] = hidden
        GN[r, :] = jnp.zeros((TILE, width), F32)

    loop(0, tiles, prep)
    run("between", 1)
    B.sib_wait(0)
    C.sib_wait(0)
    go(load_ff(0))

    steps = tiles + 2

    def ff_group(i):
        slot = lax.rem(i, 2)
        m = group(i)
        done(load_ff(i))
        pl.when((i == 0) | (i == 2))(lambda: go(load_ff(i + 1)))

        def rowwise(t):
            run("ff", i * steps + t, range(tiles), steps)
            r = tile_rows(t, TILE)
            b = BV[slot]
            c = CV[slot]
            a = dot(N2[r, :], b)
            gu = dot(DYV[r, :], c)
            u, slope = gelu_both(a)
            u = u.astype(BF)
            ga = (gu * slope).astype(BF)
            U[r, :] = u
            GA[r, :] = ga
            FF[r, :] += dot(u, c, 1, 1)
            GN[r, :] += dot(ga, b, 1, 1)

        loop(0, tiles, rowwise)
        PI.before_group(m, i)
        PO.before_group(m, i)

        run("ff", i * steps + tiles, (tiles,), steps)
        PI.put(m, slice(None), dot(N2T[...], GA[...]).astype(BF))
        run("ff", i * steps + tiles + 1, (tiles + 1,), steps)
        PO.put(m, slice(None), dot(DYT[...], U[...]).astype(BF))
        PI.after_group(m)
        PO.after_group(m)

        @pl.when(i == 1)
        def _():
            run("between", 2)
            B.sib_wait(1)
            C.sib_wait(1)
            go(load_ff(2))

    loop(0, nmp, ff_group)

    def back_group(i):
        return lax.rem(2 * (1 - h.x) + i, nmp)

    def load_attn(i):
        m, slot = back_group(i), lax.rem(i, 2)
        return (
            load(0, i, m, BV, wsem.at[0]),
            pltpu.make_async_copy(QKV.at[m], QV.at[slot], qsem.at[0, slot]),
            pltpu.make_async_copy(O.at[m], OV.at[slot], qsem.at[1, slot]),
            pltpu.make_async_copy(LSE.at[m], LV.at[slot], qsem.at[2, slot]),
        )

    for i in (nmp - 2, nmp - 1):
        done(store(i))
    go(load_attn(0))
    run("between", 3)

    def mid(t):
        r = tile_rows(t, TILE)
        hidden = HV[r, :]
        r2 = rsq(hidden)
        nh = hidden * r2
        g = GN[r, :]
        SMALL[1:2, :] += jnp.sum(g * nh, axis=0, keepdims=True)
        e = g * gain(gain2)
        gh = DYV[r, :].astype(F32) + r2 * (e - nh * jnp.mean(e * nh, axis=-1, keepdims=True))
        DYV[r, :] = FF[r, :].astype(BF)
        HV[r, :] = gh
        low = gh.astype(BF)
        N2[r, :] = low
        DYT[:, r] = low.T
        x = XV[r, :].astype(F32)
        N2T[:, r] = (x * rsq(x) * gain(gain1)).astype(BF).T
        GN[r, :] = jnp.zeros((TILE, width), F32)
        U[r, 3 * part :] = jnp.zeros((TILE, hid - 3 * part), BF)

    loop(0, tiles, mid)

    GQKV, DO = U, GA
    wide = -(-3 * part // 128) * 128

    def last(p, t):
        r = pl.ds(pl.multiple_of(p * seq + t * TILE, TILE), TILE)
        x = XV[r, :].astype(F32)
        r1 = rsq(x)
        nx = x * r1
        g = GN[r, :]
        SMALL[0:1, :] += jnp.sum(g * nx, axis=0, keepdims=True)
        e = g * gain(gain1)
        XV[r, :] = (HV[r, :] + r1 * (e - nx * jnp.mean(e * nx, axis=-1, keepdims=True))).astype(BF)


    head_of = (lax.broadcasted_iota(jnp.int32, (8, part), 1) // dh == lax.broadcasted_iota(jnp.int32, (8, part), 0)).astype(F32)

    def attn_back_group(i):
        slot = lax.rem(i, 2)
        m = back_group(i)
        toeplitz(OFFV.at[m], ST)
        D[...] = jnp.zeros_like(D)
        done(load_attn(i))
        pl.when(i + 1 < nmp)(lambda: go(load_attn(i + 1)))

        d_o = dot(N2[...], BV[slot, :, 3 * part :]).astype(BF)
        DO[:, :part] = d_o
        DL[...] = dot(head_of, OV[slot].astype(F32) * d_o.astype(F32), 1, 1, HIGHEST)

        def join(p):
            r = tile_rows(p, seq)
            GN[r, :] += dot(GQKV[r, :wide], BV[slot, :, :wide], 1, 1)

            @pl.when(i == nmp - 1)
            def _():
                loop(0, seq // TILE, functools.partial(last, p))
                pl.when(p + 1 < share)(lambda: si.start(p))

        def pair(p):
            pl.when(p > 0)(lambda: join(p - 1))
            base = pl.multiple_of(p * seq, seq)
            off = jnp.where(lens[h.mp * share + p] < seq, -1e30, 0.0).astype(F32)
            run("back", i * share + p, range(1))
            for head in range(heads_mp):
                attend_back(QV.at[slot], ST, DO, LV.at[slot], DL, GQKV, D, head, part, dh, seq, off, base)

        loop(0, share, pair)
        PA.before_group(m, i)
        pl.when((m % 2 != h.c) & (i < 2))(lambda: PI.sib_sent(False))

        PA.put(m, slice(0, 3 * part), dot(N2T[...], GQKV[:, : 3 * part]).astype(BF))
        PA.put(m, slice(3 * part, hid), dot(DYT[...], OV[slot]).astype(BF))
        PA.after_group(m)
        join(share - 1)
        sums = []
        for head in range(heads_mp):
            strip = jnp.concatenate([D[head], jnp.zeros((128, 128), F32)], 1)
            span = strip.shape[1]
            half = 64
            while half:
                strip = strip[:half] + pltpu.roll(strip[half:], span - half, 1)
                half //= 2
            sums.append(strip)
        sums = jnp.concatenate(sums + [jnp.zeros((8 - heads_mp, span), F32)], 0)
        at = pl.ds(pl.multiple_of(m * 128, 128), 128)
        SMALL[8:16, at] = dot(sums, onehot[...], 1, 1, HIGHEST)

    loop(0, nmp, attn_back_group)
    run("end", 0)

    small = [
        remote(SMALL, SR.at[i], ssmall.at[i], rsmall.at[i], who)
        for i, who in enumerate((h.at(c=1 - h.c), h.at(x=1 - h.x), h.at(y=1 - h.y), h.at(c=1 - h.c)))
    ]

    def small_z(k, mine):
        z = h.zi(k)
        b = h.z if mine else z
        return remote(SZ.at[b], SZ.at[b], ssmall.at[4 + z], rsmall.at[4 + b], h.at(z=z))

    def small_step(i):
        small[i].wait()
        SMALL[...] += SR[i]

    def on_core_0(fn):
        pl.when(h.c == 0)(fn)

    small[0].start()
    A.sent(A_BY_HOPS)
    B.sent()
    C.sent()
    for k in range(1, nmp):
        offs(k).wait_send()
    sx.sent()
    sd.sent()
    sl.come()
    sl.sent()
    small_step(0)
    on_core_0(lambda: small[1].start())
    si.start(share - 1)
    run("end", 1)

    @on_core_0
    def _():
        small_step(1)
        small[2].start()

    run("end", 2)

    @on_core_0
    def _():
        small_step(2)
        SZ[h.z] = SMALL[...]
        loop(1, nz, lambda k: small_z(k, True).start())

    run("end", 3)

    @on_core_0
    def _():
        loop(1, nz, lambda k: small_z(k, False).wait_recv())
        SMALL[...] = lax.fori_loop(1, nz, lambda z, acc: acc + SZ[z], SZ[0])
        small[3].start()

    run("end", 4)

    @pl.when(h.c == 1)
    def _():
        small[3].wait_recv()
        SMALL[...] = SR[3]

    run("end", 5)
    for T in (PA, PI, PO):
        T.result()
        T.sent()
    PA.sib_sent(True)
    PO.sib_sent(False)

    @on_core_0
    def _():
        loop(1, nz, lambda k: small_z(k, True).wait_send())
        small[3].wait_send()

    si.come()
    si.sent()


def layer(tok, cot, ws, table_t, onehot, gain1, gain2, lens, ndp, nmp, fine):
    pairs, positions, width = tok.shape
    rows, part = ws[0].shape
    hid = ws[4].shape[1]
    heads_mp = table_t.shape[0]
    seq = positions * nmp
    share = pairs // nmp
    n = share * seq
    nz = ndp // fine // 2
    any_ = pl.BlockSpec(memory_space=pl.ANY)
    vm = pl.BlockSpec(memory_space=pltpu.VMEM)
    dma = pltpu.SemaphoreType.DMA
    sds = jax.ShapeDtypeStruct
    bf = lambda *s: pltpu.VMEM(s, BF)
    fl = lambda *s: pltpu.VMEM(s, F32)
    act = sds((pairs, positions, width), BF)
    return pl.pallas_call(
        functools.partial(layer_kernel, (ndp, nmp, fine, seq, heads_mp)),
        out_shape=(act, act)
        + (
            sds((3, rows, hid), F32),
            sds((16, width), F32),
            sds((3, nmp // 2, 2, width, hid), BF),
            sds((nmp, n, 3 * part), BF),
            sds((nmp, n, part), BF),
            sds((nmp, 8, n), F32),
        ),
        in_specs=[any_, any_] + [vm] * 10 + [pl.BlockSpec(memory_space=pltpu.SMEM)],
        out_specs=(any_, any_) + (vm,) * 2 + (any_,) * 4,
        scratch_shapes=[
            bf(3, rows, hid),
            fl(nmp, 8, 2 * seq),
            bf(n, width),
            bf(n, width),
            bf(n, width),
            bf(width, n),
            bf(width, n),
            bf(n, hid),
            bf(n, hid),
            fl(n, width),
            fl(n, width),
            fl(n, width),
            bf(2, width, hid),
            bf(2, width, hid),
            bf(2, n, 3 * part),
            bf(2, n, part),
            fl(2, 8, n),
            fl(8, n),
            fl(heads_mp, 128, 2 * seq - 128),
            fl(heads_mp, 128, 2 * seq - 128),
            bf(2, 2, width, hid),
            bf(2, width, hid),
            bf(3, 2, width, hid),
            bf(3, 2, nz, rows, hid),
            bf(3, 2, nz, rows, hid),
            bf(3, rows, hid),
            fl(4, 16, width),
            fl(nz, 16, width),
            dma((3, 8, nz)),
            dma((3, 8, nz)),
        ]
        + [dma((2, nmp, share))] * 4
        + [dma((2, nmp)), dma((3, 2)), dma((2, 2)), dma((3, 2)), dma((4 + nz,)), dma((4 + nz,)), dma((3,))]
        + [dma((3, 2))] * 2
        + [dma((3, 2, nz))] * 4
        + [dma((3, 1))] * 2,
        compiler_params=pltpu.CompilerParams(collective_id=0, has_side_effects=True, vmem_limit_bytes=63 * MIB),
    )(tok, cot, *ws, table_t, onehot, gain1, gain2, lens)


def finish_kernel(heads_mp, L, I, RES_, SMALL_, L2, I2, GQ, GK, GV, GO, GI, GF, G1, G2, GB, buf, RES, SMALL, sem):
    come = [
        pltpu.make_async_copy(a, b, sem.at[0, i])
        for i, (a, b) in enumerate(((L, buf.at[0]), (I, buf.at[1]), (RES_, RES), (SMALL_, SMALL)))
    ]
    go = [pltpu.make_async_copy(buf.at[i], a, sem.at[1, i]) for i, a in enumerate((L2, I2))]
    for cp in come:
        cp.start()
    for before, after in zip(come, go):
        before.wait()
        after.start()
    come[2].wait()
    come[3].wait()
    part = GQ.shape[1]
    GQ[...] = RES[0, :, :part]
    GK[...] = RES[0, :, part : 2 * part]
    GV[...] = RES[0, :, 2 * part : 3 * part]
    GO[...] = RES[0, :, 3 * part :].T
    GI[...] = RES[1]
    GF[...] = RES[2]
    G1[...] = SMALL[0, :]
    G2[...] = SMALL[1, :]
    at = pl.ds(pl.multiple_of(lax.axis_index("mp") * 128, 128), 128)
    GB[...] = SMALL[8:16, at][:heads_mp, : GB.shape[1]]
    for cp in go:
        cp.wait()


def finish(L, I, RES, SMALL, part, heads_mp, buckets):
    _, rows, hid = RES.shape
    width = SMALL.shape[1]
    any_ = pl.BlockSpec(memory_space=pl.ANY)
    vm = pl.BlockSpec(memory_space=pltpu.VMEM)
    sds = jax.ShapeDtypeStruct
    f32 = [(rows, part)] * 3 + [(part, rows), (rows, hid), (rows, hid), (width,), (width,), (heads_mp, buckets)]
    return pl.pallas_call(
        functools.partial(finish_kernel, heads_mp),
        out_shape=(sds(L.shape, BF), sds(I.shape, BF)) + tuple(sds(s, F32) for s in f32),
        in_specs=[any_] * 4,
        out_specs=(any_, any_) + (vm,) * len(f32),
        scratch_shapes=[
            pltpu.VMEM((2,) + L.shape, BF),
            pltpu.VMEM(RES.shape, F32),
            pltpu.VMEM(SMALL.shape, F32),
            pltpu.SemaphoreType.DMA((2, 4)),
        ],
    )(L, I, RES, SMALL)


def body(tokens, cotangent, lengths, gain_attn, gain_ff, bias_table, w_query, w_key, w_value, w_out_attn, w_in_ff, w_out_ff):
    ndp, nmp = lax.axis_size("dp"), lax.axis_size("mp")
    seq = tokens.shape[1] * nmp
    buckets, heads_mp = bias_table.shape
    fine = 16 // math.gcd(w_query.shape[0], 16)
    groups = [list(range(g, g + fine)) for g in range(0, ndp, fine)]

    def join(a, dim):
        return a if fine == 1 else lax.all_gather(a, "dp", axis=dim, tiled=True, axis_index_groups=groups)

    def split(a, dim):
        if fine == 1:
            return a
        return lax.psum_scatter(a, "dp", scatter_dimension=dim, tiled=True, axis_index_groups=groups)

    dims = (0, 0, 0, 1, 0, 0)
    ws = tuple(join(w, d) for w, d in zip((w_query, w_key, w_value, w_out_attn, w_in_ff, w_out_ff.T), dims))
    place = np.arange(2 * seq)
    place = np.where(place < 2 * seq - 128, seq - 128 - place, seq - 128 + 2 * seq - place)
    onehot = (bucket_of(place, buckets)[None] == np.arange(128)[:, None]).astype(np.float32)
    out, ing, res, small = layer(
        tokens, cotangent, ws, bias_table.T, onehot, gain_attn, gain_ff, lengths, ndp, nmp, fine
    )[:4]
    if fine > 1:
        small = lax.psum(small, "dp", axis_index_groups=groups)
    out, ing, *grads, g1, g2, gb = finish(out, ing, res, small, w_query.shape[1], heads_mp, buckets)
    gq, gk, gv, go, gi, gf = (split(g, d) for g, d in zip(grads, dims))
    return out, ing, g1, g2, gb.T, gq, gk, gv, go, gi, gf.T


def solution(mesh):
    act = P("dp", "mp", None)
    rows, cols = P("dp", "mp"), P("mp", "dp")
    return jax.shard_map(
        body,
        mesh=mesh,
        in_specs=(act, act, P("dp"), P(), P(), P(None, "mp"), rows, rows, rows, cols, rows, cols),
        out_specs=(act, act, P(), P(), P(None, "mp"), rows, rows, rows, cols, rows, cols),
        check_vma=False,
    )
```
